128 devices in a mesh: group: 8 (over y, core), tensor: 16 (over z, x).
Axes of the slice: x: 4, y: 4, z: 4, core: 2. Of those that a mesh axis runs over, the one named last changes fastest.
Arguments:
- residual: bfloat16 [2048, 7168], P('group'), may hold values from -6 to 6
- queries: bfloat16 [2048, 8, 896], P('group'), may hold values from -100 to 100
- new_kv: bfloat16 [2, 2048, 8, 128], P(None, 'group'), may hold values from -6 to 6
- kv_cache: bfloat16 [2, 2048, 1024, 128], P(None, 'group', 'tensor'), may hold values from -6 to 6
- lengths: int32 [2048], P('group'), may hold values from 1 to 128
- out_weight: bfloat16 [7168, 7168], P('tensor'), may hold values from -0.09375 to 0.09375
- dense_gate: bfloat16 [7168, 4864], P(None, 'tensor'), may hold values from -0.0625 to 0.0625
- dense_up: bfloat16 [7168, 4864], P(None, 'tensor'), may hold values from -0.0625 to 0.0625
- dense_down: bfloat16 [4864, 7168], P('tensor'), may hold values from -0.125 to 0.125
- expert_ids: int32 [2048, 2], P('group'), may hold values from 0 to 7, all different within a row; in each aligned block of 256 rows (0 to 255, 256 to 511, ...) at most 128 rows name the same one
- route_weights: float32 [2048, 2], P('group'), may hold values from 0.2 to 1
- expert_gate: bfloat16 [8, 7168, 4864], P('group', None, 'tensor'), may hold values from -0.0625 to 0.0625
- expert_up: bfloat16 [8, 7168, 4864], P('group', None, 'tensor'), may hold values from -0.0625 to 0.0625
- expert_down: bfloat16 [8, 4864, 7168], P('group', 'tensor'), may hold values from -0.125 to 0.125
Outputs:
- mixed: bfloat16 [2048, 7168], P('group', 'tensor')
The draws below stay inside these ranges and needn't reach their ends.
Inputs may be any that keep to these rules, and one draw needn't show every extreme that they name: `expert_ids`: among the 256 rows of one group no expert is named by more than 128 rows, a bound that some block reaches of them.
All inputs are finite; a program needn't handle non-finite values.
Results may differ from the reference program's by a relative error of at most 0.02.
Values may be sent and summed in bfloat16 or wider, within the bound.
A program may use at most 256 MiB of HBM per device.

```python
import math
import jax
import jax.numpy as jnp
import numpy as np
from jax import lax

D = 7168
HD = 128
KVH = 8
QG = 7
FFH = 4864
FE = 4864
RG = 256
CACHE = 128
TOKENS = 2048
EXPERTS = 8
CAP = 128


def draw_queries(key, part):
    key = jax.random.fold_in(key, 11)
    noise = jax.random.normal(key, (TOKENS, KVH, QG, HD), jnp.float32)
    values = noise
    return jnp.clip(values, -100.0, 100.0).reshape(TOKENS, KVH, QG * HD).astype(jnp.bfloat16)


def draw_kv_cache(key, part):
    key = jax.random.fold_in(key, 23)
    noise = jax.random.normal(key, (2, TOKENS, KVH, CACHE, HD), jnp.float32)
    keys_part = noise[0]
    stacked = jnp.stack([keys_part, noise[1]])
    return jnp.clip(stacked, -6.0, 6.0).reshape(2, TOKENS, KVH * CACHE, HD).astype(jnp.bfloat16)


def with_ends(entries, own_key, low, top_value):
    spot = [jax.random.randint(jax.random.fold_in(own_key, axis), (), 0, length) for axis, length in enumerate(entries.shape)]
    main_axis = entries.shape.index(max(entries.shape))
    next_to = spot[:main_axis] + [(spot[main_axis] + 1) % entries.shape[main_axis]] + spot[main_axis + 1:]
    return entries.at[tuple(spot)].set(low).at[tuple(next_to)].set(top_value)


def raised(values, rng, source, target, shards_of, factor):
    owner, partner = [(jnp.arange(values.shape[axis_at]) // (values.shape[axis_at] // shards_of)).reshape([-1 if axis == axis_at else 1 for axis in range(values.ndim)]) for axis_at in (source, target)]
    chosen = jax.random.permutation(rng, shards_of)[partner]
    strong = (owner == chosen) | (owner == (partner + shards_of // 2) % shards_of)
    return jnp.where(strong, factor * values, values)


def shard_levels(key, shape, split, least, high):
    loudness = 1.0
    for axis_at, shards_of in split:
        steps = jax.random.uniform(jax.random.fold_in(jax.random.fold_in(key, 6), axis_at), (shards_of,), jnp.float32, least / len(split), high / len(split))
        loudness = loudness * jnp.repeat(jnp.exp(steps), shape[axis_at] // shards_of).reshape((-1,) + (1,) * (len(shape) - 1 - axis_at))
    return loudness


def deal_out(stream_key, own, number, rows, number_of, top, bound, slope):
    ranking = jax.random.permutation(stream_key, number_of)
    crowded, ordinary = portions_of(number_of, rows * top, bound, slope, True), portions_of(number_of, rows * top, bound, slope, False)
    places = jnp.arange(number_of)

    def named(tallies, offset_by):
        used = int((tallies > 0).sum())
        fixed = max(1, used // 4)
        moved = fixed + (places - fixed + offset_by * (used - fixed)) % max(1, number_of - fixed)
        return jnp.zeros((number_of,), jnp.int32).at[ranking[jnp.where(places < fixed, places, moved)]].set(jnp.asarray(tallies, jnp.int32))

    tallies = jnp.where(number % 4 == 0, named(crowded, number // 4), named(ordinary, number - number // 4 - 1))
    mixed = jax.random.permutation(jax.random.fold_in(own, 3), number_of)
    donor, receiver = mixed[0:number_of // 2 * 2:2], mixed[1:number_of // 2 * 2:2]
    room = jnp.minimum(tallies[donor] - 1, bound - tallies[receiver]) // 2
    room = jnp.where((donor == ranking[0]) | (receiver == ranking[0]) | (tallies[receiver] == 0), 0, jnp.maximum(room, 0))
    moved = jax.random.randint(jax.random.fold_in(own, 4), (number_of // 2,), 0, 1 << 20) % (room + 1)
    tallies = tallies.at[donor].add(-moved).at[receiver].add(moved)
    items = jnp.searchsorted(jnp.cumsum(tallies), jnp.arange(rows * top), side="right").astype(jnp.int32)
    listing = items.reshape(top, rows).T
    listing = listing[jax.random.permutation(jax.random.fold_in(own, 1), rows)]
    offset_by = jax.random.randint(jax.random.fold_in(own, 2), (rows, 1), 0, top)
    return jnp.take_along_axis(listing, (jnp.arange(top)[None, :] + offset_by) % top, axis=1)


def portions_of(number_of, total, limit, skew, full):
    weights = [(1 << 20) // math.isqrt(standing ** skew) + 1 for standing in range(1, number_of + 1)]
    largest = limit if full else min(limit, max(-(-total // number_of), total * weights[0] // sum(weights)))
    least = 1 if total - largest >= number_of - 1 else 0
    counts, rest = [largest] + [least] * (number_of - 1), total - largest - least * (number_of - 1)
    while rest > 0:
        free = [i for i in range(1, number_of) if counts[i] < largest] or [i for i in range(1, number_of) if counts[i] < limit]
        pool, budget = sum([weights[i] for i in free]), rest
        for i in free:
            addition = min(limit - counts[i], max(1, budget * weights[i] // pool), rest)
            counts[i] = counts[i] + addition
            rest = rest - addition
    return np.array(counts)


def centred(stream_key, shape, deviation, bound, cuts=(), kind=jnp.bfloat16):
    values = jax.random.normal(stream_key, shape, jnp.float32) * deviation
    if len(cuts) > 0:
        values = shard_levels(stream_key, shape, cuts, -0.22, 0.18) * values
    return jnp.clip(values, min=-bound, max=bound).astype(kind)


def noise_with(own_key, shape, scale, limit, split, heavy, kind=jnp.bfloat16):
    drawn = scale * jax.random.normal(own_key, shape, jnp.float32)
    if split:
        drawn = drawn * shard_levels(own_key, shape, split, -0.22, 0.18)
    return jnp.clip(raised(drawn, jax.random.fold_in(own_key, 3), *heavy), -limit, limit).astype(kind)


def setup_inputs(seed: int = 0) -> dict:
    keys = jax.random.split(jax.random.key(seed), 15)
    residual = centred(keys[0], (TOKENS, D), 1.0, 6.0, ((0, 8),))
    queries = draw_queries(jax.random.fold_in(keys[14], 71), 0)
    new_kv = centred(keys[2], (2, TOKENS, KVH, HD), 1.0, 6.0, ((1, 8),))
    kv_cache = draw_kv_cache(jax.random.fold_in(keys[14], 71), 0)
    lengths = with_ends(jax.random.randint(keys[4], (TOKENS,), 1, CACHE + 1), jax.random.fold_in(keys[4], 1), 1, CACHE).astype(jnp.int32)
    out_weight = noise_with(keys[5], (KVH * QG * HD, D), (KVH * QG * HD) ** -0.5, 0.09375, ((0, 16),), (0, 1, 16, 2.0))
    dense_gate = centred(keys[6], (D, FFH), D ** -0.5, 0.0625, ((1, 16),))
    dense_up = centred(keys[7], (D, FFH), D ** -0.5, 0.0625, ((1, 16),))
    dense_down = noise_with(keys[8], (FFH, D), FFH ** -0.5, 0.125, ((0, 16),), (0, 1, 16, 2.0))
    expert_ids_keys = jax.random.split(jax.random.fold_in(keys[9], 1), TOKENS // RG)
    expert_ids_turns = jax.random.permutation(jax.random.fold_in(keys[9], 3), TOKENS // RG)
    expert_ids = jax.vmap(lambda own, number: deal_out(jax.random.fold_in(keys[9], 2), own, number, RG, EXPERTS, 2, CAP, 2))(expert_ids_keys, expert_ids_turns).reshape((TOKENS, 2))
    route_weights = jnp.clip(0.2 + 0.8 * jax.random.uniform(keys[10], (TOKENS, 2), jnp.float32) ** shard_levels(keys[10], (TOKENS, 2), ((0, 8),), -0.2, 0.2), 0.2, 1.0)
    expert_gate = centred(keys[11], (EXPERTS, D, FE), D ** -0.5, 0.0625, ((0, 8), (2, 16)))
    expert_up = centred(keys[12], (EXPERTS, D, FE), D ** -0.5, 0.0625, ((0, 8), (2, 16)))
    expert_down = noise_with(keys[13], (EXPERTS, FE, D), FE ** -0.5, 0.125, ((0, 8), (1, 16)), (1, 2, 16, 2.0))
    return {"residual": residual, "queries": queries, "new_kv": new_kv, "kv_cache": kv_cache, "lengths": lengths, "out_weight": out_weight, "dense_gate": dense_gate, "dense_up": dense_up, "dense_down": dense_down, "expert_ids": expert_ids, "route_weights": route_weights, "expert_gate": expert_gate, "expert_up": expert_up, "expert_down": expert_down}


def round_half(values):
    return lax.optimization_barrier(values.astype(jnp.bfloat16)).astype(jnp.float32)

def reference(residual, queries, new_kv, kv_cache, lengths, out_weight, dense_gate, dense_up, dense_down, expert_ids, route_weights, expert_gate, expert_up, expert_down):
    token_count = residual.shape[0]
    scale = 1.0 / math.sqrt(HD)
    query_all = queries.reshape(token_count, KVH, QG, HD).astype(jnp.float32)
    key_all = kv_cache[0].reshape(token_count, KVH, CACHE, HD).astype(jnp.float32)
    value_all = kv_cache[1].reshape(token_count, KVH, CACHE, HD).astype(jnp.float32)
    new_key = new_kv[0].astype(jnp.float32)
    new_value = new_kv[1].astype(jnp.float32)
    scores = jnp.einsum('thgd,thpd->thgp', query_all, key_all) * scale
    own_score = jnp.einsum('thgd,thd->thg', query_all, new_key) * scale
    position = jnp.arange(CACHE, dtype=jnp.int32)
    usable = position[None, None, None, :] < lengths[:, None, None, None]
    masked = jnp.where(usable, scores, -1e+30)
    highest = jnp.maximum(lax.optimization_barrier(jnp.max(masked, axis=-1)), own_score)
    weights = round_half(jnp.where(usable, jnp.exp(masked - highest[..., None]), 0.0))
    own_weight = round_half(jnp.exp(own_score - highest))
    numerator = jnp.einsum('thgp,thpd->thgd', weights, value_all) + own_weight[..., None] * new_value[:, :, None, :]
    denominator = lax.optimization_barrier(jnp.sum(weights, axis=-1)) + own_weight
    attention = (numerator / denominator[..., None]).astype(jnp.bfloat16).reshape(token_count, KVH * QG * HD)
    projected = jnp.dot(attention, out_weight, preferred_element_type=jnp.float32)
    state = (residual.astype(jnp.float32) + projected).astype(jnp.bfloat16)
    state_wide = state.astype(jnp.float32)
    normed = (state_wide * lax.rsqrt(lax.optimization_barrier(jnp.mean(state_wide * state_wide, axis=-1, keepdims=True)) + 1e-05)).astype(jnp.bfloat16)
    dense_inner = (jax.nn.silu(jnp.dot(normed, dense_gate, preferred_element_type=jnp.float32)) * jnp.dot(normed, dense_up, preferred_element_type=jnp.float32)).astype(jnp.bfloat16)
    dense_out = jnp.dot(dense_inner, dense_down, preferred_element_type=jnp.float32)

    def one_expert(running, packed):
        gate_matrix, up_matrix, down_matrix, expert_index = packed
        hidden_units = (jax.nn.silu(jnp.dot(normed, gate_matrix, preferred_element_type=jnp.float32)) * jnp.dot(normed, up_matrix, preferred_element_type=jnp.float32)).astype(jnp.bfloat16)
        coefficient = lax.optimization_barrier(jnp.sum(jnp.where(expert_ids == expert_index, route_weights, 0.0), axis=1))
        return (running + coefficient[:, None] * jnp.dot(hidden_units, down_matrix, preferred_element_type=jnp.float32), None)
    total = lax.scan(one_expert, state_wide + dense_out, (expert_gate, expert_up, expert_down, jnp.arange(EXPERTS, dtype=jnp.int32)))[0]
    return total.astype(jnp.bfloat16)
```

```python
import functools
import math

import jax
import jax.numpy as jnp
from jax import lax
from jax.experimental import pallas as pl
from jax.experimental.pallas import tpu as pltpu
from jax.sharding import PartitionSpec as P

BF = jnp.bfloat16
F32 = jnp.float32
SIDE = 4
LANES = 128
CHUNK = 128
SLICE = 448
HALF = SLICE // 2
SHARED = 64
CHUNKS = 8


def ring(value, step):
    return lax.rem(value + step + SIDE, SIDE)


class Place:
    def __init__(self):
        rank = lax.axis_index("tensor")
        self.rank = rank
        self.z = rank // SIDE
        self.x = lax.rem(rank, SIDE)

    def axes(self, odd):
        p = self.x + odd * (self.z - self.x)
        q = self.z + odd * (self.x - self.z)
        return p, q

    def at(self, odd, p, q):
        even_rank = q * SIDE + p
        odd_rank = p * SIDE + q
        return even_rank + odd * (odd_rank - even_rank)


def spot(odd, z, x):
    return z * SIDE + x + odd * ((x * SIDE + z) - (z * SIDE + x))


def copy_to(src, dst, send, recv, rank):
    return pltpu.make_async_remote_copy(
        src_ref=src,
        dst_ref=dst,
        send_sem=send,
        recv_sem=recv,
        device_id={"tensor": rank},
        device_id_type=pl.DeviceIdType.MESH,
    )


def lanes_low(rows):
    return lax.broadcasted_iota(jnp.int32, (rows, LANES), 1) < SHARED


def turned(block):
    return pltpu.roll(block, SHARED, 1)


def unfold_pair(even_half, odd_half):
    low = lanes_low(SHARED)
    e, o = even_half.astype(F32), odd_half.astype(F32)
    top = jnp.where(low, e, o)
    bottom = turned(jnp.where(low, o, e))
    return jnp.concatenate([top, bottom], axis=0).astype(BF)


def fold_pair(tile):
    low = lanes_low(SHARED)
    top, bottom = tile[:SHARED], turned(tile[SHARED:])
    return jnp.where(low, top, bottom).astype(BF), jnp.where(low, bottom, top).astype(BF)


def unfold_own(half):
    half = half.astype(F32)
    return jnp.concatenate([half, turned(half)], axis=0)


def fold_own(tile, is_odd):
    low = lanes_low(SHARED).astype(jnp.int32) != is_odd
    top, bottom = tile[:SHARED], turned(tile[SHARED:])
    return jnp.where(low, top, bottom)


def natural_own(ref, is_odd):
    first = pl.multiple_of(is_odd * SHARED, SHARED)
    half = pl.multiple_of((1 - is_odd) * (SLICE - SHARED), SHARED)
    tiles = [ref[pl.ds(first + k * LANES, LANES), :].astype(F32) for k in range(3)]
    return jnp.concatenate(tiles + [unfold_own(ref[pl.ds(half, SHARED), :])], axis=1)


def store_own(ref, block, is_odd):
    first = pl.multiple_of(is_odd * SHARED, SHARED)
    half = pl.multiple_of((1 - is_odd) * (SLICE - SHARED), SHARED)
    for k in range(3):
        ref[pl.ds(first + k * LANES, LANES), :] = block[:, k * LANES : (k + 1) * LANES].astype(BF)
    ref[pl.ds(half, SHARED), :] = fold_own(block[:, 3 * LANES :], is_odd).astype(BF)


def store_quarter(part, odd, z, block):
    for pair in range(2):
        e, o = spot(odd, z, 2 * pair), spot(odd, z, 2 * pair + 1)
        tiles = [
            block[:, (pair * 7 + k) * LANES : (pair * 7 + k + 1) * LANES] for k in range(7)
        ]
        even_half, odd_half = fold_pair(tiles[3])
        for k in range(3):
            part[e, k * LANES : (k + 1) * LANES, :] = tiles[k].astype(BF)
            part[o, SHARED + k * LANES : SHARED + (k + 1) * LANES, :] = tiles[4 + k].astype(BF)
        part[e, SLICE - SHARED :, :] = even_half
        part[o, :SHARED, :] = odd_half


def load_quarter(part, odd, z):
    blocks = []
    for pair in range(2):
        e, o = spot(odd, z, 2 * pair), spot(odd, z, 2 * pair + 1)
        blocks += [part[e, k * LANES : (k + 1) * LANES, :] for k in range(3)]
        blocks.append(unfold_pair(part[e, SLICE - SHARED :, :], part[o, :SHARED, :]))
        blocks += [part[o, SHARED + k * LANES : SHARED + (k + 1) * LANES, :] for k in range(3)]
    return jnp.concatenate(blocks, axis=1)


def add_into(dst, other):
    dst[...] = (dst[...].astype(F32) + other[...].astype(F32)).astype(BF)


class Summer:
    def __init__(self, place, part, r1, r2, r3, r4, send, recv):
        self.place, self.part = place, part
        self.landing = (r1, r2, r3, r4)
        self.send, self.recv = send, recv

    def copies(self, step, c):
        odd = lax.rem(c, 2)
        place, part = self.place, self.part
        p, q = place.axes(odd)
        result = []
        for way, hop in ((0, 1), (1, -1)):
            if step == 0:
                src = part.at[c, pl.ds(ring(q, 2) * SIDE + 2 * way, 2)]
                to = place.at(odd, p, ring(q, hop))
            elif step == 1:
                src = part.at[c, pl.ds(ring(q, hop) * SIDE, SIDE)]
                to = place.at(odd, p, ring(q, hop))
            elif step == 2:
                src = part.at[c, q * SIDE + ring(p, 2), pl.ds(way * HALF, HALF)]
                to = place.at(odd, ring(p, hop), q)
            else:
                src = part.at[c, q * SIDE + ring(p, hop)]
                to = place.at(odd, ring(p, hop), q)
            result.append(
                copy_to(
                    src,
                    self.landing[step].at[c, way],
                    self.send.at[c, step, way],
                    self.recv.at[c, step, way],
                    to,
                )
            )
        return result

    def start(self, step, c):
        for copy in self.copies(step, c):
            copy.start()

    def arrive(self, step, c):
        for copy in self.copies(step, c):
            copy.wait_recv()
        odd = lax.rem(c, 2)
        part = self.part
        p, q = self.place.axes(odd)
        landed = self.landing[step].at[c]
        if step == 0:
            for way, hop in ((0, 1), (1, -1)):
                for k in range(2):
                    add_into(part.at[c, ring(q, hop) * SIDE + 2 * way + k], landed.at[way, k])
        elif step == 1:
            for k in range(SIDE):
                dst = part.at[c, q * SIDE + k]
                dst[...] = (
                    dst[...].astype(F32) + landed[0, k].astype(F32) + landed[1, k].astype(F32)
                ).astype(BF)
        elif step == 2:
            for way, hop in ((0, 1), (1, -1)):
                add_into(
                    part.at[c, q * SIDE + ring(p, hop), pl.ds(way * HALF, HALF)], landed.at[way]
                )

    def total(self, c):
        odd = lax.rem(c, 2)
        p, q = self.place.axes(odd)
        landed = self.landing[3].at[c]
        return (
            self.part[c, q * SIDE + p].astype(F32) + landed[0].astype(F32) + landed[1].astype(F32)
        )

    def sent(self, c):
        for step in range(4):
            for copy in self.copies(step, c):
                copy.wait_send()


class Spreader:
    def __init__(self, place, part, send, recv):
        self.place, self.part, self.send, self.recv = place, part, send, recv

    def copies(self, step, c):
        odd = lax.rem(c, 2)
        place, part = self.place, self.part
        p, q = place.axes(odd)
        result = []
        for way, hop in ((0, 1), (1, -1)):
            if step == 0:
                ref = part.at[c, q * SIDE + p]
                to = place.at(odd, ring(p, hop), q)
            elif step == 1:
                ref = part.at[c, q * SIDE + ring(p, -hop), pl.ds(way * HALF, HALF)]
                to = place.at(odd, ring(p, hop), q)
            elif step == 2:
                ref = part.at[c, pl.ds(q * SIDE, SIDE)]
                to = place.at(odd, p, ring(q, hop))
            else:
                ref = part.at[c, pl.ds(ring(q, -hop) * SIDE + 2 * way, 2)]
                to = place.at(odd, p, ring(q, hop))
            result.append(
                copy_to(
                    ref, ref, self.send.at[c, step, way], self.recv.at[c, step, way], to
                )
            )
        return result

    def start(self, step, c):
        for copy in self.copies(step, c):
            copy.start()

    def arrive(self, step, c):
        for copy in self.copies(step, c):
            copy.wait_recv()

    def sent(self, c):
        for step in range(4):
            for copy in self.copies(step, c):
                copy.wait_send()


def greet_plane(place, barrier):
    for hop in (1, -1):
        for rank in (
            place.at(0, ring(place.x, hop), place.z),
            place.at(0, place.x, ring(place.z, hop)),
        ):
            pl.semaphore_signal(
                barrier, inc=1, device_id={"tensor": rank}, device_id_type=pl.DeviceIdType.MESH
            )


def project_kernel(
    att_ref, weight_ref, residual_ref, state_ref, part, r1, r2, r3, r4, near, send, recv, local
):
    place = Place()
    barrier = pltpu.get_barrier_semaphore()
    greet_plane(place, barrier)
    pl.semaphore_wait(barrier, 4)
    is_odd = lax.rem(place.rank, 2)
    first_column = pl.multiple_of((place.rank // 2) * 2 * SLICE, 2 * SLICE)
    fetch = pltpu.make_async_copy(
        residual_ref.at[:, pl.ds(first_column, 2 * SLICE)], near, local
    )
    fetch.start()
    summer = Summer(place, part, r1, r2, r3, r4, send, recv)
    count = part.shape[0]
    for c in range(count):
        rows = att_ref[c * CHUNK : (c + 1) * CHUNK, :]

        @pl.loop(0, SIDE)
        def _(z):
            columns = pl.ds(pl.multiple_of(z * 4 * SLICE, 4 * SLICE), 4 * SLICE)
            block = jnp.dot(rows, weight_ref[:, columns], preferred_element_type=F32)
            store_quarter(part.at[c], c % 2, z, block)

        summer.start(0, c)
    for step in range(1, 4):
        for c in range(count):
            summer.arrive(step - 1, c)
            summer.start(step, c)
    fetch.wait()
    for c in range(count):
        summer.arrive(3, c)
        rows = pl.ds(c * CHUNK, CHUNK)
        even = [near[rows, k * LANES : (k + 1) * LANES] for k in range(4)]
        odd = [near[rows, (k + 3) * LANES : (k + 4) * LANES] for k in range(4)]
        whole = jnp.concatenate(
            [
                jnp.where(is_odd == 1, odd[k + 1].astype(F32), even[k].astype(F32))
                for k in range(3)
            ]
            + [even[3].astype(F32)],
            axis=1,
        )
        store_own(state_ref.at[c], whole, is_odd)
        state_ref[c] = (state_ref[c].astype(F32) + summer.total(c)).astype(BF)
    for c in range(count):
        summer.sent(c)


def project(attention, out_weight, residual):
    count = attention.shape[0] // CHUNK
    return pl.pallas_call(
        project_kernel,
        out_shape=jax.ShapeDtypeStruct((count, SLICE, LANES), BF),
        in_specs=[
            pl.BlockSpec(memory_space=pltpu.VMEM),
            pl.BlockSpec(memory_space=pltpu.VMEM),
            pl.BlockSpec(memory_space=pl.ANY),
        ],
        out_specs=pl.BlockSpec(memory_space=pltpu.VMEM),
        scratch_shapes=[
            pltpu.VMEM((count, 16, SLICE, LANES), BF),
            pltpu.VMEM((count, 2, 2, SLICE, LANES), BF),
            pltpu.VMEM((count, 2, SIDE, SLICE, LANES), BF),
            pltpu.VMEM((count, 2, HALF, LANES), BF),
            pltpu.VMEM((count, 2, SLICE, LANES), BF),
            pltpu.VMEM((attention.shape[0], 2 * SLICE), BF),
            pltpu.SemaphoreType.DMA((count, 4, 2)),
            pltpu.SemaphoreType.DMA((count, 4, 2)),
            pltpu.SemaphoreType.DMA,
        ],
        compiler_params=pltpu.CompilerParams(
            collective_id=1, has_side_effects=True, vmem_limit_bytes=48 * 1024 * 1024
        ),
        name="project",
    )(attention, out_weight, residual)


def flipped(group, bits):
    b = (lax.rem(group, 2), lax.rem(group // 2, 2), group // 4)
    return sum((b[k] + bits[k] - 2 * b[k] * bits[k]) * (1 << k) for k in range(3))


def chunk_bits(c):
    if isinstance(c, int):
        a, b, d = c % 2, (c // 2) % 2, c // 4
    else:
        a, b, d = lax.rem(c, 2), lax.rem(c // 2, 2), c // 4
    return a, b + d - 2 * b * d, d


def to_group(src, dst, send, recv, group):
    return pltpu.make_async_remote_copy(
        src_ref=src,
        dst_ref=dst,
        send_sem=send,
        recv_sem=recv,
        device_id={"group": group},
        device_id_type=pl.DeviceIdType.MESH,
    )


def feed_kernel(
    ids_ref,
    flat_ids_ref,
    route_ref,
    state_ref,
    expert_gate,
    expert_up,
    expert_down,
    dense_gate,
    dense_up,
    dense_down,
    mixed_ref,
    part,
    r1,
    r2,
    r3,
    r4,
    w_eg,
    w_eu,
    w_dg,
    w_du,
    w_down,
    outgoing,
    side_out,
    side_in,
    returned,
    own_pos,
    acc,
    hidden,
    summed,
    load_sem,
    spread_send,
    spread_recv,
    sum_send,
    sum_recv,
    go_send,
    go_recv,
    side_send,
    side_recv,
    back_send,
    back_recv,
):
    place = Place()
    group = lax.axis_index("group")
    rank = place.rank
    is_odd = lax.rem(rank, 2)
    hidden_size = w_eg.shape[1]
    rows = ids_ref.shape[0]
    row_blocks = rows // CHUNK
    width = 16 * SLICE

    loads = [
        pltpu.make_async_copy(expert_gate.at[0], w_eg, load_sem.at[0]),
        pltpu.make_async_copy(expert_up.at[0], w_eu, load_sem.at[1]),
        pltpu.make_async_copy(dense_gate, w_dg, load_sem.at[2]),
        pltpu.make_async_copy(dense_up, w_du, load_sem.at[3]),
        pltpu.make_async_copy(expert_down.at[0], w_down.at[pl.ds(0, hidden_size)], load_sem.at[4]),
        pltpu.make_async_copy(
            dense_down, w_down.at[pl.ds(DENSE_AT, hidden_size)], load_sem.at[5]
        ),
    ]
    for load in loads:
        load.start()

    barrier = pltpu.get_barrier_semaphore()
    greet_plane(place, barrier)
    for c in range(1, CHUNKS):
        pl.semaphore_signal(
            barrier,
            inc=1,
            device_id={"group": flipped(group, chunk_bits(c))},
            device_id_type=pl.DeviceIdType.MESH,
        )

    ids = ids_ref[...]
    flat_ids = flat_ids_ref[...]
    lane = lax.broadcasted_iota(jnp.int32, (rows, LANES), 1)
    partner_of_lane = sum(
        jnp.where(lane == c, flipped(group, chunk_bits(c)) + 1, 0) for c in range(CHUNKS)
    ) - 1
    first_choice = ids[:, 0:1] == partner_of_lane
    second_choice = ids[:, 1:2] == partner_of_lane
    named = jnp.where(first_choice | second_choice, 1.0, 0.0)
    line = lax.broadcasted_iota(jnp.int32, (rows, rows), 0)
    column = lax.broadcasted_iota(jnp.int32, (rows, rows), 1)
    before = jnp.where(column < line, 1.0, 0.0).astype(BF)
    place_in = jnp.dot(before, named.astype(BF), preferred_element_type=F32)
    own_pos[...] = jnp.where(named > 0.5, place_in, -1.0)

    sub = lax.broadcasted_iota(jnp.int32, (8, rows), 0)
    partner_of_sub = sum(
        jnp.where(sub == c, flipped(group, chunk_bits(c)) + 1, 0) for c in range(CHUNKS)
    ) - 1
    flat_named = jnp.where(
        (flat_ids[0:1, :] == partner_of_sub) | (flat_ids[1:2, :] == partner_of_sub), 1.0, 0.0
    )
    after = jnp.where(line < column, 1.0, 0.0).astype(BF)
    flat_place = jnp.dot(flat_named.astype(BF), after, preferred_element_type=F32)
    flat_pos = jnp.where(flat_named > 0.5, flat_place, -1.0)

    weight = jnp.where(first_choice, route_ref[:, 0:1], 0.0) + jnp.where(
        second_choice, route_ref[:, 1:2], 0.0
    )
    dense_here = jnp.where(first_choice, 1.0, 0.0)
    source = jnp.concatenate(
        [natural_own(state_ref.at[b], is_odd) for b in range(row_blocks)], axis=0
    ).astype(BF)
    slot_line = lax.broadcasted_iota(jnp.int32, (CHUNK, rows), 0).astype(F32)
    slot_lane = lax.broadcasted_iota(jnp.int32, (rows, CHUNK), 1).astype(F32)
    sides = lax.broadcasted_iota(jnp.int32, (8, LANES), 0)

    def own_spot(c):
        p, q = place.axes(lax.rem(c, 2))
        return q * SIDE + p

    def go(c):
        return [
            to_group(
                outgoing.at[c],
                part.at[c, own_spot(c)],
                go_send.at[c],
                go_recv.at[c],
                flipped(group, chunk_bits(c)),
            ),
            to_group(
                side_out.at[c],
                side_in.at[c],
                side_send.at[c],
                side_recv.at[c],
                flipped(group, chunk_bits(c)),
            ),
        ]

    for c in range(CHUNKS):
        pick = jnp.where(flat_pos[c : c + 1, :] == slot_line, 1.0, 0.0).astype(BF)
        chosen = jnp.dot(pick, source, preferred_element_type=F32)
        at_slot = own_pos[:, c : c + 1] == slot_lane
        w_row = jnp.sum(jnp.where(at_slot, weight[:, c : c + 1], 0.0), axis=0, keepdims=True)
        d_row = jnp.sum(jnp.where(at_slot, dense_here[:, c : c + 1], 0.0), axis=0, keepdims=True)
        side = jnp.where(sides == 0, w_row, jnp.where(sides == 1, d_row, 0.0))
        if c == 0:
            store_own(part.at[0, own_spot(0)], chosen, is_odd)
            side_in[0] = side
            pl.semaphore_wait(barrier, 4 + CHUNKS - 1)
        else:
            store_own(outgoing.at[c], chosen, is_odd)
            side_out[c] = side
            for copy in go(c):
                copy.start()

    spreader = Spreader(place, part, spread_send, spread_recv)
    summer = Summer(place, part, r1, r2, r3, r4, sum_send, sum_recv)

    def back(c):
        return to_group(
            summed.at[c],
            returned.at[c],
            back_send.at[c],
            back_recv.at[c],
            flipped(group, chunk_bits(c)),
        )

    def finish_sum(c):
        summer.arrive(3, c)
        total = summer.total(c).astype(BF)

        @pl.when(c == 0)
        def _():
            returned[0] = total

        @pl.when(c > 0)
        def _():
            summed[c] = total
            back(c).start()

    def compute(c):
        odd = lax.rem(c, 2)
        chunk = part.at[c]
        acc[...] = jnp.zeros_like(acc)

        def gather_products(z, squares):
            block = load_quarter(chunk, odd, z)
            deep = pl.ds(pl.multiple_of(z * 4 * SLICE, 4 * SLICE), 4 * SLICE)
            for k, w in enumerate((w_eg, w_eu, w_dg, w_du)):
                acc[k] += jnp.dot(block, w[deep, :], preferred_element_type=F32)
            for k in range(14):
                wide = block[:, k * LANES : (k + 1) * LANES].astype(F32)
                squares = squares + wide * wide
            return squares

        squares = lax.fori_loop(0, SIDE, gather_products, jnp.zeros((CHUNK, LANES), F32))
        scale = lax.rsqrt(jnp.sum(squares, axis=1, keepdims=True) / width + 1e-05)
        line = lax.broadcasted_iota(jnp.int32, (CHUNK, CHUNK), 0)
        column = lax.broadcasted_iota(jnp.int32, (CHUNK, CHUNK), 1)
        factors = [
            jnp.sum(jnp.where(line == column, side_in[c, k : k + 1, :], 0.0), axis=1, keepdims=True)
            for k in range(2)
        ]
        for k in range(2):
            gate, up = acc[2 * k] * scale, acc[2 * k + 1] * scale
            inner = gate / (1.0 + jnp.exp(-gate)) * up * factors[k]
            hidden[:, k * DENSE_AT : k * DENSE_AT + hidden_size] = inner.astype(BF)

        spreader.sent(c)

        @pl.loop(0, SIDE)
        def _(z):
            columns = pl.ds(pl.multiple_of(z * 4 * SLICE, 4 * SLICE), 4 * SLICE)
            block = jnp.dot(hidden[...], w_down[:, columns], preferred_element_type=F32)
            store_quarter(chunk, odd, z, block)

    hidden[...] = jnp.zeros_like(hidden)
    w_down[hidden_size:DENSE_AT, :] = jnp.zeros((DENSE_AT - hidden_size, width), BF)

    def turn(it, carry):
        def stage(lag, body):
            c = it - lag

            @pl.when((c >= 0) & (c < CHUNKS))
            def _():
                body(c)

        def begin(c):
            @pl.when(c > 0)
            def _():
                for copy in go(c):
                    copy.wait_recv()

            spreader.start(0, c)

        def spread(step):
            def body(c):
                spreader.arrive(step - 1, c)
                spreader.start(step, c)

            return body

        def add(step):
            def body(c):
                summer.arrive(step - 1, c)
                summer.start(step, c)

            return body

        def work(c):
            spreader.arrive(3, c)

            @pl.when(c == 0)
            def _():
                for load in loads:
                    load.wait()

            compute(c)
            summer.start(0, c)

        stage(0, begin)
        stage(1, spread(1))
        stage(2, spread(2))
        stage(3, spread(3))
        stage(5, add(1))
        stage(6, add(2))
        stage(7, add(3))
        stage(8, finish_sum)
        stage(4, work)
        return carry

    lax.fori_loop(0, CHUNKS + 8, turn, 0)

    total = jnp.concatenate(
        [natural_own(state_ref.at[b], is_odd) for b in range(row_blocks)], axis=0
    )
    for c in range(CHUNKS):
        if c > 0:
            back(c).wait_recv()
        at_slot = jnp.where(own_pos[:, c : c + 1] == slot_lane, 1.0, 0.0).astype(BF)
        block = natural_own(returned.at[c], is_odd).astype(BF)
        total = total + jnp.dot(at_slot, block, preferred_element_type=F32)
    for_odd = pltpu.roll(
        jnp.concatenate([total[:, 3 * LANES :], total[:, : 3 * LANES]], axis=1),
        4 * LANES - SHARED,
        1,
    )
    mixed_ref[...] = jnp.where(is_odd == 1, for_odd, total)[:, :SLICE].astype(BF)

    @pl.loop(0, CHUNKS)
    def _(c):
        summer.sent(c)

    for c in range(1, CHUNKS):
        for copy in go(c):
            copy.wait_send()
        back(c).wait_send()


DENSE_AT = 384


def feed(expert_ids, route_weights, state, expert_gate, expert_up, expert_down, dense_gate, dense_up, dense_down):
    rows = expert_ids.shape[0]
    width, hidden_size = dense_gate.shape
    vmem = pl.BlockSpec(memory_space=pltpu.VMEM)
    hbm = pl.BlockSpec(memory_space=pl.ANY)
    return pl.pallas_call(
        feed_kernel,
        out_shape=jax.ShapeDtypeStruct((rows, SLICE), BF),
        in_specs=[vmem] * 4 + [hbm] * 6,
        out_specs=vmem,
        scratch_shapes=[
            pltpu.VMEM((CHUNKS, 16, SLICE, LANES), BF),
            pltpu.VMEM((CHUNKS, 2, 2, SLICE, LANES), BF),
            pltpu.VMEM((CHUNKS, 2, SIDE, SLICE, LANES), BF),
            pltpu.VMEM((CHUNKS, 2, HALF, LANES), BF),
            pltpu.VMEM((CHUNKS, 2, SLICE, LANES), BF),
            pltpu.VMEM((width, hidden_size), BF),
            pltpu.VMEM((width, hidden_size), BF),
            pltpu.VMEM((width, hidden_size), BF),
            pltpu.VMEM((width, hidden_size), BF),
            pltpu.VMEM((DENSE_AT + hidden_size, width), BF),
            pltpu.VMEM((CHUNKS, SLICE, LANES), BF),
            pltpu.VMEM((CHUNKS, 8, LANES), F32),
            pltpu.VMEM((CHUNKS, 8, LANES), F32),
            pltpu.VMEM((CHUNKS, SLICE, LANES), BF),
            pltpu.VMEM((rows, LANES), F32),
            pltpu.VMEM((4, CHUNK, hidden_size), F32),
            pltpu.VMEM((CHUNK, DENSE_AT + hidden_size), BF),
            pltpu.VMEM((CHUNKS, SLICE, LANES), BF),
            pltpu.SemaphoreType.DMA((6,)),
            pltpu.SemaphoreType.DMA((CHUNKS, 4, 2)),
            pltpu.SemaphoreType.DMA((CHUNKS, 4, 2)),
            pltpu.SemaphoreType.DMA((CHUNKS, 4, 2)),
            pltpu.SemaphoreType.DMA((CHUNKS, 4, 2)),
            pltpu.SemaphoreType.DMA((CHUNKS,)),
            pltpu.SemaphoreType.DMA((CHUNKS,)),
            pltpu.SemaphoreType.DMA((CHUNKS,)),
            pltpu.SemaphoreType.DMA((CHUNKS,)),
            pltpu.SemaphoreType.DMA((CHUNKS,)),
            pltpu.SemaphoreType.DMA((CHUNKS,)),
        ],
        compiler_params=pltpu.CompilerParams(
            collective_id=2, has_side_effects=True, vmem_limit_bytes=64 * 1024 * 1024 - 65536
        ),
        name="feed",
    )(
        expert_ids,
        expert_ids.T,
        route_weights,
        state,
        expert_gate,
        expert_up,
        expert_down,
        dense_gate,
        dense_up,
        dense_down,
    )


def from_partner(block):
    return lax.ppermute(block, "tensor", [(i, i ^ 1) for i in range(lax.axis_size("tensor"))])


def attend(queries, new_kv, kv_cache, lengths):
    row_count = queries.shape[0]
    rank = lax.axis_index("tensor")
    my_head, my_part = rank // 2, rank % 2
    head_size = new_kv.shape[3]
    span = kv_cache.shape[2]
    rows = lax.dynamic_index_in_dim(queries, my_head, 1, keepdims=False).reshape(
        row_count, -1, head_size
    )
    new_key = lax.dynamic_index_in_dim(new_kv[0], my_head, 1, keepdims=False)
    new_value = lax.dynamic_index_in_dim(new_kv[1], my_head, 1, keepdims=False)
    scale = 1.0 / math.sqrt(head_size)
    scores = jnp.einsum("tgd,tpd->tgp", rows, kv_cache[0], preferred_element_type=F32) * scale
    own = jnp.einsum("tgd,td->tg", rows, new_key, preferred_element_type=F32) * scale
    position = my_part * span + jnp.arange(span, dtype=jnp.int32)
    usable = position[None, None, :] < lengths[:, None, None]
    masked = jnp.where(usable, scores, -1e30)
    highest = jnp.maximum(jnp.max(masked, axis=-1), own)
    weights = jnp.where(usable, jnp.exp(masked - highest[..., None]), 0.0).astype(BF)
    own_weight = jnp.exp(own - highest)
    leading = (my_part == 0).astype(F32)
    numerator = jnp.einsum("tgp,tpd->tgd", weights, kv_cache[1], preferred_element_type=F32)
    numerator = numerator + leading * own_weight[..., None] * new_value.astype(F32)[:, None, :]
    denominator = jnp.sum(weights.astype(F32), axis=-1) + leading * own_weight
    width = rows.shape[1] * head_size
    flat = numerator.reshape(row_count, width)
    mine = lax.dynamic_slice_in_dim(flat, my_part * (width // 2), width // 2, 1)
    theirs = lax.dynamic_slice_in_dim(flat, (1 - my_part) * (width // 2), width // 2, 1)
    other, other_marks = from_partner((theirs.astype(BF), jnp.stack([highest, denominator])))
    other_highest, other_denominator = other_marks[0], other_marks[1]
    top = jnp.maximum(highest, other_highest)
    keep, take = jnp.exp(highest - top), jnp.exp(other_highest - top)
    below = 1.0 / (denominator * keep + other_denominator * take)
    keep = jnp.repeat(keep * below, head_size, axis=1)
    take = jnp.repeat(take * below, head_size, axis=1)
    keep = lax.dynamic_slice_in_dim(keep, my_part * (width // 2), width // 2, 1)
    take = lax.dynamic_slice_in_dim(take, my_part * (width // 2), width // 2, 1)
    return (mine * keep + other.astype(F32) * take).astype(BF)


def shards(
    residual,
    queries,
    new_kv,
    kv_cache,
    lengths,
    out_weight,
    dense_gate,
    dense_up,
    dense_down,
    expert_ids,
    route_weights,
    expert_gate,
    expert_up,
    expert_down,
):
    attention = attend(queries, new_kv, kv_cache, lengths)
    state = project(attention, out_weight, residual)
    return feed(
        expert_ids,
        route_weights,
        state,
        expert_gate,
        expert_up,
        expert_down,
        dense_gate,
        dense_up,
        dense_down,
    )


def solution(mesh):
    placed = (
        P("group", None),
        P("group", None, None),
        P(None, "group", None, None),
        P(None, "group", "tensor", None),
        P("group"),
        P("tensor", None),
        P(None, "tensor"),
        P(None, "tensor"),
        P("tensor", None),
        P("group", None),
        P("group", None),
        P("group", None, "tensor"),
        P("group", None, "tensor"),
        P("group", "tensor", None),
    )
    return jax.shard_map(
        shards, mesh=mesh, in_specs=placed, out_specs=P("group", "tensor"), check_vma=False
    )
```

```python
import functools
import math

import jax
import jax.numpy as jnp
from jax import lax
from jax.experimental import pallas as pl
from jax.experimental.pallas import tpu as pltpu
from jax.sharding import PartitionSpec as P

BF = jnp.bfloat16
F32 = jnp.float32
SIDE = 4
LANES = 128
CHUNK = 128
SLICE = 448
HALF = SLICE // 2
SHARED = 64
CHUNKS = 8


def ring(value, step):
    return lax.rem(value + step + SIDE, SIDE)


class Place:
    def __init__(self):
        rank = lax.axis_index("tensor")
        self.rank = rank
        self.z = rank // SIDE
        self.x = lax.rem(rank, SIDE)

    def axes(self, half):
        return (self.x, self.z) if half == 0 else (self.z, self.x)

    def at(self, half, p, q):
        return q * SIDE + p if half == 0 else p * SIDE + q


def spot(half, z, x):
    return z * SIDE + x if half == 0 else x * SIDE + z


def split_rows(low, high):
    pieces = []
    if low < HALF:
        pieces.append((0, low, min(high, HALF), 0))
    if high > HALF:
        start = max(low, HALF)
        pieces.append((1, start - HALF, high - HALF, start - low))
    return pieces


def read_rows(part, z, x, low, high):
    pieces = [part[h, spot(h, z, x), a:b, :] for h, a, b, _ in split_rows(low, high)]
    return pieces[0] if len(pieces) == 1 else jnp.concatenate(pieces, axis=0)


def write_rows(part, z, x, low, value):
    for h, a, b, offset in split_rows(low, low + value.shape[0]):
        part[h, spot(h, z, x), a:b, :] = value[offset : offset + b - a]


def copy_to(src, dst, send, recv, rank):
    return pltpu.make_async_remote_copy(
        src_ref=src,
        dst_ref=dst,
        send_sem=send,
        recv_sem=recv,
        device_id={"tensor": rank},
        device_id_type=pl.DeviceIdType.MESH,
    )


def lanes_low(rows):
    return lax.broadcasted_iota(jnp.int32, (rows, LANES), 1) < SHARED


def turned(block):
    return pltpu.roll(block, SHARED, 1)


def unfold_pair(even_half, odd_half):
    low = lanes_low(SHARED)
    e, o = even_half.astype(F32), odd_half.astype(F32)
    top = jnp.where(low, e, o)
    bottom = turned(jnp.where(low, o, e))
    return jnp.concatenate([top, bottom], axis=0).astype(BF)


def fold_pair(tile):
    low = lanes_low(SHARED)
    top, bottom = tile[:SHARED], turned(tile[SHARED:])
    return jnp.where(low, top, bottom).astype(BF), jnp.where(low, bottom, top).astype(BF)


def unfold_own(half):
    half = half.astype(F32)
    return jnp.concatenate([half, turned(half)], axis=0)


def fold_own(tile, is_odd):
    low = lanes_low(SHARED).astype(jnp.int32) != is_odd
    top, bottom = tile[:SHARED], turned(tile[SHARED:])
    return jnp.where(low, top, bottom)


def natural_own(ref, is_odd):
    first = pl.multiple_of(is_odd * SHARED, SHARED)
    half = pl.multiple_of((1 - is_odd) * (SLICE - SHARED), SHARED)
    tiles = [ref[pl.ds(first + k * LANES, LANES), :].astype(F32) for k in range(3)]
    return jnp.concatenate(tiles + [unfold_own(ref[pl.ds(half, SHARED), :])], axis=1)


def store_own(ref, block, is_odd):
    first = pl.multiple_of(is_odd * SHARED, SHARED)
    half = pl.multiple_of((1 - is_odd) * (SLICE - SHARED), SHARED)
    for k in range(3):
        ref[pl.ds(first + k * LANES, LANES), :] = block[:, k * LANES : (k + 1) * LANES].astype(BF)
    ref[pl.ds(half, SHARED), :] = fold_own(block[:, 3 * LANES :], is_odd).astype(BF)


def store_quarter(part, z, block):
    for pair in range(2):
        e, o = 2 * pair, 2 * pair + 1
        tiles = [
            block[:, (pair * 7 + k) * LANES : (pair * 7 + k + 1) * LANES] for k in range(7)
        ]
        even_half, odd_half = fold_pair(tiles[3])
        for k in range(3):
            write_rows(part, z, e, k * LANES, tiles[k].astype(BF))
            write_rows(part, z, o, SHARED + k * LANES, tiles[4 + k].astype(BF))
        write_rows(part, z, e, SLICE - SHARED, even_half)
        write_rows(part, z, o, 0, odd_half)


def load_quarter(part, z):
    blocks = []
    for pair in range(2):
        e, o = 2 * pair, 2 * pair + 1
        blocks += [read_rows(part, z, e, k * LANES, (k + 1) * LANES) for k in range(3)]
        blocks.append(
            unfold_pair(
                read_rows(part, z, e, SLICE - SHARED, SLICE), read_rows(part, z, o, 0, SHARED)
            )
        )
        blocks += [
            read_rows(part, z, o, SHARED + k * LANES, SHARED + (k + 1) * LANES) for k in range(3)
        ]
    return jnp.concatenate(blocks, axis=1)


def add_into(dst, other):
    dst[...] = (dst[...].astype(F32) + other[...].astype(F32)).astype(BF)


class Exchange:
    def start(self, step, c):
        for copy in self.copies(step, c):
            copy.start()

    def arrive(self, step, c):
        for copy in self.copies(step, c):
            copy.wait_recv()

    def sent(self, c):
        for step in range(4):
            for copy in self.copies(step, c):
                copy.wait_send()


WAYS = ((0, 0, 1), (0, 1, -1), (1, 0, 1), (1, 1, -1))
QUARTER = HALF // 2


class Summer(Exchange):
    def __init__(self, place, part, landing, send, recv):
        self.place, self.part, self.landing = place, part, landing
        self.send, self.recv = send, recv

    def copies(self, step, c):
        place = self.place
        result = []
        for h, way, hop in WAYS:
            part = self.part.at[c, h]
            p, q = place.axes(h)
            if step == 0:
                src = part.at[pl.ds(ring(q, 2) * SIDE + 2 * way, 2)]
                to = place.at(h, p, ring(q, hop))
            elif step == 1:
                src = part.at[pl.ds(ring(q, hop) * SIDE, SIDE)]
                to = place.at(h, p, ring(q, hop))
            elif step == 2:
                src = part.at[q * SIDE + ring(p, 2), pl.ds(way * QUARTER, QUARTER)]
                to = place.at(h, ring(p, hop), q)
            else:
                src = part.at[q * SIDE + ring(p, hop)]
                to = place.at(h, ring(p, hop), q)
            result.append(
                copy_to(
                    src,
                    self.landing[step].at[c, h, way],
                    self.send.at[c, step, h, way],
                    self.recv.at[c, step, h, way],
                    to,
                )
            )
        return result

    def add(self, step, c):
        for h in range(2):
            part = self.part.at[c, h]
            p, q = self.place.axes(h)
            landed = self.landing[step].at[c, h]
            if step == 0:
                for way, hop in ((0, 1), (1, -1)):
                    for k in range(2):
                        add_into(part.at[ring(q, hop) * SIDE + 2 * way + k], landed.at[way, k])
            elif step == 1:
                for k in range(SIDE):
                    dst = part.at[q * SIDE + k]
                    dst[...] = (
                        dst[...].astype(F32) + landed[0, k].astype(F32) + landed[1, k].astype(F32)
                    ).astype(BF)
            elif step == 2:
                for way, hop in ((0, 1), (1, -1)):
                    add_into(
                        part.at[q * SIDE + ring(p, hop), pl.ds(way * QUARTER, QUARTER)],
                        landed.at[way],
                    )

    def total(self, c):
        halves = []
        for h in range(2):
            p, q = self.place.axes(h)
            landed = self.landing[3].at[c, h]
            halves.append(
                self.part[c, h, q * SIDE + p].astype(F32)
                + landed[0].astype(F32)
                + landed[1].astype(F32)
            )
        return jnp.concatenate(halves, axis=0)


class Spreader(Exchange):
    def __init__(self, place, part, send, recv):
        self.place, self.part, self.send, self.recv = place, part, send, recv

    def copies(self, step, c):
        place = self.place
        result = []
        for h, way, hop in WAYS:
            part = self.part.at[c, h]
            p, q = place.axes(h)
            if step == 0:
                ref = part.at[q * SIDE + p]
                to = place.at(h, ring(p, hop), q)
            elif step == 1:
                ref = part.at[q * SIDE + ring(p, -hop), pl.ds(way * QUARTER, QUARTER)]
                to = place.at(h, ring(p, hop), q)
            elif step == 2:
                ref = part.at[pl.ds(q * SIDE, SIDE)]
                to = place.at(h, p, ring(q, hop))
            else:
                ref = part.at[pl.ds(ring(q, -hop) * SIDE + 2 * way, 2)]
                to = place.at(h, p, ring(q, hop))
            result.append(
                copy_to(
                    ref,
                    ref,
                    self.send.at[c, step, h, way],
                    self.recv.at[c, step, h, way],
                    to,
                )
            )
        return result


def greet_plane(place, barrier):
    for hop in (1, -1):
        for rank in (
            place.at(0, ring(place.x, hop), place.z),
            place.at(0, place.x, ring(place.z, hop)),
        ):
            pl.semaphore_signal(
                barrier, inc=1, device_id={"tensor": rank}, device_id_type=pl.DeviceIdType.MESH
            )


def project_kernel(
    att_ref, weight_ref, residual_ref, state_ref, part, r1, r2, r3, r4, near, send, recv, local
):
    place = Place()
    barrier = pltpu.get_barrier_semaphore()
    greet_plane(place, barrier)
    pl.semaphore_wait(barrier, 4)
    is_odd = lax.rem(place.rank, 2)
    first_column = pl.multiple_of((place.rank // 2) * 2 * SLICE, 2 * SLICE)
    fetch = pltpu.make_async_copy(
        residual_ref.at[:, pl.ds(first_column, 2 * SLICE)], near, local
    )
    fetch.start()
    summer = Summer(place, part, (r1, r2, r3, r4), send, recv)
    count = part.shape[0]
    for c in range(count):
        rows = att_ref[c * CHUNK : (c + 1) * CHUNK, :]

        @pl.loop(0, SIDE)
        def _(z):
            columns = pl.ds(pl.multiple_of(z * 4 * SLICE, 4 * SLICE), 4 * SLICE)
            block = jnp.dot(rows, weight_ref[:, columns], preferred_element_type=F32)
            store_quarter(part.at[c], z, block)

        summer.start(0, c)
    for step in range(1, 4):
        for c in range(count):
            summer.arrive(step - 1, c)
            summer.add(step - 1, c)
            summer.start(step, c)
    fetch.wait()
    for c in range(count):
        summer.arrive(3, c)
        rows = pl.ds(c * CHUNK, CHUNK)
        even = [near[rows, k * LANES : (k + 1) * LANES] for k in range(4)]
        odd = [near[rows, (k + 3) * LANES : (k + 4) * LANES] for k in range(4)]
        whole = jnp.concatenate(
            [
                jnp.where(is_odd == 1, odd[k + 1].astype(F32), even[k].astype(F32))
                for k in range(3)
            ]
            + [even[3].astype(F32)],
            axis=1,
        )
        store_own(state_ref.at[c], whole, is_odd)
        state_ref[c] = (state_ref[c].astype(F32) + summer.total(c)).astype(BF)
    for c in range(count):
        summer.sent(c)


def project(attention, out_weight, residual):
    count = attention.shape[0] // CHUNK
    return pl.pallas_call(
        project_kernel,
        out_shape=jax.ShapeDtypeStruct((count, SLICE, LANES), BF),
        in_specs=[
            pl.BlockSpec(memory_space=pltpu.VMEM),
            pl.BlockSpec(memory_space=pltpu.VMEM),
            pl.BlockSpec(memory_space=pl.ANY),
        ],
        out_specs=pl.BlockSpec(memory_space=pltpu.VMEM),
        scratch_shapes=[
            pltpu.VMEM((count, 2, 16, HALF, LANES), BF),
            pltpu.VMEM((count, 2, 2, 2, HALF, LANES), BF),
            pltpu.VMEM((count, 2, 2, SIDE, HALF, LANES), BF),
            pltpu.VMEM((count, 2, 2, QUARTER, LANES), BF),
            pltpu.VMEM((count, 2, 2, HALF, LANES), BF),
            pltpu.VMEM((attention.shape[0], 2 * SLICE), BF),
            pltpu.SemaphoreType.DMA((count, 4, 2, 2)),
            pltpu.SemaphoreType.DMA((count, 4, 2, 2)),
            pltpu.SemaphoreType.DMA,
        ],
        compiler_params=pltpu.CompilerParams(
            collective_id=1, has_side_effects=True, vmem_limit_bytes=48 * 1024 * 1024
        ),
        name="project",
    )(attention, out_weight, residual)


def flipped(group, bits):
    b = (lax.rem(group, 2), lax.rem(group // 2, 2), group // 4)
    return sum((b[k] + bits[k] - 2 * b[k] * bits[k]) * (1 << k) for k in range(3))


def chunk_bits(c):
    if isinstance(c, int):
        a, b, d = c % 2, (c // 2) % 2, c // 4
    else:
        a, b, d = lax.rem(c, 2), lax.rem(c // 2, 2), c // 4
    return a, b + d - 2 * b * d, d


def to_group(src, dst, send, recv, group):
    return pltpu.make_async_remote_copy(
        src_ref=src,
        dst_ref=dst,
        send_sem=send,
        recv_sem=recv,
        device_id={"group": group},
        device_id_type=pl.DeviceIdType.MESH,
    )


def feed_kernel(
    ids_ref,
    flat_ids_ref,
    route_ref,
    state_ref,
    expert_gate,
    expert_up,
    expert_down,
    dense_gate,
    dense_up,
    dense_down,
    mixed_ref,
    part,
    r1,
    r2,
    r3,
    r4,
    w_in,
    w_down,
    outgoing,
    side_out,
    side_in,
    returned,
    own_pos,
    acc,
    hidden,
    summed,
    load_sem,
    spread_send,
    spread_recv,
    sum_send,
    sum_recv,
    go_send,
    go_recv,
    side_send,
    side_recv,
    back_send,
    back_recv,
):
    place = Place()
    group = lax.axis_index("group")
    rank = place.rank
    is_odd = lax.rem(rank, 2)
    hidden_size = w_in.shape[0] // 4
    rows = ids_ref.shape[0]
    row_blocks = rows // CHUNK
    width = 16 * SLICE

    loads = [
        pltpu.make_async_copy(
            ref, w_in.at[pl.ds(k * hidden_size, hidden_size)], load_sem.at[k]
        )
        for k, ref in enumerate((expert_gate.at[0], expert_up.at[0], dense_gate, dense_up))
    ] + [
        pltpu.make_async_copy(expert_down.at[0], w_down.at[pl.ds(0, hidden_size)], load_sem.at[4]),
        pltpu.make_async_copy(
            dense_down, w_down.at[pl.ds(DENSE_AT, hidden_size)], load_sem.at[5]
        ),
    ]
    for load in loads:
        load.start()

    barrier = pltpu.get_barrier_semaphore()
    greet_plane(place, barrier)
    for c in range(1, CHUNKS):
        pl.semaphore_signal(
            barrier,
            inc=1,
            device_id={"group": flipped(group, chunk_bits(c))},
            device_id_type=pl.DeviceIdType.MESH,
        )

    ids = ids_ref[...]
    flat_ids = flat_ids_ref[...]
    lane = lax.broadcasted_iota(jnp.int32, (rows, LANES), 1)
    partner_of_lane = sum(
        jnp.where(lane == c, flipped(group, chunk_bits(c)) + 1, 0) for c in range(CHUNKS)
    ) - 1
    first_choice = ids[:, 0:1] == partner_of_lane
    second_choice = ids[:, 1:2] == partner_of_lane
    named = jnp.where(first_choice | second_choice, 1.0, 0.0)
    line = lax.broadcasted_iota(jnp.int32, (rows, rows), 0)
    column = lax.broadcasted_iota(jnp.int32, (rows, rows), 1)
    before = jnp.where(column < line, 1.0, 0.0).astype(BF)
    place_in = jnp.dot(before, named.astype(BF), preferred_element_type=F32)
    own_pos[...] = jnp.where(named > 0.5, place_in, -1.0)

    sub = lax.broadcasted_iota(jnp.int32, (8, rows), 0)
    partner_of_sub = sum(
        jnp.where(sub == c, flipped(group, chunk_bits(c)) + 1, 0) for c in range(CHUNKS)
    ) - 1
    flat_named = jnp.where(
        (flat_ids[0:1, :] == partner_of_sub) | (flat_ids[1:2, :] == partner_of_sub), 1.0, 0.0
    )
    after = jnp.where(line < column, 1.0, 0.0).astype(BF)
    flat_place = jnp.dot(flat_named.astype(BF), after, preferred_element_type=F32)
    flat_pos = jnp.where(flat_named > 0.5, flat_place, -1.0)

    weight = jnp.where(first_choice, route_ref[:, 0:1], 0.0) + jnp.where(
        second_choice, route_ref[:, 1:2], 0.0
    )
    dense_here = jnp.where(first_choice, 1.0, 0.0)
    source = jnp.concatenate(
        [natural_own(state_ref.at[b], is_odd) for b in range(row_blocks)], axis=0
    ).astype(BF)
    slot_line = lax.broadcasted_iota(jnp.int32, (CHUNK, rows), 0).astype(F32)
    slot_lane = lax.broadcasted_iota(jnp.int32, (rows, CHUNK), 1).astype(F32)
    sides = lax.broadcasted_iota(jnp.int32, (8, LANES), 0)

    def go(c):
        to = flipped(group, chunk_bits(c))
        return [
            to_group(
                outgoing.at[c, pl.ds(h * HALF, HALF)],
                part.at[c, h, spot(h, place.z, place.x)],
                go_send.at[c, h],
                go_recv.at[c, h],
                to,
            )
            for h in range(2)
        ] + [to_group(side_out.at[c], side_in.at[c], side_send.at[c], side_recv.at[c], to)]

    for c in range(CHUNKS):
        pick = jnp.where(flat_pos[c : c + 1, :] == slot_line, 1.0, 0.0).astype(BF)
        chosen = jnp.dot(pick, source, preferred_element_type=F32)
        at_slot = own_pos[:, c : c + 1] == slot_lane
        w_row = jnp.sum(jnp.where(at_slot, weight[:, c : c + 1], 0.0), axis=0, keepdims=True)
        d_row = jnp.sum(jnp.where(at_slot, dense_here[:, c : c + 1], 0.0), axis=0, keepdims=True)
        side = jnp.where(sides == 0, w_row, jnp.where(sides == 1, d_row, 0.0))
        store_own(outgoing.at[c], chosen, is_odd)
        if c == 0:
            for h in range(2):
                part[0, h, spot(h, place.z, place.x)] = outgoing[0, h * HALF : (h + 1) * HALF, :]
            side_in[0] = side
            pl.semaphore_wait(barrier, 4 + CHUNKS - 1)
        else:
            side_out[c] = side
            for copy in go(c):
                copy.start()

    spreader = Spreader(place, part, spread_send, spread_recv)
    summer = Summer(place, part, (r1, r2, r3, r4), sum_send, sum_recv)

    def back(c):
        return to_group(
            summed.at[c],
            returned.at[c],
            back_send.at[c],
            back_recv.at[c],
            flipped(group, chunk_bits(c)),
        )

    def finish_sum(c):
        summer.arrive(3, c)
        total = summer.total(c).astype(BF)

        @pl.when(c == 0)
        def _():
            returned[0] = total

        @pl.when(c > 0)
        def _():
            summed[c] = total
            back(c).start()

    def compute(c):
        chunk = part.at[c]
        acc[...] = jnp.zeros_like(acc)

        def gather_products(z, squares):
            block = load_quarter(chunk, z)
            deep = pl.ds(pl.multiple_of(z * 4 * SLICE, 4 * SLICE), 4 * SLICE)
            acc[...] += lax.dot_general(
                block, w_in[:, deep], (((1,), (1,)), ((), ())), preferred_element_type=F32
            )
            for k in range(14):
                wide = block[:, k * LANES : (k + 1) * LANES].astype(F32)
                squares = squares + wide * wide
            return squares

        squares = lax.fori_loop(0, SIDE, gather_products, jnp.zeros((CHUNK, LANES), F32))
        scale = lax.rsqrt(jnp.sum(squares, axis=1, keepdims=True) / width + 1e-05)
        line = lax.broadcasted_iota(jnp.int32, (CHUNK, CHUNK), 0)
        column = lax.broadcasted_iota(jnp.int32, (CHUNK, CHUNK), 1)
        factors = [
            jnp.sum(jnp.where(line == column, side_in[c, k : k + 1, :], 0.0), axis=1, keepdims=True)
            for k in range(2)
        ]
        for k in range(2):
            gate, up = [
                acc[:, (2 * k + j) * hidden_size : (2 * k + j + 1) * hidden_size] * scale
                for j in range(2)
            ]
            inner = gate / (1.0 + jnp.exp(-gate)) * up * factors[k]
            hidden[:, k * DENSE_AT : k * DENSE_AT + hidden_size] = inner.astype(BF)

        spreader.sent(c)

        @pl.loop(0, SIDE)
        def _(z):
            columns = pl.ds(pl.multiple_of(z * 4 * SLICE, 4 * SLICE), 4 * SLICE)
            block = jnp.dot(hidden[...], w_down[:, columns], preferred_element_type=F32)
            store_quarter(chunk, z, block)

    hidden[...] = jnp.zeros_like(hidden)
    w_down[hidden_size:DENSE_AT, :] = jnp.zeros((DENSE_AT - hidden_size, width), BF)

    def turn(it, carry):
        def stage(lag, body):
            c = it - lag

            @pl.when((c >= 0) & (c < CHUNKS))
            def _():
                body(c)

        def begin(c):
            @pl.when(c > 0)
            def _():
                for copy in go(c):
                    copy.wait_recv()

            spreader.start(0, c)

        def spread(step):
            def body(c):
                spreader.arrive(step - 1, c)
                spreader.start(step, c)

            return body

        def add(step):
            def body(c):
                summer.arrive(step - 1, c)
                summer.add(step - 1, c)
                summer.start(step, c)

            return body

        def work(c):
            spreader.arrive(3, c)

            @pl.when(c == 0)
            def _():
                for load in loads:
                    load.wait()

            compute(c)
            summer.start(0, c)

        stage(0, begin)
        stage(1, spread(1))
        stage(2, spread(2))
        stage(3, spread(3))
        stage(5, add(1))
        stage(6, add(2))
        stage(7, add(3))
        stage(8, finish_sum)
        stage(4, work)
        return carry

    lax.fori_loop(0, CHUNKS + 8, turn, 0)

    total = jnp.concatenate(
        [natural_own(state_ref.at[b], is_odd) for b in range(row_blocks)], axis=0
    )
    for c in range(CHUNKS):
        if c > 0:
            back(c).wait_recv()
        at_slot = jnp.where(own_pos[:, c : c + 1] == slot_lane, 1.0, 0.0).astype(BF)
        block = natural_own(returned.at[c], is_odd).astype(BF)
        total = total + jnp.dot(at_slot, block, preferred_element_type=F32)
    for_odd = pltpu.roll(
        jnp.concatenate([total[:, 3 * LANES :], total[:, : 3 * LANES]], axis=1),
        4 * LANES - SHARED,
        1,
    )
    mixed_ref[...] = jnp.where(is_odd == 1, for_odd, total)[:, :SLICE].astype(BF)

    @pl.loop(0, CHUNKS)
    def _(c):
        summer.sent(c)

    for c in range(1, CHUNKS):
        for copy in go(c):
            copy.wait_send()
        back(c).wait_send()


DENSE_AT = 384


def feed(expert_ids, route_weights, state, expert_gate, expert_up, expert_down, dense_gate, dense_up, dense_down):
    rows = expert_ids.shape[0]
    width, hidden_size = dense_gate.shape
    vmem = pl.BlockSpec(memory_space=pltpu.VMEM)
    hbm = pl.BlockSpec(memory_space=pl.ANY)
    return pl.pallas_call(
        feed_kernel,
        out_shape=jax.ShapeDtypeStruct((rows, SLICE), BF),
        in_specs=[vmem] * 4 + [hbm] * 6,
        out_specs=vmem,
        scratch_shapes=[
            pltpu.VMEM((CHUNKS, 2, 16, HALF, LANES), BF),
            pltpu.VMEM((CHUNKS, 2, 2, 2, HALF, LANES), BF),
            pltpu.VMEM((CHUNKS, 2, 2, SIDE, HALF, LANES), BF),
            pltpu.VMEM((CHUNKS, 2, 2, QUARTER, LANES), BF),
            pltpu.VMEM((CHUNKS, 2, 2, HALF, LANES), BF),
            pltpu.VMEM((4 * hidden_size, width), BF),
            pltpu.VMEM((DENSE_AT + hidden_size, width), BF),
            pltpu.VMEM((CHUNKS, SLICE, LANES), BF),
            pltpu.VMEM((CHUNKS, 8, LANES), F32),
            pltpu.VMEM((CHUNKS, 8, LANES), F32),
            pltpu.VMEM((CHUNKS, SLICE, LANES), BF),
            pltpu.VMEM((rows, LANES), F32),
            pltpu.VMEM((CHUNK, 4 * hidden_size), F32),
            pltpu.VMEM((CHUNK, DENSE_AT + hidden_size), BF),
            pltpu.VMEM((CHUNKS, SLICE, LANES), BF),
            pltpu.SemaphoreType.DMA((6,)),
            pltpu.SemaphoreType.DMA((CHUNKS, 4, 2, 2)),
            pltpu.SemaphoreType.DMA((CHUNKS, 4, 2, 2)),
            pltpu.SemaphoreType.DMA((CHUNKS, 4, 2, 2)),
            pltpu.SemaphoreType.DMA((CHUNKS, 4, 2, 2)),
            pltpu.SemaphoreType.DMA((CHUNKS, 2)),
            pltpu.SemaphoreType.DMA((CHUNKS, 2)),
            pltpu.SemaphoreType.DMA((CHUNKS,)),
            pltpu.SemaphoreType.DMA((CHUNKS,)),
            pltpu.SemaphoreType.DMA((CHUNKS,)),
            pltpu.SemaphoreType.DMA((CHUNKS,)),
        ],
        compiler_params=pltpu.CompilerParams(
            collective_id=2, has_side_effects=True, vmem_limit_bytes=64 * 1024 * 1024 - 65536
        ),
        name="feed",
    )(
        expert_ids,
        expert_ids.T,
        route_weights,
        state,
        jnp.swapaxes(expert_gate, 1, 2),
        jnp.swapaxes(expert_up, 1, 2),
        expert_down,
        dense_gate.T,
        dense_up.T,
        dense_down,
    )


def from_partner(block):
    return lax.ppermute(block, "tensor", [(i, i ^ 1) for i in range(lax.axis_size("tensor"))])


def attend(queries, new_kv, kv_cache, lengths):
    row_count = queries.shape[0]
    rank = lax.axis_index("tensor")
    my_head, my_part = rank // 2, rank % 2
    head_size = new_kv.shape[3]
    span = kv_cache.shape[2]
    rows = lax.dynamic_index_in_dim(queries, my_head, 1, keepdims=False).reshape(
        row_count, -1, head_size
    )
    new_key = lax.dynamic_index_in_dim(new_kv[0], my_head, 1, keepdims=False)
    new_value = lax.dynamic_index_in_dim(new_kv[1], my_head, 1, keepdims=False)
    scale = 1.0 / math.sqrt(head_size)
    scores = jnp.einsum("tgd,tpd->tgp", rows, kv_cache[0], preferred_element_type=F32) * scale
    own = jnp.einsum("tgd,td->tg", rows, new_key, preferred_element_type=F32) * scale
    position = my_part * span + jnp.arange(span, dtype=jnp.int32)
    usable = position[None, None, :] < lengths[:, None, None]
    masked = jnp.where(usable, scores, -1e30)
    highest = jnp.maximum(jnp.max(masked, axis=-1), own)
    weights = jnp.where(usable, jnp.exp(masked - highest[..., None]), 0.0).astype(BF)
    own_weight = jnp.exp(own - highest)
    leading = (my_part == 0).astype(F32)
    numerator = jnp.einsum("tgp,tpd->tgd", weights, kv_cache[1], preferred_element_type=F32)
    numerator = numerator + leading * own_weight[..., None] * new_value.astype(F32)[:, None, :]
    denominator = jnp.sum(weights.astype(F32), axis=-1) + leading * own_weight
    width = rows.shape[1] * head_size
    flat = numerator.reshape(row_count, width)
    mine = lax.dynamic_slice_in_dim(flat, my_part * (width // 2), width // 2, 1)
    theirs = lax.dynamic_slice_in_dim(flat, (1 - my_part) * (width // 2), width // 2, 1)
    other, other_marks = from_partner((theirs.astype(BF), jnp.stack([highest, denominator])))
    other_highest, other_denominator = other_marks[0], other_marks[1]
    top = jnp.maximum(highest, other_highest)
    keep, take = jnp.exp(highest - top), jnp.exp(other_highest - top)
    below = 1.0 / (denominator * keep + other_denominator * take)
    keep = jnp.repeat(keep * below, head_size, axis=1)
    take = jnp.repeat(take * below, head_size, axis=1)
    keep = lax.dynamic_slice_in_dim(keep, my_part * (width // 2), width // 2, 1)
    take = lax.dynamic_slice_in_dim(take, my_part * (width // 2), width // 2, 1)
    return (mine * keep + other.astype(F32) * take).astype(BF)


def shards(
    residual,
    queries,
    new_kv,
    kv_cache,
    lengths,
    out_weight,
    dense_gate,
    dense_up,
    dense_down,
    expert_ids,
    route_weights,
    expert_gate,
    expert_up,
    expert_down,
):
    attention = attend(queries, new_kv, kv_cache, lengths)
    state = project(attention, out_weight, residual)
    return feed(
        expert_ids,
        route_weights,
        state,
        expert_gate,
        expert_up,
        expert_down,
        dense_gate,
        dense_up,
        dense_down,
    )


def solution(mesh):
    placed = (
        P("group", None),
        P("group", None, None),
        P(None, "group", None, None),
        P(None, "group", "tensor", None),
        P("group"),
        P("tensor", None),
        P(None, "tensor"),
        P(None, "tensor"),
        P("tensor", None),
        P("group", None),
        P("group", None),
        P("group", None, "tensor"),
        P("group", None, "tensor"),
        P("group", "tensor", None),
    )
    return jax.shard_map(
        shards, mesh=mesh, in_specs=placed, out_specs=P("group", "tensor"), check_vma=False
    )
```

```python
import functools
import math

import jax
import jax.numpy as jnp
from jax import lax
from jax.experimental import pallas as pl
from jax.experimental.pallas import tpu as pltpu
from jax.sharding import PartitionSpec as P

BF = jnp.bfloat16
F32 = jnp.float32
SIDE = 4
LANES = 128
CHUNK = 128
SLICE = 448
HALF = SLICE // 2
SHARED = 64
CHUNKS = 8


def ring(value, step):
    return lax.rem(value + step + SIDE, SIDE)


class Place:
    def __init__(self):
        rank = lax.axis_index("tensor")
        self.rank = rank
        self.z = rank // SIDE
        self.x = lax.rem(rank, SIDE)

    def axes(self, half):
        return (self.x, self.z) if half == 0 else (self.z, self.x)

    def at(self, half, p, q):
        return q * SIDE + p if half == 0 else p * SIDE + q


def spot(half, z, x):
    return z * SIDE + x if half == 0 else x * SIDE + z


def split_rows(low, high):
    pieces = []
    if low < HALF:
        pieces.append((0, low, min(high, HALF), 0))
    if high > HALF:
        start = max(low, HALF)
        pieces.append((1, start - HALF, high - HALF, start - low))
    return pieces


def read_rows(part, z, x, low, high):
    pieces = [part[h, spot(h, z, x), a:b, :] for h, a, b, _ in split_rows(low, high)]
    return pieces[0] if len(pieces) == 1 else jnp.concatenate(pieces, axis=0)


def write_rows(part, z, x, low, value):
    for h, a, b, offset in split_rows(low, low + value.shape[0]):
        part[h, spot(h, z, x), a:b, :] = value[offset : offset + b - a]


def copy_to(src, dst, send, recv, rank):
    return pltpu.make_async_remote_copy(
        src_ref=src,
        dst_ref=dst,
        send_sem=send,
        recv_sem=recv,
        device_id={"tensor": rank},
        device_id_type=pl.DeviceIdType.MESH,
    )


def lanes_low(rows):
    return lax.broadcasted_iota(jnp.int32, (rows, LANES), 1) < SHARED


def turned(block):
    return pltpu.roll(block, SHARED, 1)


def unfold_pair(even_half, odd_half):
    low = lanes_low(SHARED)
    e, o = even_half.astype(F32), odd_half.astype(F32)
    top = jnp.where(low, e, o)
    bottom = turned(jnp.where(low, o, e))
    return jnp.concatenate([top, bottom], axis=0).astype(BF)


def fold_pair(tile):
    low = lanes_low(SHARED)
    top, bottom = tile[:SHARED], turned(tile[SHARED:])
    return jnp.where(low, top, bottom).astype(BF), jnp.where(low, bottom, top).astype(BF)


def unfold_own(half):
    half = half.astype(F32)
    return jnp.concatenate([half, turned(half)], axis=0)


def fold_own(tile, is_odd):
    low = lanes_low(SHARED).astype(jnp.int32) != is_odd
    top, bottom = tile[:SHARED], turned(tile[SHARED:])
    return jnp.where(low, top, bottom)


def natural_own(ref, is_odd):
    first = pl.multiple_of(is_odd * SHARED, SHARED)
    half = pl.multiple_of((1 - is_odd) * (SLICE - SHARED), SHARED)
    tiles = [ref[pl.ds(first + k * LANES, LANES), :].astype(F32) for k in range(3)]
    return jnp.concatenate(tiles + [unfold_own(ref[pl.ds(half, SHARED), :])], axis=1)


def store_own(ref, block, is_odd):
    first = pl.multiple_of(is_odd * SHARED, SHARED)
    half = pl.multiple_of((1 - is_odd) * (SLICE - SHARED), SHARED)
    for k in range(3):
        ref[pl.ds(first + k * LANES, LANES), :] = block[:, k * LANES : (k + 1) * LANES].astype(BF)
    ref[pl.ds(half, SHARED), :] = fold_own(block[:, 3 * LANES :], is_odd).astype(BF)


def store_quarter(part, z, block):
    for pair in range(2):
        e, o = 2 * pair, 2 * pair + 1
        tiles = [
            block[:, (pair * 7 + k) * LANES : (pair * 7 + k + 1) * LANES] for k in range(7)
        ]
        even_half, odd_half = fold_pair(tiles[3])
        for k in range(3):
            write_rows(part, z, e, k * LANES, tiles[k].astype(BF))
            write_rows(part, z, o, SHARED + k * LANES, tiles[4 + k].astype(BF))
        write_rows(part, z, e, SLICE - SHARED, even_half)
        write_rows(part, z, o, 0, odd_half)


def load_quarter(part, z):
    blocks = []
    for pair in range(2):
        e, o = 2 * pair, 2 * pair + 1
        blocks += [read_rows(part, z, e, k * LANES, (k + 1) * LANES) for k in range(3)]
        blocks.append(
            unfold_pair(
                read_rows(part, z, e, SLICE - SHARED, SLICE), read_rows(part, z, o, 0, SHARED)
            )
        )
        blocks += [
            read_rows(part, z, o, SHARED + k * LANES, SHARED + (k + 1) * LANES) for k in range(3)
        ]
    return jnp.concatenate(blocks, axis=1)


def add_into(dst, other):
    dst[...] = (dst[...].astype(F32) + other[...].astype(F32)).astype(BF)


class Exchange:
    def start(self, step, c):
        for copy in self.copies(step, c):
            copy.start()

    def arrive(self, step, c):
        for copy in self.copies(step, c):
            copy.wait_recv()

    def sent(self, c):
        for step in range(4):
            for copy in self.copies(step, c):
                copy.wait_send()


WAYS = ((0, 0, 1), (0, 1, -1), (1, 0, 1), (1, 1, -1))
QUARTER = HALF // 2


class Summer(Exchange):
    def __init__(self, place, part, landing, send, recv):
        self.place, self.part, self.landing = place, part, landing
        self.send, self.recv = send, recv

    def landed(self, step, c):
        landing = self.landing[step]
        return landing.at[lax.rem(c, landing.shape[0])]

    def copies(self, step, c):
        place = self.place
        result = []
        for h, way, hop in WAYS:
            part = self.part.at[c, h]
            p, q = place.axes(h)
            if step == 0:
                src = part.at[pl.ds(ring(q, 2) * SIDE + 2 * way, 2)]
                to = place.at(h, p, ring(q, hop))
            elif step == 1:
                src = part.at[pl.ds(ring(q, hop) * SIDE, SIDE)]
                to = place.at(h, p, ring(q, hop))
            elif step == 2:
                src = part.at[q * SIDE + ring(p, 2), pl.ds(way * QUARTER, QUARTER)]
                to = place.at(h, ring(p, hop), q)
            else:
                src = part.at[q * SIDE + ring(p, hop)]
                to = place.at(h, ring(p, hop), q)
            result.append(
                copy_to(
                    src,
                    self.landed(step, c).at[h, way],
                    self.send.at[c, step, h, way],
                    self.recv.at[c, step, h, way],
                    to,
                )
            )
        return result

    def add(self, step, c):
        for h in range(2):
            part = self.part.at[c, h]
            p, q = self.place.axes(h)
            landed = self.landed(step, c).at[h]
            if step == 0:
                for way, hop in ((0, 1), (1, -1)):
                    for k in range(2):
                        add_into(part.at[ring(q, hop) * SIDE + 2 * way + k], landed.at[way, k])
            elif step == 1:
                for k in range(SIDE):
                    dst = part.at[q * SIDE + k]
                    dst[...] = (
                        dst[...].astype(F32) + landed[0, k].astype(F32) + landed[1, k].astype(F32)
                    ).astype(BF)
            elif step == 2:
                for way, hop in ((0, 1), (1, -1)):
                    add_into(
                        part.at[q * SIDE + ring(p, hop), pl.ds(way * QUARTER, QUARTER)],
                        landed.at[way],
                    )

    def total(self, c):
        halves = []
        for h in range(2):
            p, q = self.place.axes(h)
            landed = self.landed(3, c).at[h]
            halves.append(
                self.part[c, h, q * SIDE + p].astype(F32)
                + landed[0].astype(F32)
                + landed[1].astype(F32)
            )
        return jnp.concatenate(halves, axis=0)


class Spreader(Exchange):
    def __init__(self, place, part, send, recv):
        self.place, self.part, self.send, self.recv = place, part, send, recv

    def copies(self, step, c):
        place = self.place
        result = []
        for h, way, hop in WAYS:
            part = self.part.at[c, h]
            p, q = place.axes(h)
            if step == 0:
                ref = part.at[q * SIDE + p]
                to = place.at(h, ring(p, hop), q)
            elif step == 1:
                ref = part.at[q * SIDE + ring(p, -hop), pl.ds(way * QUARTER, QUARTER)]
                to = place.at(h, ring(p, hop), q)
            elif step == 2:
                ref = part.at[pl.ds(q * SIDE, SIDE)]
                to = place.at(h, p, ring(q, hop))
            else:
                ref = part.at[pl.ds(ring(q, -hop) * SIDE + 2 * way, 2)]
                to = place.at(h, p, ring(q, hop))
            result.append(
                copy_to(
                    ref,
                    ref,
                    self.send.at[c, step, h, way],
                    self.recv.at[c, step, h, way],
                    to,
                )
            )
        return result


def greet_plane(place, barrier):
    for hop in (1, -1):
        for rank in (
            place.at(0, ring(place.x, hop), place.z),
            place.at(0, place.x, ring(place.z, hop)),
        ):
            pl.semaphore_signal(
                barrier, inc=1, device_id={"tensor": rank}, device_id_type=pl.DeviceIdType.MESH
            )


def project_kernel(
    att_ref, weight_ref, residual_ref, state_ref, part, r1, r2, r3, r4, near, send, recv, local
):
    place = Place()
    barrier = pltpu.get_barrier_semaphore()
    greet_plane(place, barrier)
    pl.semaphore_wait(barrier, 4)
    is_odd = lax.rem(place.rank, 2)
    first_column = pl.multiple_of((place.rank // 2) * 2 * SLICE, 2 * SLICE)
    fetch = pltpu.make_async_copy(
        residual_ref.at[:, pl.ds(first_column, 2 * SLICE)], near, local
    )
    fetch.start()
    summer = Summer(place, part, (r1, r2, r3, r4), send, recv)
    count = part.shape[0]
    for c in range(count):
        rows = att_ref[c * CHUNK : (c + 1) * CHUNK, :]

        @pl.loop(0, SIDE)
        def _(z):
            columns = pl.ds(pl.multiple_of(z * 4 * SLICE, 4 * SLICE), 4 * SLICE)
            block = jnp.dot(rows, weight_ref[:, columns], preferred_element_type=F32)
            store_quarter(part.at[c], z, block)

        summer.start(0, c)
    for step in range(1, 4):
        for c in range(count):
            summer.arrive(step - 1, c)
            summer.add(step - 1, c)
            summer.start(step, c)
    fetch.wait()
    for c in range(count):
        summer.arrive(3, c)
        rows = pl.ds(c * CHUNK, CHUNK)
        even = [near[rows, k * LANES : (k + 1) * LANES] for k in range(4)]
        odd = [near[rows, (k + 3) * LANES : (k + 4) * LANES] for k in range(4)]
        whole = jnp.concatenate(
            [
                jnp.where(is_odd == 1, odd[k + 1].astype(F32), even[k].astype(F32))
                for k in range(3)
            ]
            + [even[3].astype(F32)],
            axis=1,
        )
        store_own(state_ref.at[c], whole, is_odd)
        state_ref[c] = (state_ref[c].astype(F32) + summer.total(c)).astype(BF)
    for c in range(count):
        summer.sent(c)


def project(attention, out_weight, residual):
    count = attention.shape[0] // CHUNK
    return pl.pallas_call(
        project_kernel,
        out_shape=jax.ShapeDtypeStruct((count, SLICE, LANES), BF),
        in_specs=[
            pl.BlockSpec(memory_space=pltpu.VMEM),
            pl.BlockSpec(memory_space=pltpu.VMEM),
            pl.BlockSpec(memory_space=pl.ANY),
        ],
        out_specs=pl.BlockSpec(memory_space=pltpu.VMEM),
        scratch_shapes=[
            pltpu.VMEM((count, 2, 16, HALF, LANES), BF),
            pltpu.VMEM((count, 2, 2, 2, HALF, LANES), BF),
            pltpu.VMEM((count, 2, 2, SIDE, HALF, LANES), BF),
            pltpu.VMEM((count, 2, 2, QUARTER, LANES), BF),
            pltpu.VMEM((count, 2, 2, HALF, LANES), BF),
            pltpu.VMEM((attention.shape[0], 2 * SLICE), BF),
            pltpu.SemaphoreType.DMA((count, 4, 2, 2)),
            pltpu.SemaphoreType.DMA((count, 4, 2, 2)),
            pltpu.SemaphoreType.DMA,
        ],
        compiler_params=pltpu.CompilerParams(
            collective_id=1, has_side_effects=True, vmem_limit_bytes=48 * 1024 * 1024
        ),
        name="project",
    )(attention, out_weight, residual)


def flipped(group, bits):
    b = (lax.rem(group, 2), lax.rem(group // 2, 2), group // 4)
    return sum((b[k] + bits[k] - 2 * b[k] * bits[k]) * (1 << k) for k in range(3))


PARTNERS = (0, 1, 3, 7, 2, 6, 4, 5)
WHOLE = (1, 4, 5)
SPREAD = (2, 3, 6, 7)
TURNS = CHUNKS // 2
SLOTS = 6


def chunk_bits(c):
    if isinstance(c, int):
        return tuple((PARTNERS[c] >> k) & 1 for k in range(3))
    return tuple(
        sum(jnp.where(c == i, 1, 0) for i in range(CHUNKS) if (PARTNERS[i] >> k) & 1)
        for k in range(3)
    )


def to_group(src, dst, send, recv, group):
    return pltpu.make_async_remote_copy(
        src_ref=src,
        dst_ref=dst,
        send_sem=send,
        recv_sem=recv,
        device_id={"group": group},
        device_id_type=pl.DeviceIdType.MESH,
    )


def feed_kernel(
    ids_ref,
    route_ref,
    state_ref,
    expert_gate,
    expert_up,
    expert_down,
    dense_gate,
    dense_up,
    dense_down,
    mixed_ref,
    part,
    full,
    ready,
    r1,
    r2,
    r3,
    r4,
    w_in,
    w_down,
    outgoing,
    side_out,
    side_in,
    returned,
    summed,
    own_pos,
    acc,
    hidden,
    mixing,
    load_sem,
    full_send,
    full_recv,
    spread_send,
    spread_recv,
    sum_send,
    sum_recv,
    go_send,
    go_recv,
    side_send,
    side_recv,
    back_send,
    back_recv,
):
    place = Place()
    group = lax.axis_index("group")
    is_odd = lax.rem(place.rank, 2)
    hidden_size = w_in.shape[0] // 4
    rows = ids_ref.shape[1]
    row_blocks = rows // CHUNK
    width = 16 * SLICE

    loads = [
        pltpu.make_async_copy(
            ref, w_in.at[pl.ds(k * hidden_size, hidden_size)], load_sem.at[k]
        )
        for k, ref in enumerate((expert_gate.at[0], expert_up.at[0], dense_gate, dense_up))
    ] + [
        pltpu.make_async_copy(
            ref, w_down.at[pl.ds(k * hidden_size, hidden_size)], load_sem.at[4 + k]
        )
        for k, ref in enumerate((expert_down.at[0], dense_down))
    ]
    for load in loads:
        load.start()

    barrier = pltpu.get_barrier_semaphore()
    greet_plane(place, barrier)
    for c in range(1, CHUNKS):
        pl.semaphore_signal(
            barrier,
            inc=1,
            device_id={"group": flipped(group, chunk_bits(c))},
            device_id_type=pl.DeviceIdType.MESH,
        )
    for b in range(row_blocks):
        for h in range(2):
            full[b, h, spot(h, place.z, place.x)] = state_ref[b, h * HALF : (h + 1) * HALF, :]
    pl.semaphore_wait(barrier, 4 + CHUNKS - 1)

    gatherer = Spreader(place, full, full_send, full_recv)
    spreader = Spreader(place, part, spread_send, spread_recv)
    summer = Summer(place, part, (r1, r2, r3, r4), sum_send, sum_recv)
    for b in range(row_blocks):
        gatherer.start(0, b)

    line = lax.broadcasted_iota(jnp.int32, (rows, rows), 0)
    column = lax.broadcasted_iota(jnp.int32, (rows, rows), 1)

    def upright(row):
        return jnp.sum(jnp.where(line == column, row, 0.0), axis=1, keepdims=True)

    flat_ids = [ids_ref[k : k + 1, :].astype(F32) for k in range(2)]
    ids = [upright(row) for row in flat_ids]
    route = [upright(route_ref[k : k + 1, :]) for k in range(2)]
    partners = [flipped(group, chunk_bits(c)).astype(F32) for c in range(CHUNKS)]
    lane = lax.broadcasted_iota(jnp.int32, (rows, LANES), 1)
    partner_of_lane = jnp.full((rows, LANES), -1.0, F32)
    sub = lax.broadcasted_iota(jnp.int32, (CHUNKS, rows), 0)
    partner_of_sub = jnp.zeros((CHUNKS, rows), F32)
    for c in range(CHUNKS):
        partner_of_lane = jnp.where(lane == c, partners[c], partner_of_lane)
        partner_of_sub = jnp.where(sub == c, partners[c], partner_of_sub)
    first_choice, second_choice = [choice == partner_of_lane for choice in ids]
    named = jnp.where(first_choice | second_choice, 1.0, 0.0)
    before = jnp.where(column < line, 1.0, 0.0).astype(BF)
    place_in = jnp.dot(before, named.astype(BF), preferred_element_type=F32)
    positions = jnp.where(named > 0.5, place_in, -1.0)
    own_pos[...] = positions
    flat_named = jnp.where(
        (flat_ids[0] == partner_of_sub) | (flat_ids[1] == partner_of_sub), 1.0, 0.0
    )
    after = jnp.where(line < column, 1.0, 0.0).astype(BF)
    flat_place = jnp.dot(flat_named.astype(BF), after, preferred_element_type=F32)
    flat_pos = jnp.where(flat_named > 0.5, flat_place, -1.0)
    weight = jnp.where(first_choice, route[0], 0.0) + jnp.where(second_choice, route[1], 0.0)
    dense_here = jnp.where(first_choice, 1.0, 0.0)
    slot_line = lax.broadcasted_iota(jnp.int32, (CHUNK, rows), 0).astype(F32)
    slot_lane = lax.broadcasted_iota(jnp.int32, (rows, CHUNK), 1).astype(F32)
    sides = lax.broadcasted_iota(jnp.int32, (8, LANES), 0)
    for b in range(row_blocks):
        mixing[b * CHUNK : (b + 1) * CHUNK, :] = natural_own(state_ref.at[b], is_odd)

    def pick(c):
        return jnp.where(flat_pos[c : c + 1, :] == slot_line, 1.0, 0.0).astype(BF)

    def partner(c):
        return flipped(group, chunk_bits(c))

    def side(c):
        return to_group(
            side_out.at[c], side_in.at[c], side_send.at[c], side_recv.at[c], partner(c)
        )

    def slices(c):
        return [
            to_group(
                outgoing.at[SPREAD.index(c), pl.ds(h * HALF, HALF)],
                part.at[c, h, spot(h, place.z, place.x)],
                go_send.at[c, h],
                go_recv.at[c, h],
                partner(c),
            )
            for h in range(2)
        ]

    def whole(c):
        slot = 1 if c == 5 else 0
        return to_group(
            ready.at[slot], part.at[c], go_send.at[c, 0], go_recv.at[c, 0], partner(c)
        )

    for c in SPREAD:
        chosen = jnp.dot(pick(c), mixing[...].astype(BF), preferred_element_type=F32)
        store_own(outgoing.at[SPREAD.index(c)], chosen, is_odd)
        for copy in slices(c):
            copy.start()
    for b in range(row_blocks):
        gatherer.arrive(0, b)
        gatherer.start(1, b)
    for c in range(CHUNKS):
        at_slot = positions[:, c : c + 1] == slot_lane
        w_row = jnp.sum(jnp.where(at_slot, weight[:, c : c + 1], 0.0), axis=0, keepdims=True)
        d_row = jnp.sum(jnp.where(at_slot, dense_here[:, c : c + 1], 0.0), axis=0, keepdims=True)
        both = jnp.where(sides == 0, w_row, jnp.where(sides == 1, d_row, 0.0))
        if c == 0:
            side_in[0] = both
        else:
            side_out[c] = both
            side(c).start()
    for b in range(row_blocks):
        gatherer.arrive(1, b)
        gatherer.start(2, b)
    for c in SPREAD[:2]:
        for copy in slices(c):
            copy.wait_recv()
        spreader.start(0, c)
    for b in range(row_blocks):
        gatherer.arrive(2, b)
        gatherer.start(3, b)
    for c in SPREAD[:2]:
        spreader.arrive(0, c)
        spreader.start(1, c)
    for b in range(row_blocks):
        gatherer.arrive(3, b)

    def choose_whole(c, target):
        chosen_rows = pick(c)

        @pl.loop(0, SIDE)
        def _(z):
            source = jnp.concatenate(
                [load_quarter(full.at[b], z) for b in range(row_blocks)], axis=0
            )
            store_quarter(
                target, z, jnp.dot(chosen_rows, source, preferred_element_type=F32)
            )

    choose_whole(1, ready.at[0])
    whole(1).start()
    choose_whole(5, ready.at[1])
    whole(5).start()
    whole(1).wait_send()
    choose_whole(4, ready.at[0])
    whole(4).start()
    choose_whole(0, part.at[0])

    def back(c):
        return to_group(
            summed.at[c], returned.at[c], back_send.at[c], back_recv.at[c], partner(c)
        )

    def finish_sum(c):
        summer.arrive(3, c)
        total = summer.total(c).astype(BF)

        @pl.when(c == 0)
        def _():
            returned[0] = total

        @pl.when(c > 0)
        def _():
            summed[c] = total
            back(c).start()

    def mix(c):
        @pl.when(c > 0)
        def _():
            back(c).wait_recv()

        position = jnp.sum(jnp.where(lane == c, own_pos[...], 0.0), axis=1, keepdims=True)
        at_slot = jnp.where(position == slot_lane, 1.0, 0.0).astype(BF)
        block = natural_own(returned.at[c], is_odd).astype(BF)
        mixing[...] += jnp.dot(at_slot, block, preferred_element_type=F32)

    def compute(j):
        chunks = [part.at[2 * j + i] for i in range(2)]
        acc[...] = jnp.zeros_like(acc)

        def gather_products(z, squares):
            block = jnp.concatenate([load_quarter(chunk, z) for chunk in chunks], axis=0)
            deep = pl.ds(pl.multiple_of(z * 4 * SLICE, 4 * SLICE), 4 * SLICE)
            acc[...] += lax.dot_general(
                block, w_in[:, deep], (((1,), (1,)), ((), ())), preferred_element_type=F32
            )
            for k in range(14):
                wide = block[:, k * LANES : (k + 1) * LANES].astype(F32)
                squares = squares + wide * wide
            return squares

        squares = lax.fori_loop(0, SIDE, gather_products, jnp.zeros((2 * CHUNK, LANES), F32))
        scale = lax.rsqrt(jnp.sum(squares, axis=1, keepdims=True) / width + 1e-05)
        diagonal = lax.broadcasted_iota(jnp.int32, (CHUNK, CHUNK), 0) == lax.broadcasted_iota(
            jnp.int32, (CHUNK, CHUNK), 1
        )
        for k in range(2):
            factor = jnp.concatenate(
                [
                    jnp.sum(
                        jnp.where(diagonal, side_in[2 * j + i, k : k + 1, :], 0.0),
                        axis=1,
                        keepdims=True,
                    )
                    for i in range(2)
                ],
                axis=0,
            )
            gate, up = [
                acc[:, (2 * k + i) * hidden_size : (2 * k + i + 1) * hidden_size] * scale
                for i in range(2)
            ]
            inner = gate / (1.0 + jnp.exp(-gate)) * up * factor
            hidden[:, k * hidden_size : (k + 1) * hidden_size] = inner.astype(BF)

        @pl.when(lax.rem(j, 2) == 1)
        def _():
            for i in range(2):
                spreader.sent(2 * j + i)

        @pl.loop(0, SIDE)
        def _(z):
            columns = pl.ds(pl.multiple_of(z * 4 * SLICE, 4 * SLICE), 4 * SLICE)
            block = jnp.dot(hidden[...], w_down[:, columns], preferred_element_type=F32)
            for i in range(2):
                store_quarter(chunks[i], z, block[i * CHUNK : (i + 1) * CHUNK])

    def turn(it, carry):
        def stage(lag, body):
            j = it - lag

            @pl.when((j >= 0) & (j < TURNS))
            def _():
                for i in range(2):
                    body(2 * j + i)

        def add(step):
            def body(c):
                summer.arrive(step - 1, c)
                summer.add(step - 1, c)
                summer.start(step, c)

            return body

        def spread(step, chunks):
            for c in chunks:
                if step == 0:
                    for copy in slices(c):
                        copy.wait_recv()
                else:
                    spreader.arrive(step - 1, c)
                if step < 4:
                    spreader.start(step, c)

        stage(5, mix)
        stage(4, finish_sum)
        stage(3, add(3))
        stage(2, add(2))
        stage(1, add(1))

        @pl.when(it == 0)
        def _():
            spread(2, SPREAD[:2])
            spread(0, SPREAD[2:])
            whole(1).wait_recv()
            side(1).wait_recv()
            for load in loads:
                load.wait()

        @pl.when(it == 1)
        def _():
            spread(2, SPREAD[2:])
            spread(4, SPREAD[:2])
            for c in SPREAD[:2]:
                side(c).wait_recv()

        @pl.when(it == 2)
        def _():
            spread(3, SPREAD[2:])
            for c in WHOLE[1:]:
                whole(c).wait_recv()
                side(c).wait_recv()

        @pl.when(it == 3)
        def _():
            spread(4, SPREAD[2:])
            for c in SPREAD[2:]:
                side(c).wait_recv()

        @pl.when(it < TURNS)
        def _():
            compute(it)
            for i in range(2):
                summer.start(0, 2 * it + i)

        @pl.when(it == 0)
        def _():
            spread(3, SPREAD[:2])
            spread(1, SPREAD[2:])

        return carry

    lax.fori_loop(0, TURNS + 5, turn, 0)

    total = mixing[...]
    for_odd = pltpu.roll(
        jnp.concatenate([total[:, 3 * LANES :], total[:, : 3 * LANES]], axis=1),
        4 * LANES - SHARED,
        1,
    )
    mixed_ref[...] = jnp.where(is_odd == 1, for_odd, total)[:, :SLICE].astype(BF)

    @pl.loop(0, CHUNKS)
    def _(c):
        summer.sent(c)

    for b in range(row_blocks):
        gatherer.sent(b)
    for c in range(1, CHUNKS):
        side(c).wait_send()
        back(c).wait_send()
    for c in SPREAD:
        for copy in slices(c):
            copy.wait_send()
    for c in WHOLE[1:]:
        whole(c).wait_send()


def feed(
    expert_ids,
    route_weights,
    state,
    expert_gate,
    expert_up,
    expert_down,
    dense_gate,
    dense_up,
    dense_down,
):
    rows = expert_ids.shape[0]
    width, hidden_size = dense_gate.shape
    vmem = pl.BlockSpec(memory_space=pltpu.VMEM)
    hbm = pl.BlockSpec(memory_space=pl.ANY)
    row_blocks = rows // CHUNK
    return pl.pallas_call(
        feed_kernel,
        out_shape=jax.ShapeDtypeStruct((rows, SLICE), BF),
        in_specs=[vmem] * 3 + [hbm] * 6,
        out_specs=vmem,
        scratch_shapes=[
            pltpu.VMEM((CHUNKS, 2, 16, HALF, LANES), BF),
            pltpu.VMEM((row_blocks, 2, 16, HALF, LANES), BF),
            pltpu.VMEM((2, 2, 16, HALF, LANES), BF),
            pltpu.VMEM((SLOTS, 2, 2, 2, HALF, LANES), BF),
            pltpu.VMEM((SLOTS, 2, 2, SIDE, HALF, LANES), BF),
            pltpu.VMEM((SLOTS, 2, 2, QUARTER, LANES), BF),
            pltpu.VMEM((SLOTS, 2, 2, HALF, LANES), BF),
            pltpu.VMEM((4 * hidden_size, width), BF),
            pltpu.VMEM((2 * hidden_size, width), BF),
            pltpu.VMEM((len(SPREAD), SLICE, LANES), BF),
            pltpu.VMEM((CHUNKS, 8, LANES), F32),
            pltpu.VMEM((CHUNKS, 8, LANES), F32),
            pltpu.VMEM((CHUNKS, SLICE, LANES), BF),
            pltpu.VMEM((CHUNKS, SLICE, LANES), BF),
            pltpu.VMEM((rows, LANES), F32),
            pltpu.VMEM((2 * CHUNK, 4 * hidden_size), F32),
            pltpu.VMEM((2 * CHUNK, 2 * hidden_size), BF),
            pltpu.VMEM((rows, 4 * LANES), F32),
            pltpu.SemaphoreType.DMA((6,)),
        ]
        + [pltpu.SemaphoreType.DMA((row_blocks, 4, 2, 2))] * 2
        + [pltpu.SemaphoreType.DMA((CHUNKS, 4, 2, 2))] * 4
        + [pltpu.SemaphoreType.DMA((CHUNKS, 2))] * 2
        + [pltpu.SemaphoreType.DMA((CHUNKS,))] * 4,
        compiler_params=pltpu.CompilerParams(
            collective_id=2, has_side_effects=True, vmem_limit_bytes=64 * 1024 * 1024 - 65536
        ),
        name="feed",
    )(
        expert_ids.T,
        route_weights.T,
        state,
        jnp.swapaxes(expert_gate, 1, 2),
        jnp.swapaxes(expert_up, 1, 2),
        expert_down,
        dense_gate.T,
        dense_up.T,
        dense_down,
    )


def from_partner(block):
    return lax.ppermute(block, "tensor", [(i, i ^ 1) for i in range(lax.axis_size("tensor"))])


def attend(queries, new_kv, kv_cache, lengths):
    row_count = queries.shape[0]
    rank = lax.axis_index("tensor")
    my_head, my_part = rank // 2, rank % 2
    head_size = new_kv.shape[3]
    span = kv_cache.shape[2]
    rows = lax.dynamic_index_in_dim(queries, my_head, 1, keepdims=False).reshape(
        row_count, -1, head_size
    )
    new_key = lax.dynamic_index_in_dim(new_kv[0], my_head, 1, keepdims=False)
    new_value = lax.dynamic_index_in_dim(new_kv[1], my_head, 1, keepdims=False)
    scale = 1.0 / math.sqrt(head_size)
    scores = jnp.einsum("tgd,tpd->tgp", rows, kv_cache[0], preferred_element_type=F32) * scale
    own = jnp.einsum("tgd,td->tg", rows, new_key, preferred_element_type=F32) * scale
    position = my_part * span + jnp.arange(span, dtype=jnp.int32)
    usable = position[None, None, :] < lengths[:, None, None]
    masked = jnp.where(usable, scores, -1e30)
    highest = jnp.maximum(jnp.max(masked, axis=-1), own)
    weights = jnp.where(usable, jnp.exp(masked - highest[..., None]), 0.0).astype(BF)
    own_weight = jnp.exp(own - highest)
    leading = (my_part == 0).astype(F32)
    numerator = jnp.einsum("tgp,tpd->tgd", weights, kv_cache[1], preferred_element_type=F32)
    numerator = numerator + leading * own_weight[..., None] * new_value.astype(F32)[:, None, :]
    denominator = jnp.sum(weights.astype(F32), axis=-1) + leading * own_weight
    width = rows.shape[1] * head_size
    flat = numerator.reshape(row_count, width)
    mine = lax.dynamic_slice_in_dim(flat, my_part * (width // 2), width // 2, 1)
    theirs = lax.dynamic_slice_in_dim(flat, (1 - my_part) * (width // 2), width // 2, 1)
    other, other_marks = from_partner((theirs.astype(BF), jnp.stack([highest, denominator])))
    other_highest, other_denominator = other_marks[0], other_marks[1]
    top = jnp.maximum(highest, other_highest)
    keep, take = jnp.exp(highest - top), jnp.exp(other_highest - top)
    below = 1.0 / (denominator * keep + other_denominator * take)
    keep = jnp.repeat(keep * below, head_size, axis=1)
    take = jnp.repeat(take * below, head_size, axis=1)
    keep = lax.dynamic_slice_in_dim(keep, my_part * (width // 2), width // 2, 1)
    take = lax.dynamic_slice_in_dim(take, my_part * (width // 2), width // 2, 1)
    return (mine * keep + other.astype(F32) * take).astype(BF)


def shards(
    residual,
    queries,
    new_kv,
    kv_cache,
    lengths,
    out_weight,
    dense_gate,
    dense_up,
    dense_down,
    expert_ids,
    route_weights,
    expert_gate,
    expert_up,
    expert_down,
):
    attention = attend(queries, new_kv, kv_cache, lengths)
    state = project(attention, out_weight, residual)
    return feed(
        expert_ids,
        route_weights,
        state,
        expert_gate,
        expert_up,
        expert_down,
        dense_gate,
        dense_up,
        dense_down,
    )


def solution(mesh):
    placed = (
        P("group", None),
        P("group", None, None),
        P(None, "group", None, None),
        P(None, "group", "tensor", None),
        P("group"),
        P("tensor", None),
        P(None, "tensor"),
        P(None, "tensor"),
        P("tensor", None),
        P("group", None),
        P("group", None),
        P("group", None, "tensor"),
        P("group", None, "tensor"),
        P("group", "tensor", None),
    )
    return jax.shard_map(
        shards, mesh=mesh, in_specs=placed, out_specs=P("group", "tensor"), check_vma=False
    )
```

```python
import functools
import math

import jax
import jax.numpy as jnp
from jax import lax
from jax.experimental import pallas as pl
from jax.experimental.pallas import tpu as pltpu
from jax.sharding import PartitionSpec as P

BF = jnp.bfloat16
F32 = jnp.float32
SIDE = 4
LANES = 128
CHUNK = 128
SLICE = 448
HALF = SLICE // 2
SHARED = 64
CHUNKS = 8


def ring(value, step):
    return lax.rem(value + step + SIDE, SIDE)


class Place:
    def __init__(self):
        rank = lax.axis_index("tensor")
        self.rank = rank
        self.z = rank // SIDE
        self.x = lax.rem(rank, SIDE)

    def axes(self, half):
        return (self.x, self.z) if half == 0 else (self.z, self.x)

    def at(self, half, p, q):
        return q * SIDE + p if half == 0 else p * SIDE + q


def spot(half, z, x):
    return z * SIDE + x if half == 0 else x * SIDE + z


def split_rows(low, high):
    pieces = []
    if low < HALF:
        pieces.append((0, low, min(high, HALF), 0))
    if high > HALF:
        start = max(low, HALF)
        pieces.append((1, start - HALF, high - HALF, start - low))
    return pieces


def read_rows(part, z, x, low, high):
    pieces = [part[h, spot(h, z, x), a:b, :] for h, a, b, _ in split_rows(low, high)]
    return pieces[0] if len(pieces) == 1 else jnp.concatenate(pieces, axis=0)


def write_rows(part, z, x, low, value, halves=(0, 1)):
    for h, a, b, offset in split_rows(low, low + value.shape[0]):
        if h in halves:
            part[h, spot(h, z, x), a:b, :] = value[offset : offset + b - a]


def copy_to(src, dst, send, recv, rank):
    return pltpu.make_async_remote_copy(
        src_ref=src,
        dst_ref=dst,
        send_sem=send,
        recv_sem=recv,
        device_id={"tensor": rank},
        device_id_type=pl.DeviceIdType.MESH,
    )


def lanes_low(rows):
    return lax.broadcasted_iota(jnp.int32, (rows, LANES), 1) < SHARED


def turned(block):
    return pltpu.roll(block, SHARED, 1)


def unfold_pair(even_half, odd_half):
    low = lanes_low(SHARED)
    e, o = even_half.astype(F32), odd_half.astype(F32)
    top = jnp.where(low, e, o)
    bottom = turned(jnp.where(low, o, e))
    return jnp.concatenate([top, bottom], axis=0).astype(BF)


def fold_pair(tile):
    low = lanes_low(SHARED)
    top, bottom = tile[:SHARED], turned(tile[SHARED:])
    return jnp.where(low, top, bottom).astype(BF), jnp.where(low, bottom, top).astype(BF)


def unfold_own(half):
    half = half.astype(F32)
    return jnp.concatenate([half, turned(half)], axis=0)


def fold_own(tile, is_odd):
    low = lanes_low(SHARED).astype(jnp.int32) != is_odd
    top, bottom = tile[:SHARED], turned(tile[SHARED:])
    return jnp.where(low, top, bottom)


def natural_own(ref, is_odd):
    first = pl.multiple_of(is_odd * SHARED, SHARED)
    half = pl.multiple_of((1 - is_odd) * (SLICE - SHARED), SHARED)
    tiles = [ref[pl.ds(first + k * LANES, LANES), :].astype(F32) for k in range(3)]
    return jnp.concatenate(tiles + [unfold_own(ref[pl.ds(half, SHARED), :])], axis=1)


def store_own(ref, block, is_odd):
    first = pl.multiple_of(is_odd * SHARED, SHARED)
    half = pl.multiple_of((1 - is_odd) * (SLICE - SHARED), SHARED)
    for k in range(3):
        ref[pl.ds(first + k * LANES, LANES), :] = block[:, k * LANES : (k + 1) * LANES].astype(BF)
    ref[pl.ds(half, SHARED), :] = fold_own(block[:, 3 * LANES :], is_odd).astype(BF)


def store_quarter(part, z, block, halves=(0, 1)):
    for pair in range(2):
        e, o = 2 * pair, 2 * pair + 1
        tiles = [
            block[:, (pair * 7 + k) * LANES : (pair * 7 + k + 1) * LANES] for k in range(7)
        ]
        even_half, odd_half = fold_pair(tiles[3])
        for k in range(3):
            write_rows(part, z, e, k * LANES, tiles[k].astype(BF), halves)
            write_rows(part, z, o, SHARED + k * LANES, tiles[4 + k].astype(BF), halves)
        write_rows(part, z, e, SLICE - SHARED, even_half, halves)
        write_rows(part, z, o, 0, odd_half, halves)


def load_quarter(part, z):
    blocks = []
    for pair in range(2):
        e, o = 2 * pair, 2 * pair + 1
        blocks += [read_rows(part, z, e, k * LANES, (k + 1) * LANES) for k in range(3)]
        blocks.append(
            unfold_pair(
                read_rows(part, z, e, SLICE - SHARED, SLICE), read_rows(part, z, o, 0, SHARED)
            )
        )
        blocks += [
            read_rows(part, z, o, SHARED + k * LANES, SHARED + (k + 1) * LANES) for k in range(3)
        ]
    return jnp.concatenate(blocks, axis=1)


def add_into(dst, other):
    dst[...] = (dst[...].astype(F32) + other[...].astype(F32)).astype(BF)


class Exchange:
    def start(self, step, c):
        for copy in self.copies(step, c):
            copy.start()

    def arrive(self, step, c):
        for copy in self.copies(step, c):
            copy.wait_recv()

    def sent(self, c):
        for step in range(4):
            for copy in self.copies(step, c):
                copy.wait_send()


WAYS = ((0, 0, 1), (0, 1, -1), (1, 0, 1), (1, 1, -1))
QUARTER = HALF // 2


class Summer(Exchange):
    def __init__(self, place, part, landing, send, recv):
        self.place, self.part, self.landing = place, part, landing
        self.send, self.recv = send, recv

    def landed(self, step, c):
        landing = self.landing[step]
        return landing.at[lax.rem(c, landing.shape[0])]

    def copies(self, step, c):
        place = self.place
        result = []
        for h, way, hop in WAYS:
            part = self.part.at[c, h]
            p, q = place.axes(h)
            if step == 0:
                src = part.at[pl.ds(ring(q, 2) * SIDE + 2 * way, 2)]
                to = place.at(h, p, ring(q, hop))
            elif step == 1:
                src = part.at[pl.ds(ring(q, hop) * SIDE, SIDE)]
                to = place.at(h, p, ring(q, hop))
            elif step == 2:
                src = part.at[q * SIDE + ring(p, 2), pl.ds(way * QUARTER, QUARTER)]
                to = place.at(h, ring(p, hop), q)
            else:
                src = part.at[q * SIDE + ring(p, hop)]
                to = place.at(h, ring(p, hop), q)
            result.append(
                copy_to(
                    src,
                    self.landed(step, c).at[h, way],
                    self.send.at[c, step, h, way],
                    self.recv.at[c, step, h, way],
                    to,
                )
            )
        return result

    def add(self, step, c):
        for h in range(2):
            part = self.part.at[c, h]
            p, q = self.place.axes(h)
            landed = self.landed(step, c).at[h]
            if step == 0:
                for way, hop in ((0, 1), (1, -1)):
                    for k in range(2):
                        add_into(part.at[ring(q, hop) * SIDE + 2 * way + k], landed.at[way, k])
            elif step == 1:
                for k in range(SIDE):
                    dst = part.at[q * SIDE + k]
                    dst[...] = (
                        dst[...].astype(F32) + landed[0, k].astype(F32) + landed[1, k].astype(F32)
                    ).astype(BF)
            elif step == 2:
                for way, hop in ((0, 1), (1, -1)):
                    add_into(
                        part.at[q * SIDE + ring(p, hop), pl.ds(way * QUARTER, QUARTER)],
                        landed.at[way],
                    )

    def total(self, c):
        halves = []
        for h in range(2):
            p, q = self.place.axes(h)
            landed = self.landed(3, c).at[h]
            halves.append(
                self.part[c, h, q * SIDE + p].astype(F32)
                + landed[0].astype(F32)
                + landed[1].astype(F32)
            )
        return jnp.concatenate(halves, axis=0)


class Spreader(Exchange):
    def __init__(self, place, part, send, recv, halves=None):
        self.place, self.part, self.send, self.recv = place, part, send, recv
        self.halves = halves or {}

    def copies(self, step, c):
        place = self.place
        result = []
        for h, way, hop in WAYS:
            if h not in self.halves.get(c, (0, 1)):
                continue
            part = self.part.at[c, h]
            p, q = place.axes(h)
            if step == 0:
                ref = part.at[q * SIDE + p]
                to = place.at(h, ring(p, hop), q)
            elif step == 1:
                ref = part.at[q * SIDE + ring(p, -hop), pl.ds(way * QUARTER, QUARTER)]
                to = place.at(h, ring(p, hop), q)
            elif step == 2:
                ref = part.at[pl.ds(q * SIDE, SIDE)]
                to = place.at(h, p, ring(q, hop))
            else:
                ref = part.at[pl.ds(ring(q, -hop) * SIDE + 2 * way, 2)]
                to = place.at(h, p, ring(q, hop))
            result.append(
                copy_to(
                    ref,
                    ref,
                    self.send.at[c, step, h, way],
                    self.recv.at[c, step, h, way],
                    to,
                )
            )
        return result


def greet_plane(place, barrier):
    for hop in (1, -1):
        for rank in (
            place.at(0, ring(place.x, hop), place.z),
            place.at(0, place.x, ring(place.z, hop)),
        ):
            pl.semaphore_signal(
                barrier, inc=1, device_id={"tensor": rank}, device_id_type=pl.DeviceIdType.MESH
            )


def project_kernel(
    att_ref, weight_ref, residual_ref, state_ref, part, r1, r2, r3, r4, near, send, recv, local
):
    place = Place()
    barrier = pltpu.get_barrier_semaphore()
    greet_plane(place, barrier)
    pl.semaphore_wait(barrier, 4)
    is_odd = lax.rem(place.rank, 2)
    first_column = pl.multiple_of((place.rank // 2) * 2 * SLICE, 2 * SLICE)
    fetch = pltpu.make_async_copy(
        residual_ref.at[:, pl.ds(first_column, 2 * SLICE)], near, local
    )
    fetch.start()
    summer = Summer(place, part, (r1, r2, r3, r4), send, recv)
    count = part.shape[0]
    for c in range(count):
        rows = att_ref[c * CHUNK : (c + 1) * CHUNK, :]

        @pl.loop(0, SIDE)
        def _(z):
            columns = pl.ds(pl.multiple_of(z * 4 * SLICE, 4 * SLICE), 4 * SLICE)
            block = jnp.dot(rows, weight_ref[:, columns], preferred_element_type=F32)
            store_quarter(part.at[c], z, block)

        summer.start(0, c)
    for step in range(1, 4):
        for c in range(count):
            summer.arrive(step - 1, c)
            summer.add(step - 1, c)
            summer.start(step, c)
    fetch.wait()
    for c in range(count):
        summer.arrive(3, c)
        rows = pl.ds(c * CHUNK, CHUNK)
        even = [near[rows, k * LANES : (k + 1) * LANES] for k in range(4)]
        odd = [near[rows, (k + 3) * LANES : (k + 4) * LANES] for k in range(4)]
        whole = jnp.concatenate(
            [
                jnp.where(is_odd == 1, odd[k + 1].astype(F32), even[k].astype(F32))
                for k in range(3)
            ]
            + [even[3].astype(F32)],
            axis=1,
        )
        store_own(state_ref.at[c], whole, is_odd)
        state_ref[c] = (state_ref[c].astype(F32) + summer.total(c)).astype(BF)
    for c in range(count):
        summer.sent(c)


def project(attention, out_weight, residual):
    count = attention.shape[0] // CHUNK
    return pl.pallas_call(
        project_kernel,
        out_shape=jax.ShapeDtypeStruct((count, SLICE, LANES), BF),
        in_specs=[
            pl.BlockSpec(memory_space=pltpu.VMEM),
            pl.BlockSpec(memory_space=pltpu.VMEM),
            pl.BlockSpec(memory_space=pl.ANY),
        ],
        out_specs=pl.BlockSpec(memory_space=pltpu.VMEM),
        scratch_shapes=[
            pltpu.VMEM((count, 2, 16, HALF, LANES), BF),
            pltpu.VMEM((count, 2, 2, 2, HALF, LANES), BF),
            pltpu.VMEM((count, 2, 2, SIDE, HALF, LANES), BF),
            pltpu.VMEM((count, 2, 2, QUARTER, LANES), BF),
            pltpu.VMEM((count, 2, 2, HALF, LANES), BF),
            pltpu.VMEM((attention.shape[0], 2 * SLICE), BF),
            pltpu.SemaphoreType.DMA((count, 4, 2, 2)),
            pltpu.SemaphoreType.DMA((count, 4, 2, 2)),
            pltpu.SemaphoreType.DMA,
        ],
        compiler_params=pltpu.CompilerParams(
            collective_id=1, has_side_effects=True, vmem_limit_bytes=48 * 1024 * 1024
        ),
        name="project",
    )(attention, out_weight, residual)


def flipped(group, bits):
    b = (lax.rem(group, 2), lax.rem(group // 2, 2), group // 4)
    return sum((b[k] + bits[k] - 2 * b[k] * bits[k]) * (1 << k) for k in range(3))


PARTNERS = (0, 1, 4, 5, 2, 6, 3, 7)
WHOLE = (1, 4, 5)
SPREAD = (2, 3, 6, 7)
SPREAD_HALVES = {2: (0, 1), 3: (0, 1), 6: (1,), 7: (0,)}
TURNS = CHUNKS // 2
SLOTS = 6


def chunk_bits(c):
    if isinstance(c, int):
        return tuple((PARTNERS[c] >> k) & 1 for k in range(3))
    return tuple(
        sum(jnp.where(c == i, 1, 0) for i in range(CHUNKS) if (PARTNERS[i] >> k) & 1)
        for k in range(3)
    )


def to_group(src, dst, send, recv, group):
    return pltpu.make_async_remote_copy(
        src_ref=src,
        dst_ref=dst,
        send_sem=send,
        recv_sem=recv,
        device_id={"group": group},
        device_id_type=pl.DeviceIdType.MESH,
    )


def feed_kernel(
    ids_ref,
    route_ref,
    state_ref,
    expert_gate,
    expert_up,
    expert_down,
    dense_gate,
    dense_up,
    dense_down,
    mixed_ref,
    part,
    full,
    ready,
    r1,
    r2,
    r3,
    r4,
    w_in,
    w_down,
    outgoing,
    side_out,
    side_in,
    returned,
    summed,
    own_pos,
    acc,
    hidden,
    mixing,
    load_sem,
    full_send,
    full_recv,
    spread_send,
    spread_recv,
    sum_send,
    sum_recv,
    go_send,
    go_recv,
    side_send,
    side_recv,
    back_send,
    back_recv,
):
    place = Place()
    group = lax.axis_index("group")
    is_odd = lax.rem(place.rank, 2)
    hidden_size = w_in.shape[0] // 4
    rows = ids_ref.shape[1]
    row_blocks = rows // CHUNK
    width = 16 * SLICE

    loads = [
        pltpu.make_async_copy(
            ref, w_in.at[pl.ds(k * hidden_size, hidden_size)], load_sem.at[k]
        )
        for k, ref in enumerate((expert_gate.at[0], expert_up.at[0], dense_gate, dense_up))
    ] + [
        pltpu.make_async_copy(
            ref, w_down.at[pl.ds(k * hidden_size, hidden_size)], load_sem.at[4 + k]
        )
        for k, ref in enumerate((expert_down.at[0], dense_down))
    ]
    for load in loads:
        load.start()

    barrier = pltpu.get_barrier_semaphore()
    greet_plane(place, barrier)
    for c in range(1, CHUNKS):
        pl.semaphore_signal(
            barrier,
            inc=1,
            device_id={"group": flipped(group, chunk_bits(c))},
            device_id_type=pl.DeviceIdType.MESH,
        )
    for b in range(row_blocks):
        for h in range(2):
            full[b, h, spot(h, place.z, place.x)] = state_ref[b, h * HALF : (h + 1) * HALF, :]
    pl.semaphore_wait(barrier, 4 + CHUNKS - 1)

    gatherer = Spreader(place, full, full_send, full_recv)
    spreader = Spreader(place, part, spread_send, spread_recv, SPREAD_HALVES)
    summer = Summer(place, part, (r1, r2, r3, r4), sum_send, sum_recv)
    for b in range(row_blocks):
        gatherer.start(0, b)

    line = lax.broadcasted_iota(jnp.int32, (rows, rows), 0)
    column = lax.broadcasted_iota(jnp.int32, (rows, rows), 1)

    def upright(row):
        return jnp.sum(jnp.where(line == column, row, 0.0), axis=1, keepdims=True)

    flat_ids = [ids_ref[k : k + 1, :].astype(F32) for k in range(2)]
    ids = [upright(row) for row in flat_ids]
    route = [upright(route_ref[k : k + 1, :]) for k in range(2)]
    partners = [flipped(group, chunk_bits(c)).astype(F32) for c in range(CHUNKS)]
    lane = lax.broadcasted_iota(jnp.int32, (rows, LANES), 1)
    partner_of_lane = jnp.full((rows, LANES), -1.0, F32)
    sub = lax.broadcasted_iota(jnp.int32, (CHUNKS, rows), 0)
    partner_of_sub = jnp.zeros((CHUNKS, rows), F32)
    for c in range(CHUNKS):
        partner_of_lane = jnp.where(lane == c, partners[c], partner_of_lane)
        partner_of_sub = jnp.where(sub == c, partners[c], partner_of_sub)
    first_choice, second_choice = [choice == partner_of_lane for choice in ids]
    named = jnp.where(first_choice | second_choice, 1.0, 0.0)
    before = jnp.where(column < line, 1.0, 0.0).astype(BF)
    place_in = jnp.dot(before, named.astype(BF), preferred_element_type=F32)
    positions = jnp.where(named > 0.5, place_in, -1.0)
    own_pos[...] = positions
    flat_named = jnp.where(
        (flat_ids[0] == partner_of_sub) | (flat_ids[1] == partner_of_sub), 1.0, 0.0
    )
    after = jnp.where(line < column, 1.0, 0.0).astype(BF)
    flat_place = jnp.dot(flat_named.astype(BF), after, preferred_element_type=F32)
    flat_pos = jnp.where(flat_named > 0.5, flat_place, -1.0)
    weight = jnp.where(first_choice, route[0], 0.0) + jnp.where(second_choice, route[1], 0.0)
    dense_here = jnp.where(first_choice, 1.0, 0.0)
    slot_line = lax.broadcasted_iota(jnp.int32, (CHUNK, rows), 0).astype(F32)
    slot_lane = lax.broadcasted_iota(jnp.int32, (rows, CHUNK), 1).astype(F32)
    sides = lax.broadcasted_iota(jnp.int32, (8, LANES), 0)
    for b in range(row_blocks):
        mixing[b * CHUNK : (b + 1) * CHUNK, :] = natural_own(state_ref.at[b], is_odd)

    def pick(c):
        return jnp.where(flat_pos[c : c + 1, :] == slot_line, 1.0, 0.0).astype(BF)

    def partner(c):
        return flipped(group, chunk_bits(c))

    def side(c):
        return to_group(
            side_out.at[c], side_in.at[c], side_send.at[c], side_recv.at[c], partner(c)
        )

    def slices(c):
        return [
            to_group(
                outgoing.at[SPREAD.index(c), pl.ds(h * HALF, HALF)],
                part.at[c, h, spot(h, place.z, place.x)],
                go_send.at[c, h],
                go_recv.at[c, h],
                partner(c),
            )
            for h in SPREAD_HALVES[c]
        ]

    def whole(c):
        slot = 1 if c == 5 else 0
        return to_group(
            ready.at[slot], part.at[c], go_send.at[c, 0], go_recv.at[c, 0], partner(c)
        )

    def other_half(c):
        h = 1 - SPREAD_HALVES[c][0]
        return to_group(
            ready.at[c - 6, h], part.at[c, h], go_send.at[c, h], go_recv.at[c, h], partner(c)
        )

    for c in SPREAD:
        chosen = jnp.dot(pick(c), mixing[...].astype(BF), preferred_element_type=F32)
        store_own(outgoing.at[SPREAD.index(c)], chosen, is_odd)
        for copy in slices(c):
            copy.start()
    for b in range(row_blocks):
        gatherer.arrive(0, b)
        gatherer.start(1, b)
    for c in range(CHUNKS):
        at_slot = positions[:, c : c + 1] == slot_lane
        w_row = jnp.sum(jnp.where(at_slot, weight[:, c : c + 1], 0.0), axis=0, keepdims=True)
        d_row = jnp.sum(jnp.where(at_slot, dense_here[:, c : c + 1], 0.0), axis=0, keepdims=True)
        both = jnp.where(sides == 0, w_row, jnp.where(sides == 1, d_row, 0.0))
        if c == 0:
            side_in[0] = both
        else:
            side_out[c] = both
            side(c).start()
    for b in range(row_blocks):
        gatherer.arrive(1, b)
        gatherer.start(2, b)
    for c in SPREAD[:2]:
        for copy in slices(c):
            copy.wait_recv()
        spreader.start(0, c)
    for b in range(row_blocks):
        gatherer.arrive(2, b)
        gatherer.start(3, b)
    for c in SPREAD[:2]:
        spreader.arrive(0, c)
        spreader.start(1, c)
    for c in SPREAD[:2]:
        spreader.arrive(1, c)
        spreader.start(2, c)
    for b in range(row_blocks):
        gatherer.arrive(3, b)

    def choose_whole(c, target, halves=(0, 1)):
        chosen_rows = pick(c)

        @pl.loop(0, SIDE)
        def _(z):
            source = jnp.concatenate(
                [load_quarter(full.at[b], z) for b in range(row_blocks)], axis=0
            )
            store_quarter(
                target, z, jnp.dot(chosen_rows, source, preferred_element_type=F32), halves
            )

    choose_whole(1, ready.at[0])
    whole(1).start()
    choose_whole(5, ready.at[1])
    whole(5).start()
    whole(1).wait_send()
    choose_whole(4, ready.at[0])
    whole(4).start()
    choose_whole(0, part.at[0])

    def back(c):
        return to_group(
            summed.at[c], returned.at[c], back_send.at[c], back_recv.at[c], partner(c)
        )

    def finish_sum(c):
        summer.arrive(3, c)
        total = summer.total(c).astype(BF)

        @pl.when(c == 0)
        def _():
            returned[0] = total

        @pl.when(c > 0)
        def _():
            summed[c] = total
            back(c).start()

    def mix(c):
        @pl.when(c > 0)
        def _():
            back(c).wait_recv()

        position = jnp.sum(jnp.where(lane == c, own_pos[...], 0.0), axis=1, keepdims=True)
        at_slot = jnp.where(position == slot_lane, 1.0, 0.0).astype(BF)
        block = natural_own(returned.at[c], is_odd).astype(BF)
        mixing[...] += jnp.dot(at_slot, block, preferred_element_type=F32)

    def compute(j):
        chunks = [part.at[2 * j + i] for i in range(2)]
        acc[...] = jnp.zeros_like(acc)

        def gather_products(z, squares):
            block = jnp.concatenate([load_quarter(chunk, z) for chunk in chunks], axis=0)
            deep = pl.ds(pl.multiple_of(z * 4 * SLICE, 4 * SLICE), 4 * SLICE)
            acc[...] += lax.dot_general(
                block, w_in[:, deep], (((1,), (1,)), ((), ())), preferred_element_type=F32
            )
            for k in range(14):
                wide = block[:, k * LANES : (k + 1) * LANES].astype(F32)
                squares = squares + wide * wide
            return squares

        squares = lax.fori_loop(0, SIDE, gather_products, jnp.zeros((2 * CHUNK, LANES), F32))
        scale = lax.rsqrt(jnp.sum(squares, axis=1, keepdims=True) / width + 1e-05)
        diagonal = lax.broadcasted_iota(jnp.int32, (CHUNK, CHUNK), 0) == lax.broadcasted_iota(
            jnp.int32, (CHUNK, CHUNK), 1
        )
        for k in range(2):
            factor = jnp.concatenate(
                [
                    jnp.sum(
                        jnp.where(diagonal, side_in[2 * j + i, k : k + 1, :], 0.0),
                        axis=1,
                        keepdims=True,
                    )
                    for i in range(2)
                ],
                axis=0,
            )
            gate, up = [
                acc[:, (2 * k + i) * hidden_size : (2 * k + i + 1) * hidden_size] * scale
                for i in range(2)
            ]
            inner = gate / (1.0 + jnp.exp(-gate)) * up * factor
            hidden[:, k * hidden_size : (k + 1) * hidden_size] = inner.astype(BF)

        for chosen in (SPREAD[:2], SPREAD[2:]):

            @pl.when(2 * j == chosen[0])
            def _():
                for c in chosen:
                    spreader.sent(c)

        @pl.loop(0, SIDE)
        def _(z):
            columns = pl.ds(pl.multiple_of(z * 4 * SLICE, 4 * SLICE), 4 * SLICE)
            block = jnp.dot(hidden[...], w_down[:, columns], preferred_element_type=F32)
            for i in range(2):
                store_quarter(chunks[i], z, block[i * CHUNK : (i + 1) * CHUNK])

    def turn(it, carry):
        def stage(lag, body):
            j = it - lag

            @pl.when((j >= 0) & (j < TURNS))
            def _():
                for i in range(2):
                    body(2 * j + i)

        def add(step):
            def body(c):
                summer.arrive(step - 1, c)
                summer.add(step - 1, c)
                summer.start(step, c)

            return body

        def spread(step, chunks):
            for c in chunks:
                if step == 0:
                    for copy in slices(c):
                        copy.wait_recv()
                else:
                    spreader.arrive(step - 1, c)
                if step < 4:
                    spreader.start(step, c)

        stage(5, mix)
        stage(4, finish_sum)
        stage(3, add(3))
        stage(2, add(2))
        stage(1, add(1))

        @pl.when(it == 0)
        def _():
            spread(0, SPREAD[2:])
            spread(3, SPREAD[:2])
            whole(1).wait_recv()
            side(1).wait_recv()
            for load in loads:
                load.wait()

        @pl.when(it == 1)
        def _():
            spread(2, SPREAD[2:])
            spread(4, SPREAD[:2])
            for c in SPREAD[:2]:
                side(c).wait_recv()

        @pl.when(it == 2)
        def _():
            for c in WHOLE[1:]:
                whole(c).wait_send()
            for c in SPREAD[2:]:
                choose_whole(c, ready.at[c - 6], (1 - SPREAD_HALVES[c][0],))
                other_half(c).start()
            for c in WHOLE[1:]:
                whole(c).wait_recv()
                side(c).wait_recv()

        @pl.when(it == 3)
        def _():
            spread(4, SPREAD[2:])
            for c in SPREAD[2:]:
                other_half(c).wait_recv()
                side(c).wait_recv()

        @pl.when(it < TURNS)
        def _():
            compute(it)
            for i in range(2):
                summer.start(0, 2 * it + i)

        @pl.when(it == 0)
        def _():
            spread(1, SPREAD[2:])

        @pl.when(it == 1)
        def _():
            spread(3, SPREAD[2:])

        return carry

    lax.fori_loop(0, TURNS + 5, turn, 0)

    total = mixing[...]
    for_odd = pltpu.roll(
        jnp.concatenate([total[:, 3 * LANES :], total[:, : 3 * LANES]], axis=1),
        4 * LANES - SHARED,
        1,
    )
    mixed_ref[...] = jnp.where(is_odd == 1, for_odd, total)[:, :SLICE].astype(BF)

    @pl.loop(0, CHUNKS)
    def _(c):
        summer.sent(c)

    for b in range(row_blocks):
        gatherer.sent(b)
    for c in range(1, CHUNKS):
        side(c).wait_send()
        back(c).wait_send()
    for c in SPREAD:
        for copy in slices(c):
            copy.wait_send()
    for c in SPREAD[2:]:
        other_half(c).wait_send()


def feed(
    expert_ids,
    route_weights,
    state,
    expert_gate,
    expert_up,
    expert_down,
    dense_gate,
    dense_up,
    dense_down,
):
    rows = expert_ids.shape[0]
    width, hidden_size = dense_gate.shape
    vmem = pl.BlockSpec(memory_space=pltpu.VMEM)
    hbm = pl.BlockSpec(memory_space=pl.ANY)
    row_blocks = rows // CHUNK
    return pl.pallas_call(
        feed_kernel,
        out_shape=jax.ShapeDtypeStruct((rows, SLICE), BF),
        in_specs=[vmem] * 3 + [hbm] * 6,
        out_specs=vmem,
        scratch_shapes=[
            pltpu.VMEM((CHUNKS, 2, 16, HALF, LANES), BF),
            pltpu.VMEM((row_blocks, 2, 16, HALF, LANES), BF),
            pltpu.VMEM((2, 2, 16, HALF, LANES), BF),
            pltpu.VMEM((SLOTS, 2, 2, 2, HALF, LANES), BF),
            pltpu.VMEM((SLOTS, 2, 2, SIDE, HALF, LANES), BF),
            pltpu.VMEM((SLOTS, 2, 2, QUARTER, LANES), BF),
            pltpu.VMEM((SLOTS, 2, 2, HALF, LANES), BF),
            pltpu.VMEM((4 * hidden_size, width), BF),
            pltpu.VMEM((2 * hidden_size, width), BF),
            pltpu.VMEM((len(SPREAD), SLICE, LANES), BF),
            pltpu.VMEM((CHUNKS, 8, LANES), F32),
            pltpu.VMEM((CHUNKS, 8, LANES), F32),
            pltpu.VMEM((CHUNKS, SLICE, LANES), BF),
            pltpu.VMEM((CHUNKS, SLICE, LANES), BF),
            pltpu.VMEM((rows, LANES), F32),
            pltpu.VMEM((2 * CHUNK, 4 * hidden_size), F32),
            pltpu.VMEM((2 * CHUNK, 2 * hidden_size), BF),
            pltpu.VMEM((rows, 4 * LANES), F32),
            pltpu.SemaphoreType.DMA((6,)),
        ]
        + [pltpu.SemaphoreType.DMA((row_blocks, 4, 2, 2))] * 2
        + [pltpu.SemaphoreType.DMA((CHUNKS, 4, 2, 2))] * 4
        + [pltpu.SemaphoreType.DMA((CHUNKS, 2))] * 2
        + [pltpu.SemaphoreType.DMA((CHUNKS,))] * 4,
        compiler_params=pltpu.CompilerParams(
            collective_id=2, has_side_effects=True, vmem_limit_bytes=64 * 1024 * 1024 - 65536
        ),
        name="feed",
    )(
        expert_ids.T,
        route_weights.T,
        state,
        jnp.swapaxes(expert_gate, 1, 2),
        jnp.swapaxes(expert_up, 1, 2),
        expert_down,
        dense_gate.T,
        dense_up.T,
        dense_down,
    )


def from_partner(block):
    return lax.ppermute(block, "tensor", [(i, i ^ 1) for i in range(lax.axis_size("tensor"))])


def attend(queries, new_kv, kv_cache, lengths):
    row_count = queries.shape[0]
    rank = lax.axis_index("tensor")
    my_head, my_part = rank // 2, rank % 2
    head_size = new_kv.shape[3]
    span = kv_cache.shape[2]
    rows = lax.dynamic_index_in_dim(queries, my_head, 1, keepdims=False).reshape(
        row_count, -1, head_size
    )
    new_key = lax.dynamic_index_in_dim(new_kv[0], my_head, 1, keepdims=False)
    new_value = lax.dynamic_index_in_dim(new_kv[1], my_head, 1, keepdims=False)
    scale = 1.0 / math.sqrt(head_size)
    scores = jnp.einsum("tgd,tpd->tgp", rows, kv_cache[0], preferred_element_type=F32) * scale
    own = jnp.einsum("tgd,td->tg", rows, new_key, preferred_element_type=F32) * scale
    position = my_part * span + jnp.arange(span, dtype=jnp.int32)
    usable = position[None, None, :] < lengths[:, None, None]
    masked = jnp.where(usable, scores, -1e30)
    highest = jnp.maximum(jnp.max(masked, axis=-1), own)
    weights = jnp.where(usable, jnp.exp(masked - highest[..., None]), 0.0).astype(BF)
    own_weight = jnp.exp(own - highest)
    leading = (my_part == 0).astype(F32)
    numerator = jnp.einsum("tgp,tpd->tgd", weights, kv_cache[1], preferred_element_type=F32)
    numerator = numerator + leading * own_weight[..., None] * new_value.astype(F32)[:, None, :]
    denominator = jnp.sum(weights.astype(F32), axis=-1) + leading * own_weight
    width = rows.shape[1] * head_size
    flat = numerator.reshape(row_count, width)
    mine = lax.dynamic_slice_in_dim(flat, my_part * (width // 2), width // 2, 1)
    theirs = lax.dynamic_slice_in_dim(flat, (1 - my_part) * (width // 2), width // 2, 1)
    other, other_marks = from_partner((theirs.astype(BF), jnp.stack([highest, denominator])))
    other_highest, other_denominator = other_marks[0], other_marks[1]
    top = jnp.maximum(highest, other_highest)
    keep, take = jnp.exp(highest - top), jnp.exp(other_highest - top)
    below = 1.0 / (denominator * keep + other_denominator * take)
    keep = jnp.repeat(keep * below, head_size, axis=1)
    take = jnp.repeat(take * below, head_size, axis=1)
    keep = lax.dynamic_slice_in_dim(keep, my_part * (width // 2), width // 2, 1)
    take = lax.dynamic_slice_in_dim(take, my_part * (width // 2), width // 2, 1)
    return (mine * keep + other.astype(F32) * take).astype(BF)


def shards(
    residual,
    queries,
    new_kv,
    kv_cache,
    lengths,
    out_weight,
    dense_gate,
    dense_up,
    dense_down,
    expert_ids,
    route_weights,
    expert_gate,
    expert_up,
    expert_down,
):
    attention = attend(queries, new_kv, kv_cache, lengths)
    state = project(attention, out_weight, residual)
    return feed(
        expert_ids,
        route_weights,
        state,
        expert_gate,
        expert_up,
        expert_down,
        dense_gate,
        dense_up,
        dense_down,
    )


def solution(mesh):
    placed = (
        P("group", None),
        P("group", None, None),
        P(None, "group", None, None),
        P(None, "group", "tensor", None),
        P("group"),
        P("tensor", None),
        P(None, "tensor"),
        P(None, "tensor"),
        P("tensor", None),
        P("group", None),
        P("group", None),
        P("group", None, "tensor"),
        P("group", None, "tensor"),
        P("group", "tensor", None),
    )
    return jax.shard_map(
        shards, mesh=mesh, in_specs=placed, out_specs=P("group", "tensor"), check_vma=False
    )
```

```python
import functools
import math

import jax
import jax.numpy as jnp
from jax import lax
from jax.experimental import pallas as pl
from jax.experimental.pallas import tpu as pltpu
from jax.sharding import PartitionSpec as P

BF = jnp.bfloat16
F32 = jnp.float32
SIDE = 4
LANES = 128
CHUNK = 128
SLICE = 448
HALF = SLICE // 2
SHARED = 64
CHUNKS = 8


def ring(value, step):
    return lax.rem(value + step + SIDE, SIDE)


class Place:
    def __init__(self):
        rank = lax.axis_index("tensor")
        self.rank = rank
        self.z = rank // SIDE
        self.x = lax.rem(rank, SIDE)

    def axes(self, half):
        return (self.x, self.z) if half == 0 else (self.z, self.x)

    def at(self, half, p, q):
        return q * SIDE + p if half == 0 else p * SIDE + q


def spot(half, z, x):
    return z * SIDE + x if half == 0 else x * SIDE + z


def split_rows(low, high):
    pieces = []
    if low < HALF:
        pieces.append((0, low, min(high, HALF), 0))
    if high > HALF:
        start = max(low, HALF)
        pieces.append((1, start - HALF, high - HALF, start - low))
    return pieces


def read_rows(part, z, x, low, high):
    pieces = [part[h, spot(h, z, x), a:b, :] for h, a, b, _ in split_rows(low, high)]
    return pieces[0] if len(pieces) == 1 else jnp.concatenate(pieces, axis=0)


def write_rows(part, z, x, low, value, halves=(0, 1)):
    for h, a, b, offset in split_rows(low, low + value.shape[0]):
        if h in halves:
            part[h, spot(h, z, x), a:b, :] = value[offset : offset + b - a]


def copy_to(src, dst, send, recv, rank):
    return pltpu.make_async_remote_copy(
        src_ref=src,
        dst_ref=dst,
        send_sem=send,
        recv_sem=recv,
        device_id={"tensor": rank},
        device_id_type=pl.DeviceIdType.MESH,
    )


def lanes_low(rows):
    return lax.broadcasted_iota(jnp.int32, (rows, LANES), 1) < SHARED


def turned(block):
    return pltpu.roll(block, SHARED, 1)


def unfold_pair(even_half, odd_half):
    low = lanes_low(SHARED)
    e, o = even_half.astype(F32), odd_half.astype(F32)
    top = jnp.where(low, e, o)
    bottom = turned(jnp.where(low, o, e))
    return jnp.concatenate([top, bottom], axis=0).astype(BF)


def fold_pair(tile):
    low = lanes_low(SHARED)
    top, bottom = tile[:SHARED], turned(tile[SHARED:])
    return jnp.where(low, top, bottom).astype(BF), jnp.where(low, bottom, top).astype(BF)


def unfold_own(half):
    half = half.astype(F32)
    return jnp.concatenate([half, turned(half)], axis=0)


def fold_own(tile, is_odd):
    low = lanes_low(SHARED).astype(jnp.int32) != is_odd
    top, bottom = tile[:SHARED], turned(tile[SHARED:])
    return jnp.where(low, top, bottom)


def natural_own(ref, is_odd):
    first = pl.multiple_of(is_odd * SHARED, SHARED)
    half = pl.multiple_of((1 - is_odd) * (SLICE - SHARED), SHARED)
    tiles = [ref[pl.ds(first + k * LANES, LANES), :].astype(F32) for k in range(3)]
    return jnp.concatenate(tiles + [unfold_own(ref[pl.ds(half, SHARED), :])], axis=1)


def store_own(ref, block, is_odd):
    first = pl.multiple_of(is_odd * SHARED, SHARED)
    half = pl.multiple_of((1 - is_odd) * (SLICE - SHARED), SHARED)
    for k in range(3):
        ref[pl.ds(first + k * LANES, LANES), :] = block[:, k * LANES : (k + 1) * LANES].astype(BF)
    ref[pl.ds(half, SHARED), :] = fold_own(block[:, 3 * LANES :], is_odd).astype(BF)


def store_quarter(part, z, block, halves=(0, 1)):
    for pair in range(2):
        e, o = 2 * pair, 2 * pair + 1
        tiles = [
            block[:, (pair * 7 + k) * LANES : (pair * 7 + k + 1) * LANES] for k in range(7)
        ]
        even_half, odd_half = fold_pair(tiles[3])
        for k in range(3):
            write_rows(part, z, e, k * LANES, tiles[k].astype(BF), halves)
            write_rows(part, z, o, SHARED + k * LANES, tiles[4 + k].astype(BF), halves)
        write_rows(part, z, e, SLICE - SHARED, even_half, halves)
        write_rows(part, z, o, 0, odd_half, halves)


def load_quarter(part, z):
    blocks = []
    for pair in range(2):
        e, o = 2 * pair, 2 * pair + 1
        blocks += [read_rows(part, z, e, k * LANES, (k + 1) * LANES) for k in range(3)]
        blocks.append(
            unfold_pair(
                read_rows(part, z, e, SLICE - SHARED, SLICE), read_rows(part, z, o, 0, SHARED)
            )
        )
        blocks += [
            read_rows(part, z, o, SHARED + k * LANES, SHARED + (k + 1) * LANES) for k in range(3)
        ]
    return jnp.concatenate(blocks, axis=1)


def add_into(dst, other):
    dst[...] = (dst[...].astype(F32) + other[...].astype(F32)).astype(BF)


class Exchange:
    def start(self, step, c):
        for copy in self.copies(step, c):
            copy.start()

    def arrive(self, step, c):
        for copy in self.copies(step, c):
            copy.wait_recv()

    def sent(self, c):
        for step in range(4):
            for copy in self.copies(step, c):
                copy.wait_send()


WAYS = ((0, 0, 1), (0, 1, -1), (1, 0, 1), (1, 1, -1))
QUARTER = HALF // 2


class Summer(Exchange):
    def __init__(self, place, part, landing, send, recv):
        self.place, self.part, self.landing = place, part, landing
        self.send, self.recv = send, recv

    def landed(self, step, c):
        landing = self.landing[step]
        return landing.at[lax.rem(c, landing.shape[0])]

    def copies(self, step, c):
        place = self.place
        result = []
        for h, way, hop in WAYS:
            part = self.part.at[c, h]
            p, q = place.axes(h)
            if step == 0:
                src = part.at[pl.ds(ring(q, 2) * SIDE + 2 * way, 2)]
                to = place.at(h, p, ring(q, hop))
            elif step == 1:
                src = part.at[pl.ds(ring(q, hop) * SIDE, SIDE)]
                to = place.at(h, p, ring(q, hop))
            elif step == 2:
                src = part.at[q * SIDE + ring(p, 2), pl.ds(way * QUARTER, QUARTER)]
                to = place.at(h, ring(p, hop), q)
            else:
                src = part.at[q * SIDE + ring(p, hop)]
                to = place.at(h, ring(p, hop), q)
            result.append(
                copy_to(
                    src,
                    self.landed(step, c).at[h, way],
                    self.send.at[c, step, h, way],
                    self.recv.at[c, step, h, way],
                    to,
                )
            )
        return result

    def add(self, step, c):
        for h in range(2):
            part = self.part.at[c, h]
            p, q = self.place.axes(h)
            landed = self.landed(step, c).at[h]
            if step == 0:
                for way, hop in ((0, 1), (1, -1)):
                    for k in range(2):
                        add_into(part.at[ring(q, hop) * SIDE + 2 * way + k], landed.at[way, k])
            elif step == 1:
                for k in range(SIDE):
                    dst = part.at[q * SIDE + k]
                    dst[...] = (
                        dst[...].astype(F32) + landed[0, k].astype(F32) + landed[1, k].astype(F32)
                    ).astype(BF)
            elif step == 2:
                for way, hop in ((0, 1), (1, -1)):
                    add_into(
                        part.at[q * SIDE + ring(p, hop), pl.ds(way * QUARTER, QUARTER)],
                        landed.at[way],
                    )

    def total(self, c):
        halves = []
        for h in range(2):
            p, q = self.place.axes(h)
            landed = self.landed(3, c).at[h]
            halves.append(
                self.part[c, h, q * SIDE + p].astype(F32)
                + landed[0].astype(F32)
                + landed[1].astype(F32)
            )
        return jnp.concatenate(halves, axis=0)


class Spreader(Exchange):
    def __init__(self, place, part, send, recv, halves=None):
        self.place, self.part, self.send, self.recv = place, part, send, recv
        self.halves = halves or {}

    def copies(self, step, c):
        place = self.place
        result = []
        for h, way, hop in WAYS:
            if h not in self.halves.get(c, (0, 1)):
                continue
            part = self.part.at[c, h]
            p, q = place.axes(h)
            if step == 0:
                ref = part.at[q * SIDE + p]
                to = place.at(h, ring(p, hop), q)
            elif step == 1:
                ref = part.at[q * SIDE + ring(p, -hop), pl.ds(way * QUARTER, QUARTER)]
                to = place.at(h, ring(p, hop), q)
            elif step == 2:
                ref = part.at[pl.ds(q * SIDE, SIDE)]
                to = place.at(h, p, ring(q, hop))
            else:
                ref = part.at[pl.ds(ring(q, -hop) * SIDE + 2 * way, 2)]
                to = place.at(h, p, ring(q, hop))
            result.append(
                copy_to(
                    ref,
                    ref,
                    self.send.at[c, step, h, way],
                    self.recv.at[c, step, h, way],
                    to,
                )
            )
        return result


def greet_plane(place, barrier):
    for hop in (1, -1):
        for rank in (
            place.at(0, ring(place.x, hop), place.z),
            place.at(0, place.x, ring(place.z, hop)),
        ):
            pl.semaphore_signal(
                barrier, inc=1, device_id={"tensor": rank}, device_id_type=pl.DeviceIdType.MESH
            )


def flipped(group, bits):
    b = (lax.rem(group, 2), lax.rem(group // 2, 2), group // 4)
    return sum((b[k] + bits[k] - 2 * b[k] * bits[k]) * (1 << k) for k in range(3))


PARTNERS = (0, 1, 4, 5, 2, 6, 3, 7)
WHOLE = (1, 4, 5)
SPREAD = (2, 3, 6, 7)
SPREAD_HALVES = {2: (0, 1), 3: (0, 1), 6: (1,), 7: (0,)}
TURNS = CHUNKS // 2
SLOTS = 4


def chunk_bits(c):
    if isinstance(c, int):
        return tuple((PARTNERS[c] >> k) & 1 for k in range(3))
    return tuple(
        sum(jnp.where(c == i, 1, 0) for i in range(CHUNKS) if (PARTNERS[i] >> k) & 1)
        for k in range(3)
    )


def to_group(src, dst, send, recv, group):
    return pltpu.make_async_remote_copy(
        src_ref=src,
        dst_ref=dst,
        send_sem=send,
        recv_sem=recv,
        device_id={"group": group},
        device_id_type=pl.DeviceIdType.MESH,
    )


def layer_kernel(
    numerator_ref,
    marks_ref,
    ids_ref,
    route_ref,
    residual_ref,
    out_weight,
    expert_gate,
    expert_up,
    expert_down,
    dense_gate,
    dense_up,
    dense_down,
    mixed_ref,
    other,
    other_marks,
    near,
    state_ref,
    part,
    full,
    ready,
    r1,
    r2,
    r3,
    r4,
    w_in,
    w_down,
    outgoing,
    side_out,
    side_in,
    returned,
    own_pos,
    acc,
    hidden,
    mixing,
    load_sem,
    first_sem,
    swap_send,
    swap_recv,
    state_send,
    state_recv,
    full_send,
    full_recv,
    spread_send,
    spread_recv,
    sum_send,
    sum_recv,
    go_send,
    go_recv,
    side_send,
    side_recv,
    back_send,
    back_recv,
):
    place = Place()
    group = lax.axis_index("group")
    is_odd = lax.rem(place.rank, 2)
    hidden_size = w_in.shape[0] // 4
    rows = ids_ref.shape[1]
    row_blocks = rows // CHUNK
    width = 16 * SLICE

    head_part = lax.rem(place.rank, 2)
    skipped = pl.multiple_of(head_part * SHARED, SHARED)
    fetch_out = pltpu.make_async_copy(
        out_weight, w_in.at[pl.ds(skipped, SLICE)], first_sem.at[0]
    )
    first_column = pl.multiple_of((place.rank // 2) * 2 * SLICE, 2 * SLICE)
    fetch_near = pltpu.make_async_copy(
        residual_ref.at[:, pl.ds(first_column, 2 * SLICE)], near, first_sem.at[1]
    )
    loads = [
        pltpu.make_async_copy(
            ref, w_in.at[pl.ds(k * hidden_size, hidden_size)], load_sem.at[k]
        )
        for k, ref in enumerate((expert_gate.at[0], expert_up.at[0], dense_gate, dense_up))
    ] + [
        pltpu.make_async_copy(
            ref, w_down.at[pl.ds(k * hidden_size, hidden_size)], load_sem.at[4 + k]
        )
        for k, ref in enumerate((expert_down.at[0], dense_down))
    ]
    fetch_out.start()
    fetch_near.start()
    for load in loads[4:]:
        load.start()
    w_in[pl.ds(pl.multiple_of((1 - head_part) * SLICE, SHARED), SHARED), :] = jnp.zeros(
        (SHARED, width), BF
    )

    barrier = pltpu.get_barrier_semaphore()
    greet_plane(place, barrier)
    for c in range(1, CHUNKS):
        pl.semaphore_signal(
            barrier,
            inc=1,
            device_id={"group": flipped(group, chunk_bits(c))},
            device_id_type=pl.DeviceIdType.MESH,
        )
    pl.semaphore_wait(barrier, 4 + CHUNKS - 1)

    mate = place.rank + 1 - 2 * head_part
    theirs = pl.multiple_of((1 - head_part) * 3 * LANES, LANES)
    mine = head_part * 3 * LANES

    swaps = [copy_to(marks_ref, other_marks, swap_send.at[0], swap_recv.at[0], mate)] + [
        copy_to(
            numerator_ref.at[pl.ds(b * CHUNK, CHUNK), pl.ds(theirs, 4 * LANES)],
            other.at[pl.ds(b * CHUNK, CHUNK)],
            swap_send.at[1 + b],
            swap_recv.at[1 + b],
            mate,
        )
        for b in range(row_blocks)
    ]
    for copy in swaps:
        copy.start()

    gatherer = Spreader(place, full, full_send, full_recv)
    spreader = Spreader(place, part, spread_send, spread_recv, SPREAD_HALVES)
    summer = Summer(place, part, (r1, r2, r3, r4), sum_send, sum_recv)
    state_summer = Summer(place, ready, (r1, r2, r3, r4), state_send, state_recv)

    line = lax.broadcasted_iota(jnp.int32, (rows, rows), 0)
    column = lax.broadcasted_iota(jnp.int32, (rows, rows), 1)

    def upright(row):
        return jnp.sum(jnp.where(line == column, row, 0.0), axis=1, keepdims=True)

    flat_ids = [ids_ref[k : k + 1, :].astype(F32) for k in range(2)]
    ids = [upright(row) for row in flat_ids]
    route = [upright(route_ref[k : k + 1, :]) for k in range(2)]
    partners = [flipped(group, chunk_bits(c)).astype(F32) for c in range(CHUNKS)]
    lane = lax.broadcasted_iota(jnp.int32, (rows, LANES), 1)
    partner_of_lane = jnp.full((rows, LANES), -1.0, F32)
    sub = lax.broadcasted_iota(jnp.int32, (CHUNKS, rows), 0)
    partner_of_sub = jnp.zeros((CHUNKS, rows), F32)
    for c in range(CHUNKS):
        partner_of_lane = jnp.where(lane == c, partners[c], partner_of_lane)
        partner_of_sub = jnp.where(sub == c, partners[c], partner_of_sub)
    first_choice, second_choice = [choice == partner_of_lane for choice in ids]
    named = jnp.where(first_choice | second_choice, 1.0, 0.0)
    before = jnp.where(column < line, 1.0, 0.0).astype(BF)
    place_in = jnp.dot(before, named.astype(BF), preferred_element_type=F32)
    positions = jnp.where(named > 0.5, place_in, -1.0)
    own_pos[...] = positions
    flat_named = jnp.where(
        (flat_ids[0] == partner_of_sub) | (flat_ids[1] == partner_of_sub), 1.0, 0.0
    )
    after = jnp.where(line < column, 1.0, 0.0).astype(BF)
    flat_place = jnp.dot(flat_named.astype(BF), after, preferred_element_type=F32)
    flat_pos = jnp.where(flat_named > 0.5, flat_place, -1.0)
    weight = jnp.where(first_choice, route[0], 0.0) + jnp.where(second_choice, route[1], 0.0)
    dense_here = jnp.where(first_choice, 1.0, 0.0)
    slot_line = lax.broadcasted_iota(jnp.int32, (CHUNK, rows), 0).astype(F32)
    slot_lane = lax.broadcasted_iota(jnp.int32, (rows, CHUNK), 1).astype(F32)
    sides = lax.broadcasted_iota(jnp.int32, (8, LANES), 0)

    def pick(c):
        return jnp.where(flat_pos[c : c + 1, :] == slot_line, 1.0, 0.0).astype(BF)

    def partner(c):
        return flipped(group, chunk_bits(c))

    def side(c):
        return to_group(
            side_out.at[c], side_in.at[c], side_send.at[c], side_recv.at[c], partner(c)
        )

    def slices(c):
        return [
            to_group(
                outgoing.at[SPREAD.index(c), pl.ds(h * HALF, HALF)],
                part.at[c, h, spot(h, place.z, place.x)],
                go_send.at[c, h],
                go_recv.at[c, h],
                partner(c),
            )
            for h in SPREAD_HALVES[c]
        ]

    def whole(c):
        slot = 1 if c == 5 else 0
        return to_group(
            ready.at[slot], part.at[c], go_send.at[c, 0], go_recv.at[c, 0], partner(c)
        )

    def other_half(c):
        h = 1 - SPREAD_HALVES[c][0]
        return to_group(
            ready.at[c - 6, h], part.at[c, h], go_send.at[c, h], go_recv.at[c, h], partner(c)
        )

    swaps[0].wait_recv()
    top = jnp.maximum(marks_ref[0:8, :], other_marks[0:8, :])
    keep = jnp.exp(marks_ref[0:8, :] - top)
    take = jnp.exp(other_marks[0:8, :] - top)
    below = 1.0 / (marks_ref[8:16, :] * keep + other_marks[8:16, :] * take)
    scales = jnp.concatenate(
        [keep * below, take * below, jnp.zeros((LANES - 16, rows), F32)], axis=0
    ).T
    low = lanes_low(CHUNK)
    for b in range(row_blocks):
        swaps[1 + b].wait_recv()
        block_rows = slice(b * CHUNK, (b + 1) * CHUNK)
        joined = []
        for k in range(4):
            factors = [
                jnp.where(
                    head_part == 1,
                    scales[block_rows, at + k + 3 : at + k + 4],
                    scales[block_rows, at + k : at + k + 1],
                )
                for at in (0, 8)
            ]
            here = numerator_ref[
                block_rows, pl.ds(pl.multiple_of(mine + k * LANES, LANES), LANES)
            ].astype(F32)
            there = other[block_rows, k * LANES : (k + 1) * LANES].astype(F32)
            tile = here * factors[0] + there * factors[1]
            if k == 0:
                tile = jnp.where(low & (head_part == 1), 0.0, tile)
            if k == 3:
                tile = jnp.where(low | (head_part == 1), tile, 0.0)
            joined.append(tile.astype(BF))
        attention = jnp.concatenate(joined, axis=1)
        if b == 0:
            fetch_out.wait()

        @pl.loop(0, SIDE)
        def _(z):
            columns = pl.ds(pl.multiple_of(z * 4 * SLICE, 4 * SLICE), 4 * SLICE)
            block = jnp.dot(
                attention, w_in[: SLICE + SHARED, columns], preferred_element_type=F32
            )
            store_quarter(ready.at[b], z, block)

        state_summer.start(0, b)
    for load in loads[:4]:
        load.start()
    for b in range(row_blocks):
        state_summer.arrive(0, b)
        state_summer.add(0, b)
        state_summer.start(1, b)
    for c in range(CHUNKS):
        at_slot = positions[:, c : c + 1] == slot_lane
        w_row = jnp.sum(jnp.where(at_slot, weight[:, c : c + 1], 0.0), axis=0, keepdims=True)
        d_row = jnp.sum(jnp.where(at_slot, dense_here[:, c : c + 1], 0.0), axis=0, keepdims=True)
        both = jnp.where(sides == 0, w_row, jnp.where(sides == 1, d_row, 0.0))
        if c == 0:
            side_in[0] = both
        else:
            side_out[c] = both
            side(c).start()
    for step in range(2, 4):
        for b in range(row_blocks):
            state_summer.arrive(step - 1, b)
            state_summer.add(step - 1, b)
            state_summer.start(step, b)
    fetch_near.wait()
    for b in range(row_blocks):
        block_rows = slice(b * CHUNK, (b + 1) * CHUNK)
        even = [near[block_rows, k * LANES : (k + 1) * LANES].astype(F32) for k in range(4)]
        odd = [near[block_rows, (k + 4) * LANES : (k + 5) * LANES].astype(F32) for k in range(3)]
        whole_tiles = [jnp.where(is_odd == 1, odd[k], even[k]) for k in range(3)]
        store_own(state_ref.at[b], jnp.concatenate(whole_tiles + [even[3]], axis=1), is_odd)
        state_summer.arrive(3, b)
        state = (state_ref[b].astype(F32) + state_summer.total(b)).astype(BF)
        state_ref[b] = state
        for h in range(2):
            full[b, h, spot(h, place.z, place.x)] = state[h * HALF : (h + 1) * HALF]
        gatherer.start(0, b)
    for b in range(row_blocks):
        mixing[b * CHUNK : (b + 1) * CHUNK, :] = natural_own(state_ref.at[b], is_odd)

    for c in SPREAD:
        chosen = jnp.dot(pick(c), mixing[...].astype(BF), preferred_element_type=F32)
        store_own(outgoing.at[SPREAD.index(c)], chosen, is_odd)
        for copy in slices(c):
            copy.start()
    for b in range(row_blocks):
        gatherer.arrive(0, b)
        gatherer.start(1, b)
    for b in range(row_blocks):
        gatherer.arrive(1, b)
        gatherer.start(2, b)
    for c in SPREAD[:2]:
        for copy in slices(c):
            copy.wait_recv()
        spreader.start(0, c)
    for b in range(row_blocks):
        gatherer.arrive(2, b)
        gatherer.start(3, b)
    for c in SPREAD[:2]:
        spreader.arrive(0, c)
        spreader.start(1, c)
    for c in SPREAD[:2]:
        spreader.arrive(1, c)
        spreader.start(2, c)
    for b in range(row_blocks):
        gatherer.arrive(3, b)

    def choose_whole(c, target, halves=(0, 1)):
        chosen_rows = pick(c)

        @pl.loop(0, SIDE)
        def _(z):
            source = jnp.concatenate(
                [load_quarter(full.at[b], z) for b in range(row_blocks)], axis=0
            )
            store_quarter(
                target, z, jnp.dot(chosen_rows, source, preferred_element_type=F32), halves
            )

    for b in range(row_blocks):
        state_summer.sent(b)
    choose_whole(1, ready.at[0])
    whole(1).start()
    choose_whole(5, ready.at[1])
    whole(5).start()
    whole(1).wait_send()
    choose_whole(4, ready.at[0])
    whole(4).start()
    choose_whole(0, part.at[0])

    def back(c):
        return [
            to_group(
                ready.at[0, 1, 2 * c + h],
                returned.at[c, pl.ds(h * HALF, HALF)],
                back_send.at[c, h],
                back_recv.at[c, h],
                partner(c),
            )
            for h in range(2)
        ]

    def finish_sum(c):
        summer.arrive(3, c)
        total = summer.total(c).astype(BF)

        @pl.when(c == 0)
        def _():
            returned[0] = total

        @pl.when(c > 0)
        def _():
            for h, copy in enumerate(back(c)):
                ready[0, 1, 2 * c + h] = total[h * HALF : (h + 1) * HALF]
                copy.start()

    def mix(c):
        @pl.when(c > 0)
        def _():
            for copy in back(c):
                copy.wait_recv()

        position = jnp.sum(jnp.where(lane == c, own_pos[...], 0.0), axis=1, keepdims=True)
        at_slot = jnp.where(position == slot_lane, 1.0, 0.0).astype(BF)
        block = natural_own(returned.at[c], is_odd).astype(BF)
        mixing[...] += jnp.dot(at_slot, block, preferred_element_type=F32)

    def compute(j):
        chunks = [part.at[2 * j + i] for i in range(2)]
        acc[...] = jnp.zeros_like(acc)

        def gather_products(z, squares):
            block = jnp.concatenate([load_quarter(chunk, z) for chunk in chunks], axis=0)
            deep = pl.ds(pl.multiple_of(z * 4 * SLICE, 4 * SLICE), 4 * SLICE)
            acc[...] += lax.dot_general(
                block, w_in[:, deep], (((1,), (1,)), ((), ())), preferred_element_type=F32
            )
            for k in range(14):
                wide = block[:, k * LANES : (k + 1) * LANES].astype(F32)
                squares = squares + wide * wide
            return squares

        squares = lax.fori_loop(0, SIDE, gather_products, jnp.zeros((2 * CHUNK, LANES), F32))
        scale = lax.rsqrt(jnp.sum(squares, axis=1, keepdims=True) / width + 1e-05)
        diagonal = lax.broadcasted_iota(jnp.int32, (CHUNK, CHUNK), 0) == lax.broadcasted_iota(
            jnp.int32, (CHUNK, CHUNK), 1
        )
        for k in range(2):
            factor = jnp.concatenate(
                [
                    jnp.sum(
                        jnp.where(diagonal, side_in[2 * j + i, k : k + 1, :], 0.0),
                        axis=1,
                        keepdims=True,
                    )
                    for i in range(2)
                ],
                axis=0,
            )
            gate, up = [
                acc[:, (2 * k + i) * hidden_size : (2 * k + i + 1) * hidden_size] * scale
                for i in range(2)
            ]
            inner = gate / (1.0 + jnp.exp(-gate)) * up * factor
            hidden[:, k * hidden_size : (k + 1) * hidden_size] = inner.astype(BF)

        for chosen in (SPREAD[:2], SPREAD[2:]):

            @pl.when(2 * j == chosen[0])
            def _():
                for c in chosen:
                    spreader.sent(c)

        @pl.loop(0, SIDE)
        def _(z):
            columns = pl.ds(pl.multiple_of(z * 4 * SLICE, 4 * SLICE), 4 * SLICE)
            block = jnp.dot(hidden[...], w_down[:, columns], preferred_element_type=F32)
            for i in range(2):
                store_quarter(chunks[i], z, block[i * CHUNK : (i + 1) * CHUNK])

    def turn(it, carry):
        def stage(lag, body):
            j = it - lag

            @pl.when((j >= 0) & (j < TURNS))
            def _():
                for i in range(2):
                    body(2 * j + i)

        def add(step):
            def body(c):
                summer.arrive(step - 1, c)
                summer.add(step - 1, c)
                summer.start(step, c)

            return body

        def spread(step, chunks):
            for c in chunks:
                if step == 0:
                    for copy in slices(c):
                        copy.wait_recv()
                else:
                    spreader.arrive(step - 1, c)
                if step < 4:
                    spreader.start(step, c)

        stage(5, mix)
        stage(4, finish_sum)
        stage(3, add(3))
        stage(2, add(2))
        stage(1, add(1))

        @pl.when(it == 0)
        def _():
            spread(0, SPREAD[2:])
            spread(3, SPREAD[:2])
            whole(1).wait_recv()
            side(1).wait_recv()
            for load in loads:
                load.wait()

        @pl.when(it == 1)
        def _():
            spread(2, SPREAD[2:])
            spread(4, SPREAD[:2])
            for c in SPREAD[:2]:
                side(c).wait_recv()

        @pl.when(it == 2)
        def _():
            for c in WHOLE[1:]:
                whole(c).wait_send()
            for c in SPREAD[2:]:
                choose_whole(c, ready.at[c - 6], (1 - SPREAD_HALVES[c][0],))
                other_half(c).start()
            for c in WHOLE[1:]:
                whole(c).wait_recv()
                side(c).wait_recv()

        @pl.when(it == 3)
        def _():
            spread(4, SPREAD[2:])
            for c in SPREAD[2:]:
                other_half(c).wait_recv()
                side(c).wait_recv()

        @pl.when(it < TURNS)
        def _():
            compute(it)
            for i in range(2):
                summer.start(0, 2 * it + i)

        @pl.when(it == 0)
        def _():
            spread(1, SPREAD[2:])

        @pl.when(it == 1)
        def _():
            spread(3, SPREAD[2:])

        return carry

    lax.fori_loop(0, TURNS + 5, turn, 0)

    total = mixing[...]
    for_odd = pltpu.roll(
        jnp.concatenate([total[:, 3 * LANES :], total[:, : 3 * LANES]], axis=1),
        4 * LANES - SHARED,
        1,
    )
    mixed_ref[...] = jnp.where(is_odd == 1, for_odd, total)[:, :SLICE].astype(BF)

    @pl.loop(0, CHUNKS)
    def _(c):
        summer.sent(c)

    for copy in swaps:
        copy.wait_send()
    for b in range(row_blocks):
        gatherer.sent(b)
    for c in range(1, CHUNKS):
        side(c).wait_send()
        for copy in back(c):
            copy.wait_send()
    for c in SPREAD:
        for copy in slices(c):
            copy.wait_send()
    for c in SPREAD[2:]:
        other_half(c).wait_send()


def finish_layer(
    numerator,
    marks,
    residual,
    out_weight,
    expert_ids,
    route_weights,
    expert_gate,
    expert_up,
    expert_down,
    dense_gate,
    dense_up,
    dense_down,
):
    rows = expert_ids.shape[0]
    width, hidden_size = dense_gate.shape
    vmem = pl.BlockSpec(memory_space=pltpu.VMEM)
    hbm = pl.BlockSpec(memory_space=pl.ANY)
    row_blocks = rows // CHUNK
    return pl.pallas_call(
        layer_kernel,
        out_shape=jax.ShapeDtypeStruct((rows, SLICE), BF),
        in_specs=[vmem] * 4 + [hbm] * 8,
        out_specs=vmem,
        scratch_shapes=[
            pltpu.VMEM((rows, 4 * LANES), BF),
            pltpu.VMEM((16, rows), F32),
            pltpu.VMEM((rows, 2 * SLICE), BF),
            pltpu.VMEM((row_blocks, SLICE, LANES), BF),
            pltpu.VMEM((CHUNKS, 2, 16, HALF, LANES), BF),
            pltpu.VMEM((row_blocks, 2, 16, HALF, LANES), BF),
            pltpu.VMEM((2, 2, 16, HALF, LANES), BF),
            pltpu.VMEM((SLOTS, 2, 2, 2, HALF, LANES), BF),
            pltpu.VMEM((SLOTS, 2, 2, SIDE, HALF, LANES), BF),
            pltpu.VMEM((SLOTS, 2, 2, QUARTER, LANES), BF),
            pltpu.VMEM((SLOTS, 2, 2, HALF, LANES), BF),
            pltpu.VMEM((4 * hidden_size, width), BF),
            pltpu.VMEM((2 * hidden_size, width), BF),
            pltpu.VMEM((len(SPREAD), SLICE, LANES), BF),
            pltpu.VMEM((CHUNKS, 8, LANES), F32),
            pltpu.VMEM((CHUNKS, 8, LANES), F32),
            pltpu.VMEM((CHUNKS, SLICE, LANES), BF),
            pltpu.VMEM((rows, LANES), F32),
            pltpu.VMEM((2 * CHUNK, 4 * hidden_size), F32),
            pltpu.VMEM((2 * CHUNK, 2 * hidden_size), BF),
            pltpu.VMEM((rows, 4 * LANES), F32),
            pltpu.SemaphoreType.DMA((6,)),
            pltpu.SemaphoreType.DMA((2,)),
            pltpu.SemaphoreType.DMA((1 + row_blocks,)),
            pltpu.SemaphoreType.DMA((1 + row_blocks,)),
        ]
        + [pltpu.SemaphoreType.DMA((row_blocks, 4, 2, 2))] * 4
        + [pltpu.SemaphoreType.DMA((CHUNKS, 4, 2, 2))] * 4
        + [pltpu.SemaphoreType.DMA((CHUNKS, 2))] * 2
        + [pltpu.SemaphoreType.DMA((CHUNKS,))] * 2
        + [pltpu.SemaphoreType.DMA((CHUNKS, 2))] * 2,
        compiler_params=pltpu.CompilerParams(
            collective_id=1, has_side_effects=True, vmem_limit_bytes=64 * 1024 * 1024 - 65536
        ),
        name="layer",
    )(
        numerator,
        marks,
        expert_ids.T,
        route_weights.T,
        residual,
        out_weight,
        jnp.swapaxes(expert_gate, 1, 2),
        jnp.swapaxes(expert_up, 1, 2),
        expert_down,
        dense_gate.T,
        dense_up.T,
        dense_down,
    )


def attend(queries, new_kv, kv_cache, lengths):
    row_count = queries.shape[0]
    rank = lax.axis_index("tensor")
    my_head, my_part = rank // 2, rank % 2
    head_size = new_kv.shape[3]
    span = kv_cache.shape[2]
    rows = lax.dynamic_index_in_dim(queries, my_head, 1, keepdims=False).reshape(
        row_count, -1, head_size
    )
    new_key = lax.dynamic_index_in_dim(new_kv[0], my_head, 1, keepdims=False)
    new_value = lax.dynamic_index_in_dim(new_kv[1], my_head, 1, keepdims=False)
    scale = 1.0 / math.sqrt(head_size)
    scores = jnp.einsum("tgd,tpd->tgp", rows, kv_cache[0], preferred_element_type=F32) * scale
    own = jnp.einsum("tgd,td->tg", rows, new_key, preferred_element_type=F32) * scale
    position = my_part * span + jnp.arange(span, dtype=jnp.int32)
    usable = position[None, None, :] < lengths[:, None, None]
    masked = jnp.where(usable, scores, -1e30)
    highest = jnp.maximum(jnp.max(masked, axis=-1), own)
    weights = jnp.where(usable, jnp.exp(masked - highest[..., None]), 0.0).astype(BF)
    own_weight = jnp.exp(own - highest)
    leading = (my_part == 0).astype(F32)
    numerator = jnp.einsum("tgp,tpd->tgd", weights, kv_cache[1], preferred_element_type=F32)
    numerator = numerator + leading * own_weight[..., None] * new_value.astype(F32)[:, None, :]
    denominator = jnp.sum(weights.astype(F32), axis=-1) + leading * own_weight
    flat = numerator.astype(BF).reshape(row_count, -1)
    marks = jnp.concatenate(
        [
            jnp.pad(highest.T, ((0, 1), (0, 0))),
            jnp.pad(denominator.T, ((0, 1), (0, 0)), constant_values=1.0),
        ]
    )
    return flat, marks


def shards(
    residual,
    queries,
    new_kv,
    kv_cache,
    lengths,
    out_weight,
    dense_gate,
    dense_up,
    dense_down,
    expert_ids,
    route_weights,
    expert_gate,
    expert_up,
    expert_down,
):
    numerator, marks = attend(queries, new_kv, kv_cache, lengths)
    return finish_layer(
        numerator,
        marks,
        residual,
        out_weight,
        expert_ids,
        route_weights,
        expert_gate,
        expert_up,
        expert_down,
        dense_gate,
        dense_up,
        dense_down,
    )


def solution(mesh):
    placed = (
        P("group", None),
        P("group", None, None),
        P(None, "group", None, None),
        P(None, "group", "tensor", None),
        P("group"),
        P("tensor", None),
        P(None, "tensor"),
        P(None, "tensor"),
        P("tensor", None),
        P("group", None),
        P("group", None),
        P("group", None, "tensor"),
        P("group", None, "tensor"),
        P("group", "tensor", None),
    )
    return jax.shard_map(
        shards, mesh=mesh, in_specs=placed, out_specs=P("group", "tensor"), check_vma=False
    )
```

```python
import functools
import math

import jax
import jax.numpy as jnp
from jax import lax
from jax.experimental import pallas as pl
from jax.experimental.pallas import tpu as pltpu
from jax.sharding import PartitionSpec as P

BF = jnp.bfloat16
F32 = jnp.float32
SIDE = 4
LANES = 128
CHUNK = 128
SLICE = 448
HALF = SLICE // 2
SHARED = 64
CHUNKS = 8


def ring(value, step):
    return lax.rem(value + step + SIDE, SIDE)


class Place:
    def __init__(self):
        rank = lax.axis_index("tensor")
        self.rank = rank
        self.z = rank // SIDE
        self.x = lax.rem(rank, SIDE)

    def axes(self, half):
        return (self.x, self.z) if half == 0 else (self.z, self.x)

    def at(self, half, p, q):
        return q * SIDE + p if half == 0 else p * SIDE + q


def spot(half, z, x):
    return z * SIDE + x if half == 0 else x * SIDE + z


def split_rows(low, high):
    pieces = []
    if low < HALF:
        pieces.append((0, low, min(high, HALF), 0))
    if high > HALF:
        start = max(low, HALF)
        pieces.append((1, start - HALF, high - HALF, start - low))
    return pieces


def read_rows(part, z, x, low, high):
    pieces = [part[h, spot(h, z, x), a:b, :] for h, a, b, _ in split_rows(low, high)]
    return pieces[0] if len(pieces) == 1 else jnp.concatenate(pieces, axis=0)


def write_rows(part, z, x, low, value, halves=(0, 1)):
    for h, a, b, offset in split_rows(low, low + value.shape[0]):
        if h in halves:
            part[h, spot(h, z, x), a:b, :] = value[offset : offset + b - a]


def copy_to(src, dst, send, recv, rank):
    return pltpu.make_async_remote_copy(
        src_ref=src,
        dst_ref=dst,
        send_sem=send,
        recv_sem=recv,
        device_id={"tensor": rank},
        device_id_type=pl.DeviceIdType.MESH,
    )


def lanes_low(rows):
    return lax.broadcasted_iota(jnp.int32, (rows, LANES), 1) < SHARED


def turned(block):
    return pltpu.roll(block, SHARED, 1)


def unfold_pair(even_half, odd_half):
    low = lanes_low(SHARED)
    e, o = even_half.astype(F32), odd_half.astype(F32)
    top = jnp.where(low, e, o)
    bottom = turned(jnp.where(low, o, e))
    return jnp.concatenate([top, bottom], axis=0).astype(BF)


def fold_pair(tile):
    low = lanes_low(SHARED)
    top, bottom = tile[:SHARED], turned(tile[SHARED:])
    return jnp.where(low, top, bottom).astype(BF), jnp.where(low, bottom, top).astype(BF)


def unfold_own(half):
    half = half.astype(F32)
    return jnp.concatenate([half, turned(half)], axis=0)


def fold_own(tile, is_odd):
    low = lanes_low(SHARED).astype(jnp.int32) != is_odd
    top, bottom = tile[:SHARED], turned(tile[SHARED:])
    return jnp.where(low, top, bottom)


def natural_own(ref, is_odd):
    first = pl.multiple_of(is_odd * SHARED, SHARED)
    half = pl.multiple_of((1 - is_odd) * (SLICE - SHARED), SHARED)
    tiles = [ref[pl.ds(first + k * LANES, LANES), :].astype(F32) for k in range(3)]
    return jnp.concatenate(tiles + [unfold_own(ref[pl.ds(half, SHARED), :])], axis=1)


def store_own(ref, block, is_odd):
    first = pl.multiple_of(is_odd * SHARED, SHARED)
    half = pl.multiple_of((1 - is_odd) * (SLICE - SHARED), SHARED)
    for k in range(3):
        ref[pl.ds(first + k * LANES, LANES), :] = block[:, k * LANES : (k + 1) * LANES].astype(BF)
    ref[pl.ds(half, SHARED), :] = fold_own(block[:, 3 * LANES :], is_odd).astype(BF)


def store_quarter(part, z, block, halves=(0, 1)):
    for pair in range(2):
        e, o = 2 * pair, 2 * pair + 1
        tiles = [
            block[:, (pair * 7 + k) * LANES : (pair * 7 + k + 1) * LANES] for k in range(7)
        ]
        even_half, odd_half = fold_pair(tiles[3])
        for k in range(3):
            write_rows(part, z, e, k * LANES, tiles[k].astype(BF), halves)
            write_rows(part, z, o, SHARED + k * LANES, tiles[4 + k].astype(BF), halves)
        write_rows(part, z, e, SLICE - SHARED, even_half, halves)
        write_rows(part, z, o, 0, odd_half, halves)


def load_quarter(part, z):
    blocks = []
    for pair in range(2):
        e, o = 2 * pair, 2 * pair + 1
        blocks += [read_rows(part, z, e, k * LANES, (k + 1) * LANES) for k in range(3)]
        blocks.append(
            unfold_pair(
                read_rows(part, z, e, SLICE - SHARED, SLICE), read_rows(part, z, o, 0, SHARED)
            )
        )
        blocks += [
            read_rows(part, z, o, SHARED + k * LANES, SHARED + (k + 1) * LANES) for k in range(3)
        ]
    return jnp.concatenate(blocks, axis=1)


def add_into(dst, other):
    dst[...] = (dst[...].astype(F32) + other[...].astype(F32)).astype(BF)


class Exchange:
    def start(self, step, c, halves=(0, 1)):
        for copy in self.copies(step, c, halves):
            copy.start()

    def arrive(self, step, c, halves=(0, 1)):
        for copy in self.copies(step, c, halves):
            copy.wait_recv()

    def sent(self, c):
        for step in range(4):
            for copy in self.copies(step, c):
                copy.wait_send()


WAYS = ((0, 0, 1), (0, 1, -1), (1, 0, 1), (1, 1, -1))
QUARTER = HALF // 2


class Summer(Exchange):
    def __init__(self, place, part, landing, send, recv):
        self.place, self.part, self.landing = place, part, landing
        self.send, self.recv = send, recv

    def landed(self, step, c):
        landing = self.landing[step]
        return landing.at[lax.rem(c, landing.shape[0])]

    def copies(self, step, c, halves=(0, 1)):
        place = self.place
        result = []
        for h, way, hop in WAYS:
            if h not in halves:
                continue
            part = self.part.at[c, h]
            p, q = place.axes(h)
            if step == 0:
                src = part.at[pl.ds(ring(q, 2) * SIDE + 2 * way, 2)]
                to = place.at(h, p, ring(q, hop))
            elif step == 1:
                src = part.at[pl.ds(ring(q, hop) * SIDE, SIDE)]
                to = place.at(h, p, ring(q, hop))
            elif step == 2:
                src = part.at[q * SIDE + ring(p, 2), pl.ds(way * QUARTER, QUARTER)]
                to = place.at(h, ring(p, hop), q)
            else:
                src = part.at[q * SIDE + ring(p, hop)]
                to = place.at(h, ring(p, hop), q)
            result.append(
                copy_to(
                    src,
                    self.landed(step, c).at[h, way],
                    self.send.at[c, step, h, way],
                    self.recv.at[c, step, h, way],
                    to,
                )
            )
        return result

    def pass_on(self, step, c):
        for h in range(2):
            self.arrive(step, c, (h,))
            self.add(step, c, h)
            self.start(step + 1, c, (h,))

    def add(self, step, c, h):
        part = self.part.at[c, h]
        p, q = self.place.axes(h)
        landed = self.landed(step, c).at[h]
        if step == 0:
            for way, hop in ((0, 1), (1, -1)):
                for k in range(2):
                    add_into(part.at[ring(q, hop) * SIDE + 2 * way + k], landed.at[way, k])
        elif step == 1:
            for k in range(SIDE):
                dst = part.at[q * SIDE + k]
                dst[...] = (
                    dst[...].astype(F32) + landed[0, k].astype(F32) + landed[1, k].astype(F32)
                ).astype(BF)
        elif step == 2:
            for way, hop in ((0, 1), (1, -1)):
                add_into(
                    part.at[q * SIDE + ring(p, hop), pl.ds(way * QUARTER, QUARTER)],
                    landed.at[way],
                )

    def total(self, c):
        halves = []
        for h in range(2):
            p, q = self.place.axes(h)
            landed = self.landed(3, c).at[h]
            halves.append(
                self.part[c, h, q * SIDE + p].astype(F32)
                + landed[0].astype(F32)
                + landed[1].astype(F32)
            )
        return jnp.concatenate(halves, axis=0)


class Spreader(Exchange):
    def __init__(self, place, part, send, recv, halves=None):
        self.place, self.part, self.send, self.recv = place, part, send, recv
        self.halves = halves or {}

    def copies(self, step, c, halves=(0, 1)):
        place = self.place
        result = []
        for h, way, hop in WAYS:
            if h not in halves or h not in self.halves.get(c, (0, 1)):
                continue
            part = self.part.at[c, h]
            p, q = place.axes(h)
            if step == 0:
                ref = part.at[q * SIDE + p]
                to = place.at(h, ring(p, hop), q)
            elif step == 1:
                ref = part.at[q * SIDE + ring(p, -hop), pl.ds(way * QUARTER, QUARTER)]
                to = place.at(h, ring(p, hop), q)
            elif step == 2:
                ref = part.at[pl.ds(q * SIDE, SIDE)]
                to = place.at(h, p, ring(q, hop))
            else:
                ref = part.at[pl.ds(ring(q, -hop) * SIDE + 2 * way, 2)]
                to = place.at(h, p, ring(q, hop))
            result.append(
                copy_to(
                    ref,
                    ref,
                    self.send.at[c, step, h, way],
                    self.recv.at[c, step, h, way],
                    to,
                )
            )
        return result


def greet_plane(place, barrier):
    for hop in (1, -1):
        for rank in (
            place.at(0, ring(place.x, hop), place.z),
            place.at(0, place.x, ring(place.z, hop)),
        ):
            pl.semaphore_signal(
                barrier, inc=1, device_id={"tensor": rank}, device_id_type=pl.DeviceIdType.MESH
            )


def flipped(group, bits):
    b = (lax.rem(group, 2), lax.rem(group // 2, 2), group // 4)
    return sum((b[k] + bits[k] - 2 * b[k] * bits[k]) * (1 << k) for k in range(3))


PARTNERS = (0, 1, 4, 5, 2, 6, 3, 7)
WHOLE = (1, 4, 5)
SPREAD = (2, 3, 6, 7)
SPREAD_HALVES = {2: (0, 1), 3: (0, 1), 6: (1,), 7: (0,)}
TURNS = CHUNKS // 2
SLOTS = 4


def chunk_bits(c):
    if isinstance(c, int):
        return tuple((PARTNERS[c] >> k) & 1 for k in range(3))
    return tuple(
        sum(jnp.where(c == i, 1, 0) for i in range(CHUNKS) if (PARTNERS[i] >> k) & 1)
        for k in range(3)
    )


def to_group(src, dst, send, recv, group):
    return pltpu.make_async_remote_copy(
        src_ref=src,
        dst_ref=dst,
        send_sem=send,
        recv_sem=recv,
        device_id={"group": group},
        device_id_type=pl.DeviceIdType.MESH,
    )


def layer_kernel(
    numerator_ref,
    marks_ref,
    ids_ref,
    route_ref,
    residual_ref,
    out_weight,
    expert_gate,
    expert_up,
    expert_down,
    dense_gate,
    dense_up,
    dense_down,
    mixed_ref,
    other,
    other_marks,
    near,
    state_ref,
    part,
    full,
    ready,
    r1,
    r2,
    r3,
    r4,
    w_in,
    w_down,
    outgoing,
    side_out,
    side_in,
    returned,
    own_pos,
    acc,
    hidden,
    mixing,
    load_sem,
    first_sem,
    swap_send,
    swap_recv,
    state_send,
    state_recv,
    full_send,
    full_recv,
    spread_send,
    spread_recv,
    sum_send,
    sum_recv,
    go_send,
    go_recv,
    side_send,
    side_recv,
    back_send,
    back_recv,
):
    place = Place()
    group = lax.axis_index("group")
    is_odd = lax.rem(place.rank, 2)
    hidden_size = w_in.shape[0] // 4
    rows = ids_ref.shape[1]
    row_blocks = rows // CHUNK
    width = 16 * SLICE

    head_part = lax.rem(place.rank, 2)
    skipped = pl.multiple_of(head_part * SHARED, SHARED)
    fetch_out = pltpu.make_async_copy(
        out_weight, w_in.at[pl.ds(skipped, SLICE)], first_sem.at[0]
    )
    first_column = pl.multiple_of((place.rank // 2) * 2 * SLICE, 2 * SLICE)
    fetch_near = pltpu.make_async_copy(
        residual_ref.at[:, pl.ds(first_column, 2 * SLICE)], near, first_sem.at[1]
    )
    loads = [
        pltpu.make_async_copy(
            ref, w_in.at[pl.ds(k * hidden_size, hidden_size)], load_sem.at[k]
        )
        for k, ref in enumerate((expert_gate.at[0], expert_up.at[0], dense_gate, dense_up))
    ] + [
        pltpu.make_async_copy(
            ref, w_down.at[pl.ds(k * hidden_size, hidden_size)], load_sem.at[4 + k]
        )
        for k, ref in enumerate((expert_down.at[0], dense_down))
    ]
    fetch_out.start()
    fetch_near.start()
    for load in loads[4:]:
        load.start()
    w_in[pl.ds(pl.multiple_of((1 - head_part) * SLICE, SHARED), SHARED), :] = jnp.zeros(
        (SHARED, width), BF
    )

    barrier = pltpu.get_barrier_semaphore()
    greet_plane(place, barrier)
    for c in range(1, CHUNKS):
        pl.semaphore_signal(
            barrier,
            inc=1,
            device_id={"group": flipped(group, chunk_bits(c))},
            device_id_type=pl.DeviceIdType.MESH,
        )
    pl.semaphore_wait(barrier, 4 + CHUNKS - 1)

    mate = place.rank + 1 - 2 * head_part
    theirs = pl.multiple_of((1 - head_part) * 3 * LANES, LANES)
    mine = head_part * 3 * LANES

    swaps = [copy_to(marks_ref, other_marks, swap_send.at[0], swap_recv.at[0], mate)] + [
        copy_to(
            numerator_ref.at[pl.ds(b * CHUNK, CHUNK), pl.ds(theirs, 4 * LANES)],
            other.at[pl.ds(b * CHUNK, CHUNK)],
            swap_send.at[1 + b],
            swap_recv.at[1 + b],
            mate,
        )
        for b in range(row_blocks)
    ]
    for copy in swaps:
        copy.start()

    gatherer = Spreader(place, full, full_send, full_recv)
    spreader = Spreader(place, part, spread_send, spread_recv, SPREAD_HALVES)
    summer = Summer(place, part, (r1, r2, r3, r4), sum_send, sum_recv)
    state_summer = Summer(place, ready, (r1, r2, r3, r4), state_send, state_recv)

    line = lax.broadcasted_iota(jnp.int32, (rows, rows), 0)
    column = lax.broadcasted_iota(jnp.int32, (rows, rows), 1)

    def upright(row):
        return jnp.sum(jnp.where(line == column, row, 0.0), axis=1, keepdims=True)

    flat_ids = [ids_ref[k : k + 1, :].astype(F32) for k in range(2)]
    ids = [upright(row) for row in flat_ids]
    route = [upright(route_ref[k : k + 1, :]) for k in range(2)]
    partners = [flipped(group, chunk_bits(c)).astype(F32) for c in range(CHUNKS)]
    lane = lax.broadcasted_iota(jnp.int32, (rows, LANES), 1)
    partner_of_lane = jnp.full((rows, LANES), -1.0, F32)
    sub = lax.broadcasted_iota(jnp.int32, (CHUNKS, rows), 0)
    partner_of_sub = jnp.zeros((CHUNKS, rows), F32)
    for c in range(CHUNKS):
        partner_of_lane = jnp.where(lane == c, partners[c], partner_of_lane)
        partner_of_sub = jnp.where(sub == c, partners[c], partner_of_sub)
    first_choice, second_choice = [choice == partner_of_lane for choice in ids]
    named = jnp.where(first_choice | second_choice, 1.0, 0.0)
    before = jnp.where(column < line, 1.0, 0.0).astype(BF)
    place_in = jnp.dot(before, named.astype(BF), preferred_element_type=F32)
    positions = jnp.where(named > 0.5, place_in, -1.0)
    own_pos[...] = positions
    flat_named = jnp.where(
        (flat_ids[0] == partner_of_sub) | (flat_ids[1] == partner_of_sub), 1.0, 0.0
    )
    after = jnp.where(line < column, 1.0, 0.0).astype(BF)
    flat_place = jnp.dot(flat_named.astype(BF), after, preferred_element_type=F32)
    flat_pos = jnp.where(flat_named > 0.5, flat_place, -1.0)
    weight = jnp.where(first_choice, route[0], 0.0) + jnp.where(second_choice, route[1], 0.0)
    dense_here = jnp.where(first_choice, 1.0, 0.0)
    slot_line = lax.broadcasted_iota(jnp.int32, (CHUNK, rows), 0).astype(F32)
    slot_lane = lax.broadcasted_iota(jnp.int32, (rows, CHUNK), 1).astype(F32)
    sides = lax.broadcasted_iota(jnp.int32, (8, LANES), 0)

    def pick(c):
        return jnp.where(flat_pos[c : c + 1, :] == slot_line, 1.0, 0.0).astype(BF)

    def partner(c):
        return flipped(group, chunk_bits(c))

    def side(c):
        return to_group(
            side_out.at[c], side_in.at[c], side_send.at[c], side_recv.at[c], partner(c)
        )

    def slices(c):
        return [
            to_group(
                outgoing.at[SPREAD.index(c), pl.ds(h * HALF, HALF)],
                part.at[c, h, spot(h, place.z, place.x)],
                go_send.at[c, h],
                go_recv.at[c, h],
                partner(c),
            )
            for h in SPREAD_HALVES[c]
        ]

    def whole(c):
        slot = 1 if c == 5 else 0
        return to_group(
            ready.at[slot], part.at[c], go_send.at[c, 0], go_recv.at[c, 0], partner(c)
        )

    def other_half(c):
        h = 1 - SPREAD_HALVES[c][0]
        return to_group(
            ready.at[c - 6, h], part.at[c, h], go_send.at[c, h], go_recv.at[c, h], partner(c)
        )

    swaps[0].wait_recv()
    top = jnp.maximum(marks_ref[0:8, :], other_marks[0:8, :])
    keep = jnp.exp(marks_ref[0:8, :] - top)
    take = jnp.exp(other_marks[0:8, :] - top)
    below = 1.0 / (marks_ref[8:16, :] * keep + other_marks[8:16, :] * take)
    scales = jnp.concatenate(
        [keep * below, take * below, jnp.zeros((LANES - 16, rows), F32)], axis=0
    ).T
    low = lanes_low(CHUNK)
    for b in range(row_blocks):
        swaps[1 + b].wait_recv()
        block_rows = slice(b * CHUNK, (b + 1) * CHUNK)
        joined = []
        for k in range(4):
            factors = [
                jnp.where(
                    head_part == 1,
                    scales[block_rows, at + k + 3 : at + k + 4],
                    scales[block_rows, at + k : at + k + 1],
                )
                for at in (0, 8)
            ]
            here = numerator_ref[
                block_rows, pl.ds(pl.multiple_of(mine + k * LANES, LANES), LANES)
            ].astype(F32)
            there = other[block_rows, k * LANES : (k + 1) * LANES].astype(F32)
            tile = here * factors[0] + there * factors[1]
            if k == 0:
                tile = jnp.where(low & (head_part == 1), 0.0, tile)
            if k == 3:
                tile = jnp.where(low | (head_part == 1), tile, 0.0)
            joined.append(tile.astype(BF))
        attention = jnp.concatenate(joined, axis=1)
        if b == 0:
            fetch_out.wait()

        @pl.loop(0, SIDE)
        def _(z):
            columns = pl.ds(pl.multiple_of(z * 4 * SLICE, 4 * SLICE), 4 * SLICE)
            block = jnp.dot(
                attention, w_in[: SLICE + SHARED, columns], preferred_element_type=F32
            )
            store_quarter(ready.at[b], z, block)

        state_summer.start(0, b)
    for load in loads[:4]:
        load.start()
    for b in range(row_blocks):
        state_summer.pass_on(0, b)
    for c in range(CHUNKS):
        at_slot = positions[:, c : c + 1] == slot_lane
        w_row = jnp.sum(jnp.where(at_slot, weight[:, c : c + 1], 0.0), axis=0, keepdims=True)
        d_row = jnp.sum(jnp.where(at_slot, dense_here[:, c : c + 1], 0.0), axis=0, keepdims=True)
        both = jnp.where(sides == 0, w_row, jnp.where(sides == 1, d_row, 0.0))
        if c == 0:
            side_in[0] = both
        else:
            side_out[c] = both
            side(c).start()
    for step in range(2, 4):
        for b in range(row_blocks):
            state_summer.pass_on(step - 1, b)
    fetch_near.wait()
    for b in range(row_blocks):
        block_rows = slice(b * CHUNK, (b + 1) * CHUNK)
        even = [near[block_rows, k * LANES : (k + 1) * LANES].astype(F32) for k in range(4)]
        odd = [near[block_rows, (k + 4) * LANES : (k + 5) * LANES].astype(F32) for k in range(3)]
        whole_tiles = [jnp.where(is_odd == 1, odd[k], even[k]) for k in range(3)]
        store_own(state_ref.at[b], jnp.concatenate(whole_tiles + [even[3]], axis=1), is_odd)
        state_summer.arrive(3, b)
        state = (state_ref[b].astype(F32) + state_summer.total(b)).astype(BF)
        state_ref[b] = state
        for h in range(2):
            full[b, h, spot(h, place.z, place.x)] = state[h * HALF : (h + 1) * HALF]
        gatherer.start(0, b)
    for b in range(row_blocks):
        mixing[b * CHUNK : (b + 1) * CHUNK, :] = natural_own(state_ref.at[b], is_odd)

    for c in SPREAD:
        chosen = jnp.dot(pick(c), mixing[...].astype(BF), preferred_element_type=F32)
        store_own(outgoing.at[SPREAD.index(c)], chosen, is_odd)
        for copy in slices(c):
            copy.start()
    for b in range(row_blocks):
        for h in range(2):
            gatherer.arrive(0, b, (h,))
            gatherer.start(1, b, (h,))
    for b in range(row_blocks):
        for h in range(2):
            gatherer.arrive(1, b, (h,))
            gatherer.start(2, b, (h,))
    for c in SPREAD[:2]:
        for copy in slices(c):
            copy.wait_recv()
        spreader.start(0, c)
    for b in range(row_blocks):
        for h in range(2):
            gatherer.arrive(2, b, (h,))
            gatherer.start(3, b, (h,))
    for c in SPREAD[:2]:
        spreader.arrive(0, c)
        spreader.start(1, c)
    for c in SPREAD[:2]:
        spreader.arrive(1, c)
        spreader.start(2, c)
    for b in range(row_blocks):
        gatherer.arrive(3, b)

    def choose_whole(c, target, halves=(0, 1)):
        chosen_rows = pick(c)

        @pl.loop(0, SIDE)
        def _(z):
            source = jnp.concatenate(
                [load_quarter(full.at[b], z) for b in range(row_blocks)], axis=0
            )
            store_quarter(
                target, z, jnp.dot(chosen_rows, source, preferred_element_type=F32), halves
            )

    for b in range(row_blocks):
        state_summer.sent(b)
    choose_whole(1, ready.at[0])
    whole(1).start()
    choose_whole(5, ready.at[1])
    whole(5).start()
    whole(1).wait_send()
    choose_whole(4, ready.at[0])
    whole(4).start()
    choose_whole(0, part.at[0])

    def back(c):
        return [
            to_group(
                ready.at[0, 1, 2 * c + h],
                returned.at[c, pl.ds(h * HALF, HALF)],
                back_send.at[c, h],
                back_recv.at[c, h],
                partner(c),
            )
            for h in range(2)
        ]

    def finish_sum(c):
        summer.arrive(3, c)
        total = summer.total(c).astype(BF)

        @pl.when(c == 0)
        def _():
            returned[0] = total

        @pl.when(c > 0)
        def _():
            for h, copy in enumerate(back(c)):
                ready[0, 1, 2 * c + h] = total[h * HALF : (h + 1) * HALF]
                copy.start()

    def mix(c):
        @pl.when(c > 0)
        def _():
            for copy in back(c):
                copy.wait_recv()

        position = jnp.sum(jnp.where(lane == c, own_pos[...], 0.0), axis=1, keepdims=True)
        at_slot = jnp.where(position == slot_lane, 1.0, 0.0).astype(BF)
        block = natural_own(returned.at[c], is_odd).astype(BF)
        mixing[...] += jnp.dot(at_slot, block, preferred_element_type=F32)

    def spread(step, chunks):
        for c in chunks:
            if step == 0:
                for copy in slices(c):
                    copy.wait_recv()
            else:
                spreader.arrive(step - 1, c)
            if step < 4:
                spreader.start(step, c)

    def compute(j):
        chunks = [part.at[2 * j + i] for i in range(2)]
        acc[...] = jnp.zeros_like(acc)

        def gather_products(z, squares):
            block = jnp.concatenate([load_quarter(chunk, z) for chunk in chunks], axis=0)
            deep = pl.ds(pl.multiple_of(z * 4 * SLICE, 4 * SLICE), 4 * SLICE)
            acc[...] += lax.dot_general(
                block, w_in[:, deep], (((1,), (1,)), ((), ())), preferred_element_type=F32
            )
            for k in range(14):
                wide = block[:, k * LANES : (k + 1) * LANES].astype(F32)
                squares = squares + wide * wide
            return squares

        squares = lax.fori_loop(0, SIDE, gather_products, jnp.zeros((2 * CHUNK, LANES), F32))
        scale = lax.rsqrt(jnp.sum(squares, axis=1, keepdims=True) / width + 1e-05)
        diagonal = lax.broadcasted_iota(jnp.int32, (CHUNK, CHUNK), 0) == lax.broadcasted_iota(
            jnp.int32, (CHUNK, CHUNK), 1
        )
        for k in range(2):
            factor = jnp.concatenate(
                [
                    jnp.sum(
                        jnp.where(diagonal, side_in[2 * j + i, k : k + 1, :], 0.0),
                        axis=1,
                        keepdims=True,
                    )
                    for i in range(2)
                ],
                axis=0,
            )
            gate, up = [
                acc[:, (2 * k + i) * hidden_size : (2 * k + i + 1) * hidden_size] * scale
                for i in range(2)
            ]
            inner = gate / (1.0 + jnp.exp(-gate)) * up * factor
            hidden[:, k * hidden_size : (k + 1) * hidden_size] = inner.astype(BF)

        @pl.when(j == 0)
        def _():
            spread(3, SPREAD[:2])
            spread(1, SPREAD[2:])

        for chosen in (SPREAD[:2], SPREAD[2:]):

            @pl.when(2 * j == chosen[0])
            def _():
                for c in chosen:
                    spreader.sent(c)


        @pl.loop(0, SIDE)
        def _(step):
            z = ring(place.z, step + 2 - SIDE)
            columns = pl.ds(pl.multiple_of(z * 4 * SLICE, 4 * SLICE), 4 * SLICE)
            block = jnp.dot(hidden[...], w_down[:, columns], preferred_element_type=F32)
            for i in range(2):
                store_quarter(chunks[i], z, block[i * CHUNK : (i + 1) * CHUNK])

            @pl.when(step == 0)
            def _():
                for i in range(2):
                    summer.start(0, 2 * j + i, (0,))

    def turn(it, carry):
        def stage(lag, body):
            j = it - lag

            @pl.when((j >= 0) & (j < TURNS))
            def _():
                for i in range(2):
                    body(2 * j + i)

        def add(step):
            def body(c):
                summer.pass_on(step - 1, c)

            return body

        stage(5, mix)
        stage(4, finish_sum)
        stage(3, add(3))
        stage(2, add(2))
        stage(1, add(1))

        @pl.when(it == 0)
        def _():
            spread(0, SPREAD[2:])
            whole(1).wait_recv()
            side(1).wait_recv()
            for load in loads:
                load.wait()

        @pl.when(it == 1)
        def _():
            spread(2, SPREAD[2:])
            spread(4, SPREAD[:2])
            for c in SPREAD[:2]:
                side(c).wait_recv()

        @pl.when(it == 2)
        def _():
            for c in WHOLE[1:]:
                whole(c).wait_send()
            for c in SPREAD[2:]:
                choose_whole(c, ready.at[c - 6], (1 - SPREAD_HALVES[c][0],))
                other_half(c).start()
            for c in WHOLE[1:]:
                whole(c).wait_recv()
                side(c).wait_recv()

        @pl.when(it == 3)
        def _():
            spread(4, SPREAD[2:])
            for c in SPREAD[2:]:
                other_half(c).wait_recv()
                side(c).wait_recv()

        @pl.when(it < TURNS)
        def _():
            compute(it)
            for i in range(2):
                summer.start(0, 2 * it + i, (1,))

        @pl.when(it == 1)
        def _():
            spread(3, SPREAD[2:])

        return carry

    lax.fori_loop(0, TURNS + 5, turn, 0)

    total = mixing[...].T
    for_odd = jnp.concatenate([total[3 * LANES + SHARED :], total[: 3 * LANES]], axis=0)
    mixed_ref[...] = jnp.where(is_odd == 1, for_odd, total[:SLICE]).astype(BF)

    @pl.loop(0, CHUNKS)
    def _(c):
        summer.sent(c)

    for copy in swaps:
        copy.wait_send()
    for b in range(row_blocks):
        gatherer.sent(b)
    for c in range(1, CHUNKS):
        side(c).wait_send()
        for copy in back(c):
            copy.wait_send()
    for c in SPREAD:
        for copy in slices(c):
            copy.wait_send()
    for c in SPREAD[2:]:
        other_half(c).wait_send()


def finish_layer(
    numerator,
    marks,
    residual,
    out_weight,
    expert_ids,
    route_weights,
    expert_gate,
    expert_up,
    expert_down,
    dense_gate,
    dense_up,
    dense_down,
):
    rows = expert_ids.shape[0]
    width, hidden_size = dense_gate.shape
    vmem = pl.BlockSpec(memory_space=pltpu.VMEM)
    hbm = pl.BlockSpec(memory_space=pl.ANY)
    row_blocks = rows // CHUNK
    return pl.pallas_call(
        layer_kernel,
        out_shape=jax.ShapeDtypeStruct((SLICE, rows), BF),
        in_specs=[vmem] * 4 + [hbm] * 8,
        out_specs=vmem,
        scratch_shapes=[
            pltpu.VMEM((rows, 4 * LANES), BF),
            pltpu.VMEM((16, rows), F32),
            pltpu.VMEM((rows, 2 * SLICE), BF),
            pltpu.VMEM((row_blocks, SLICE, LANES), BF),
            pltpu.VMEM((CHUNKS, 2, 16, HALF, LANES), BF),
            pltpu.VMEM((row_blocks, 2, 16, HALF, LANES), BF),
            pltpu.VMEM((2, 2, 16, HALF, LANES), BF),
            pltpu.VMEM((SLOTS, 2, 2, 2, HALF, LANES), BF),
            pltpu.VMEM((SLOTS, 2, 2, SIDE, HALF, LANES), BF),
            pltpu.VMEM((SLOTS, 2, 2, QUARTER, LANES), BF),
            pltpu.VMEM((SLOTS, 2, 2, HALF, LANES), BF),
            pltpu.VMEM((4 * hidden_size, width), BF),
            pltpu.VMEM((2 * hidden_size, width), BF),
            pltpu.VMEM((len(SPREAD), SLICE, LANES), BF),
            pltpu.VMEM((CHUNKS, 8, LANES), F32),
            pltpu.VMEM((CHUNKS, 8, LANES), F32),
            pltpu.VMEM((CHUNKS, SLICE, LANES), BF),
            pltpu.VMEM((rows, LANES), F32),
            pltpu.VMEM((2 * CHUNK, 4 * hidden_size), F32),
            pltpu.VMEM((2 * CHUNK, 2 * hidden_size), BF),
            pltpu.VMEM((rows, 4 * LANES), F32),
            pltpu.SemaphoreType.DMA((6,)),
            pltpu.SemaphoreType.DMA((2,)),
            pltpu.SemaphoreType.DMA((1 + row_blocks,)),
            pltpu.SemaphoreType.DMA((1 + row_blocks,)),
        ]
        + [pltpu.SemaphoreType.DMA((row_blocks, 4, 2, 2))] * 4
        + [pltpu.SemaphoreType.DMA((CHUNKS, 4, 2, 2))] * 4
        + [pltpu.SemaphoreType.DMA((CHUNKS, 2))] * 2
        + [pltpu.SemaphoreType.DMA((CHUNKS,))] * 2
        + [pltpu.SemaphoreType.DMA((CHUNKS, 2))] * 2,
        compiler_params=pltpu.CompilerParams(
            collective_id=1, has_side_effects=True, vmem_limit_bytes=64 * 1024 * 1024 - 65536
        ),
        name="layer",
    )(
        numerator,
        marks,
        expert_ids.T,
        route_weights.T,
        residual,
        out_weight,
        jnp.swapaxes(expert_gate, 1, 2),
        jnp.swapaxes(expert_up, 1, 2),
        expert_down,
        dense_gate.T,
        dense_up.T,
        dense_down,
    ).T


def attend(queries, new_kv, kv_cache, lengths):
    row_count = queries.shape[0]
    rank = lax.axis_index("tensor")
    my_head, my_part = rank // 2, rank % 2
    head_size = new_kv.shape[3]
    span = kv_cache.shape[2]
    heads = jnp.arange(queries.shape[1], dtype=jnp.int32)[None, :, None] == my_head
    rows = jnp.sum(jnp.where(heads, queries, 0).astype(F32), axis=1).astype(BF)
    rows = rows.reshape(row_count, -1, head_size)
    new_key = lax.dynamic_index_in_dim(new_kv[0], my_head, 1, keepdims=False)
    new_value = lax.dynamic_index_in_dim(new_kv[1], my_head, 1, keepdims=False)
    scale = 1.0 / math.sqrt(head_size)
    scores = jnp.einsum("tgd,tpd->tgp", rows, kv_cache[0], preferred_element_type=F32) * scale
    own = jnp.einsum("tgd,td->tg", rows, new_key, preferred_element_type=F32) * scale
    position = my_part * span + jnp.arange(span, dtype=jnp.int32)
    usable = position[None, None, :] < lengths[:, None, None]
    masked = jnp.where(usable, scores, -1e30)
    highest = jnp.maximum(jnp.max(masked, axis=-1), own)
    weights = jnp.where(usable, jnp.exp(masked - highest[..., None]), 0.0).astype(BF)
    own_weight = jnp.exp(own - highest)
    leading = (my_part == 0).astype(F32)
    numerator = jnp.einsum("tgp,tpd->tgd", weights, kv_cache[1], preferred_element_type=F32)
    numerator = numerator + leading * own_weight[..., None] * new_value.astype(F32)[:, None, :]
    denominator = jnp.sum(weights.astype(F32), axis=-1) + leading * own_weight
    flat = numerator.astype(BF).reshape(row_count, -1)
    marks = jnp.concatenate(
        [
            jnp.pad(highest.T, ((0, 1), (0, 0))),
            jnp.pad(denominator.T, ((0, 1), (0, 0)), constant_values=1.0),
        ]
    )
    return flat, marks


def shards(
    residual,
    queries,
    new_kv,
    kv_cache,
    lengths,
    out_weight,
    dense_gate,
    dense_up,
    dense_down,
    expert_ids,
    route_weights,
    expert_gate,
    expert_up,
    expert_down,
):
    numerator, marks = attend(queries, new_kv, kv_cache, lengths)
    return finish_layer(
        numerator,
        marks,
        residual,
        out_weight,
        expert_ids,
        route_weights,
        expert_gate,
        expert_up,
        expert_down,
        dense_gate,
        dense_up,
        dense_down,
    )


def solution(mesh):
    placed = (
        P("group", None),
        P("group", None, None),
        P(None, "group", None, None),
        P(None, "group", "tensor", None),
        P("group"),
        P("tensor", None),
        P(None, "tensor"),
        P(None, "tensor"),
        P("tensor", None),
        P("group", None),
        P("group", None),
        P("group", None, "tensor"),
        P("group", None, "tensor"),
        P("group", "tensor", None),
    )
    return jax.shard_map(
        shards, mesh=mesh, in_specs=placed, out_specs=P("group", "tensor"), check_vma=False
    )
```

```python
import functools
import math

import jax
import jax.numpy as jnp
from jax import lax
from jax.experimental import pallas as pl
from jax.experimental.pallas import tpu as pltpu
from jax.sharding import PartitionSpec as P

BF = jnp.bfloat16
F32 = jnp.float32
SIDE = 4
LANES = 128
CHUNK = 128
SLICE = 448
HALF = SLICE // 2
SHARED = 64
CHUNKS = 8


def ring(value, step):
    return lax.rem(value + step + SIDE, SIDE)


class Place:
    def __init__(self):
        rank = lax.axis_index("tensor")
        self.rank = rank
        self.z = rank // SIDE
        self.x = lax.rem(rank, SIDE)

    def axes(self, half):
        return (self.x, self.z) if half == 0 else (self.z, self.x)

    def at(self, half, p, q):
        return q * SIDE + p if half == 0 else p * SIDE + q


def spot(half, z, x):
    return z * SIDE + x if half == 0 else x * SIDE + z


def split_rows(low, high):
    pieces = []
    if low < HALF:
        pieces.append((0, low, min(high, HALF), 0))
    if high > HALF:
        start = max(low, HALF)
        pieces.append((1, start - HALF, high - HALF, start - low))
    return pieces


def read_rows(part, z, x, low, high):
    pieces = [part[h, spot(h, z, x), a:b, :] for h, a, b, _ in split_rows(low, high)]
    return pieces[0] if len(pieces) == 1 else jnp.concatenate(pieces, axis=0)


def write_rows(part, z, x, low, value, halves=(0, 1)):
    for h, a, b, offset in split_rows(low, low + value.shape[0]):
        if h in halves:
            part[h, spot(h, z, x), a:b, :] = value[offset : offset + b - a]


def copy_to(src, dst, send, recv, rank):
    return pltpu.make_async_remote_copy(
        src_ref=src,
        dst_ref=dst,
        send_sem=send,
        recv_sem=recv,
        device_id={"tensor": rank},
        device_id_type=pl.DeviceIdType.MESH,
    )


def lanes_low(rows):
    return lax.broadcasted_iota(jnp.int32, (rows, LANES), 1) < SHARED


def turned(block):
    return pltpu.roll(block, SHARED, 1)


def unfold_pair(even_half, odd_half):
    low = lanes_low(SHARED)
    e, o = even_half.astype(F32), odd_half.astype(F32)
    top = jnp.where(low, e, o)
    bottom = turned(jnp.where(low, o, e))
    return jnp.concatenate([top, bottom], axis=0).astype(BF)


def fold_pair(tile):
    low = lanes_low(SHARED)
    top, bottom = tile[:SHARED], turned(tile[SHARED:])
    return jnp.where(low, top, bottom).astype(BF), jnp.where(low, bottom, top).astype(BF)


def unfold_own(half):
    half = half.astype(F32)
    return jnp.concatenate([half, turned(half)], axis=0)


def fold_own(tile, is_odd):
    low = lanes_low(SHARED).astype(jnp.int32) != is_odd
    top, bottom = tile[:SHARED], turned(tile[SHARED:])
    return jnp.where(low, top, bottom)


def natural_own(ref, is_odd):
    first = pl.multiple_of(is_odd * SHARED, SHARED)
    half = pl.multiple_of((1 - is_odd) * (SLICE - SHARED), SHARED)
    tiles = [ref[pl.ds(first + k * LANES, LANES), :].astype(F32) for k in range(3)]
    return jnp.concatenate(tiles + [unfold_own(ref[pl.ds(half, SHARED), :])], axis=1)


def store_own(ref, block, is_odd):
    first = pl.multiple_of(is_odd * SHARED, SHARED)
    half = pl.multiple_of((1 - is_odd) * (SLICE - SHARED), SHARED)
    for k in range(3):
        ref[pl.ds(first + k * LANES, LANES), :] = block[:, k * LANES : (k + 1) * LANES].astype(BF)
    ref[pl.ds(half, SHARED), :] = fold_own(block[:, 3 * LANES :], is_odd).astype(BF)


def store_quarter(part, z, block, halves=(0, 1)):
    for pair in range(2):
        e, o = 2 * pair, 2 * pair + 1
        tiles = [
            block[:, (pair * 7 + k) * LANES : (pair * 7 + k + 1) * LANES] for k in range(7)
        ]
        even_half, odd_half = fold_pair(tiles[3])
        for k in range(3):
            write_rows(part, z, e, k * LANES, tiles[k].astype(BF), halves)
            write_rows(part, z, o, SHARED + k * LANES, tiles[4 + k].astype(BF), halves)
        write_rows(part, z, e, SLICE - SHARED, even_half, halves)
        write_rows(part, z, o, 0, odd_half, halves)


def load_quarter(part, z):
    blocks = []
    for pair in range(2):
        e, o = 2 * pair, 2 * pair + 1
        blocks += [read_rows(part, z, e, k * LANES, (k + 1) * LANES) for k in range(3)]
        blocks.append(
            unfold_pair(
                read_rows(part, z, e, SLICE - SHARED, SLICE), read_rows(part, z, o, 0, SHARED)
            )
        )
        blocks += [
            read_rows(part, z, o, SHARED + k * LANES, SHARED + (k + 1) * LANES) for k in range(3)
        ]
    return jnp.concatenate(blocks, axis=1)


def add_into(dst, other):
    dst[...] = (dst[...].astype(F32) + other[...].astype(F32)).astype(BF)


class Exchange:
    def start(self, step, c, halves=(0, 1)):
        for copy in self.copies(step, c, halves):
            copy.start()

    def arrive(self, step, c, halves=(0, 1)):
        for copy in self.copies(step, c, halves):
            copy.wait_recv()

    def sent(self, c):
        for step in range(4):
            for copy in self.copies(step, c):
                copy.wait_send()


WAYS = ((0, 0, 1), (0, 1, -1), (1, 0, 1), (1, 1, -1))
QUARTER = HALF // 2


class Summer(Exchange):
    def __init__(self, place, part, landing, send, recv):
        self.place, self.part, self.landing = place, part, landing
        self.send, self.recv = send, recv

    def landed(self, step, c):
        landing = self.landing[step]
        return landing.at[lax.rem(c, landing.shape[0])]

    def copies(self, step, c, halves=(0, 1)):
        place = self.place
        result = []
        for h, way, hop in WAYS:
            if h not in halves:
                continue
            part = self.part.at[c, h]
            p, q = place.axes(h)
            if step == 0:
                src = part.at[pl.ds(ring(q, 2) * SIDE + 2 * way, 2)]
                to = place.at(h, p, ring(q, hop))
            elif step == 1:
                src = part.at[pl.ds(ring(q, hop) * SIDE, SIDE)]
                to = place.at(h, p, ring(q, hop))
            elif step == 2:
                src = part.at[q * SIDE + ring(p, 2), pl.ds(way * QUARTER, QUARTER)]
                to = place.at(h, ring(p, hop), q)
            else:
                src = part.at[q * SIDE + ring(p, hop)]
                to = place.at(h, ring(p, hop), q)
            result.append(
                copy_to(
                    src,
                    self.landed(step, c).at[h, way],
                    self.send.at[c, step, h, way],
                    self.recv.at[c, step, h, way],
                    to,
                )
            )
        return result

    def pass_on(self, step, c):
        for h in range(2):
            self.arrive(step, c, (h,))
            self.add(step, c, h)
            self.start(step + 1, c, (h,))

    def add(self, step, c, h):
        part = self.part.at[c, h]
        p, q = self.place.axes(h)
        landed = self.landed(step, c).at[h]
        if step == 0:
            for way, hop in ((0, 1), (1, -1)):
                for k in range(2):
                    add_into(part.at[ring(q, hop) * SIDE + 2 * way + k], landed.at[way, k])
        elif step == 1:
            for k in range(SIDE):
                dst = part.at[q * SIDE + k]
                dst[...] = (
                    dst[...].astype(F32) + landed[0, k].astype(F32) + landed[1, k].astype(F32)
                ).astype(BF)
        elif step == 2:
            for way, hop in ((0, 1), (1, -1)):
                add_into(
                    part.at[q * SIDE + ring(p, hop), pl.ds(way * QUARTER, QUARTER)],
                    landed.at[way],
                )

    def total(self, c):
        halves = []
        for h in range(2):
            p, q = self.place.axes(h)
            landed = self.landed(3, c).at[h]
            halves.append(
                self.part[c, h, q * SIDE + p].astype(F32)
                + landed[0].astype(F32)
                + landed[1].astype(F32)
            )
        return jnp.concatenate(halves, axis=0)


class Spreader(Exchange):
    def __init__(self, place, part, send, recv):
        self.place, self.part, self.send, self.recv = place, part, send, recv

    def copies(self, step, c, halves=(0, 1)):
        place = self.place
        result = []
        for h, way, hop in WAYS:
            if h not in halves:
                continue
            part = self.part.at[c, h]
            p, q = place.axes(h)
            if step == 0:
                ref = part.at[q * SIDE + p]
                to = place.at(h, ring(p, hop), q)
            elif step == 1:
                ref = part.at[q * SIDE + ring(p, -hop), pl.ds(way * QUARTER, QUARTER)]
                to = place.at(h, ring(p, hop), q)
            elif step == 2:
                ref = part.at[pl.ds(q * SIDE, SIDE)]
                to = place.at(h, p, ring(q, hop))
            else:
                ref = part.at[pl.ds(ring(q, -hop) * SIDE + 2 * way, 2)]
                to = place.at(h, p, ring(q, hop))
            result.append(
                copy_to(
                    ref,
                    ref,
                    self.send.at[c, step, h, way],
                    self.recv.at[c, step, h, way],
                    to,
                )
            )
        return result


def greet_plane(place, barrier):
    for hop in (1, -1):
        for rank in (
            place.at(0, ring(place.x, hop), place.z),
            place.at(0, place.x, ring(place.z, hop)),
        ):
            pl.semaphore_signal(
                barrier, inc=1, device_id={"tensor": rank}, device_id_type=pl.DeviceIdType.MESH
            )


def flipped(group, bits):
    b = (lax.rem(group, 2), lax.rem(group // 2, 2), group // 4)
    return sum((b[k] + bits[k] - 2 * b[k] * bits[k]) * (1 << k) for k in range(3))


PARTNERS = (0, 1, 3, 7, 4, 5, 2, 6)
WHOLE = (1, 6, 7)
SPREAD = (2, 3, 4, 5)
TURNS = CHUNKS // 2
SLOTS = 4


def chunk_bits(c):
    if isinstance(c, int):
        return tuple((PARTNERS[c] >> k) & 1 for k in range(3))
    return tuple(
        sum(jnp.where(c == i, 1, 0) for i in range(CHUNKS) if (PARTNERS[i] >> k) & 1)
        for k in range(3)
    )


def to_group(src, dst, send, recv, group):
    return pltpu.make_async_remote_copy(
        src_ref=src,
        dst_ref=dst,
        send_sem=send,
        recv_sem=recv,
        device_id={"group": group},
        device_id_type=pl.DeviceIdType.MESH,
    )


def layer_kernel(
    numerator_ref,
    marks_ref,
    ids_ref,
    route_ref,
    residual_ref,
    out_weight,
    expert_gate,
    expert_up,
    expert_down,
    dense_gate,
    dense_up,
    dense_down,
    mixed_ref,
    other,
    other_marks,
    near,
    state_ref,
    part,
    full,
    ready,
    r1,
    r2,
    r3,
    r4,
    w_in,
    w_down,
    outgoing,
    side_out,
    side_in,
    returned,
    own_pos,
    acc,
    hidden,
    mixing,
    load_sem,
    first_sem,
    swap_send,
    swap_recv,
    state_send,
    state_recv,
    full_send,
    full_recv,
    spread_send,
    spread_recv,
    sum_send,
    sum_recv,
    go_send,
    go_recv,
    side_send,
    side_recv,
    back_send,
    back_recv,
):
    place = Place()
    group = lax.axis_index("group")
    is_odd = lax.rem(place.rank, 2)
    hidden_size = w_in.shape[0] // 4
    rows = ids_ref.shape[1]
    row_blocks = rows // CHUNK
    width = 16 * SLICE

    head_part = lax.rem(place.rank, 2)
    skipped = pl.multiple_of(head_part * SHARED, SHARED)
    fetch_out = pltpu.make_async_copy(
        out_weight, w_in.at[pl.ds(skipped, SLICE)], first_sem.at[0]
    )
    first_column = pl.multiple_of((place.rank // 2) * 2 * SLICE, 2 * SLICE)
    fetch_near = pltpu.make_async_copy(
        residual_ref.at[:, pl.ds(first_column, 2 * SLICE)], near, first_sem.at[1]
    )
    loads = [
        pltpu.make_async_copy(
            ref, w_in.at[pl.ds(k * hidden_size, hidden_size)], load_sem.at[k]
        )
        for k, ref in enumerate((expert_gate.at[0], expert_up.at[0], dense_gate, dense_up))
    ] + [
        pltpu.make_async_copy(
            ref, w_down.at[pl.ds(k * hidden_size, hidden_size)], load_sem.at[4 + k]
        )
        for k, ref in enumerate((expert_down.at[0], dense_down))
    ]
    fetch_out.start()
    fetch_near.start()
    for load in loads[4:]:
        load.start()
    w_in[pl.ds(pl.multiple_of((1 - head_part) * SLICE, SHARED), SHARED), :] = jnp.zeros(
        (SHARED, width), BF
    )

    barrier = pltpu.get_barrier_semaphore()
    greet_plane(place, barrier)
    for c in range(1, CHUNKS):
        pl.semaphore_signal(
            barrier,
            inc=1,
            device_id={"group": flipped(group, chunk_bits(c))},
            device_id_type=pl.DeviceIdType.MESH,
        )
    pl.semaphore_wait(barrier, 4 + CHUNKS - 1)

    mate = place.rank + 1 - 2 * head_part
    theirs = pl.multiple_of((1 - head_part) * 3 * LANES, LANES)
    mine = head_part * 3 * LANES

    swaps = [copy_to(marks_ref, other_marks, swap_send.at[0], swap_recv.at[0], mate)] + [
        copy_to(
            numerator_ref.at[pl.ds(b * CHUNK, CHUNK), pl.ds(theirs, 4 * LANES)],
            other.at[pl.ds(b * CHUNK, CHUNK)],
            swap_send.at[1 + b],
            swap_recv.at[1 + b],
            mate,
        )
        for b in range(row_blocks)
    ]
    for copy in swaps:
        copy.start()

    gatherer = Spreader(place, full, full_send, full_recv)
    spreader = Spreader(place, part, spread_send, spread_recv)
    summer = Summer(place, part, (r1, r2, r3, r4), sum_send, sum_recv)
    state_summer = Summer(place, ready, (r1, r2, r3, r4), state_send, state_recv)

    line = lax.broadcasted_iota(jnp.int32, (rows, rows), 0)
    column = lax.broadcasted_iota(jnp.int32, (rows, rows), 1)

    def upright(row):
        return jnp.sum(jnp.where(line == column, row, 0.0), axis=1, keepdims=True)

    flat_ids = [ids_ref[k : k + 1, :].astype(F32) for k in range(2)]
    ids = [upright(row) for row in flat_ids]
    route = [upright(route_ref[k : k + 1, :]) for k in range(2)]
    partners = [flipped(group, chunk_bits(c)).astype(F32) for c in range(CHUNKS)]
    lane = lax.broadcasted_iota(jnp.int32, (rows, LANES), 1)
    partner_of_lane = jnp.full((rows, LANES), -1.0, F32)
    sub = lax.broadcasted_iota(jnp.int32, (CHUNKS, rows), 0)
    partner_of_sub = jnp.zeros((CHUNKS, rows), F32)
    for c in range(CHUNKS):
        partner_of_lane = jnp.where(lane == c, partners[c], partner_of_lane)
        partner_of_sub = jnp.where(sub == c, partners[c], partner_of_sub)
    first_choice, second_choice = [choice == partner_of_lane for choice in ids]
    named = jnp.where(first_choice | second_choice, 1.0, 0.0)
    before = jnp.where(column < line, 1.0, 0.0).astype(BF)
    place_in = jnp.dot(before, named.astype(BF), preferred_element_type=F32)
    positions = jnp.where(named > 0.5, place_in, -1.0)
    own_pos[...] = positions
    flat_named = jnp.where(
        (flat_ids[0] == partner_of_sub) | (flat_ids[1] == partner_of_sub), 1.0, 0.0
    )
    after = jnp.where(line < column, 1.0, 0.0).astype(BF)
    flat_place = jnp.dot(flat_named.astype(BF), after, preferred_element_type=F32)
    flat_pos = jnp.where(flat_named > 0.5, flat_place, -1.0)
    weight = jnp.where(first_choice, route[0], 0.0) + jnp.where(second_choice, route[1], 0.0)
    dense_here = jnp.where(first_choice, 1.0, 0.0)
    slot_line = lax.broadcasted_iota(jnp.int32, (CHUNK, rows), 0).astype(F32)
    slot_lane = lax.broadcasted_iota(jnp.int32, (rows, CHUNK), 1).astype(F32)
    sides = lax.broadcasted_iota(jnp.int32, (8, LANES), 0)

    def pick(c):
        return jnp.where(flat_pos[c : c + 1, :] == slot_line, 1.0, 0.0).astype(BF)

    def partner(c):
        return flipped(group, chunk_bits(c))

    def side(c):
        return to_group(
            side_out.at[c], side_in.at[c], side_send.at[c], side_recv.at[c], partner(c)
        )

    def slices(c):
        return [
            to_group(
                outgoing.at[SPREAD.index(c), pl.ds(h * HALF, HALF)],
                part.at[c, h, spot(h, place.z, place.x)],
                go_send.at[c, h],
                go_recv.at[c, h],
                partner(c),
            )
            for h in range(2)
        ]

    def whole(c):
        slot = 1 if c == 7 else 0
        return to_group(
            ready.at[slot], part.at[c], go_send.at[c, 0], go_recv.at[c, 0], partner(c)
        )

    swaps[0].wait_recv()
    top = jnp.maximum(marks_ref[0:8, :], other_marks[0:8, :])
    keep = jnp.exp(marks_ref[0:8, :] - top)
    take = jnp.exp(other_marks[0:8, :] - top)
    below = 1.0 / (marks_ref[8:16, :] * keep + other_marks[8:16, :] * take)
    scales = jnp.concatenate(
        [keep * below, take * below, jnp.zeros((LANES - 16, rows), F32)], axis=0
    ).T
    low = lanes_low(CHUNK)
    for b in range(row_blocks):
        swaps[1 + b].wait_recv()
        block_rows = slice(b * CHUNK, (b + 1) * CHUNK)
        joined = []
        for k in range(4):
            factors = [
                jnp.where(
                    head_part == 1,
                    scales[block_rows, at + k + 3 : at + k + 4],
                    scales[block_rows, at + k : at + k + 1],
                )
                for at in (0, 8)
            ]
            here = numerator_ref[
                block_rows, pl.ds(pl.multiple_of(mine + k * LANES, LANES), LANES)
            ].astype(F32)
            there = other[block_rows, k * LANES : (k + 1) * LANES].astype(F32)
            tile = here * factors[0] + there * factors[1]
            if k == 0:
                tile = jnp.where(low & (head_part == 1), 0.0, tile)
            if k == 3:
                tile = jnp.where(low | (head_part == 1), tile, 0.0)
            joined.append(tile.astype(BF))
        attention = jnp.concatenate(joined, axis=1)
        if b == 0:
            fetch_out.wait()

        @pl.loop(0, SIDE)
        def _(z):
            columns = pl.ds(pl.multiple_of(z * 4 * SLICE, 4 * SLICE), 4 * SLICE)
            block = jnp.dot(
                attention, w_in[: SLICE + SHARED, columns], preferred_element_type=F32
            )
            store_quarter(ready.at[b], z, block)

        state_summer.start(0, b)
    for load in loads[:4]:
        load.start()
    for b in range(row_blocks):
        state_summer.pass_on(0, b)
    for c in range(CHUNKS):
        at_slot = positions[:, c : c + 1] == slot_lane
        w_row = jnp.sum(jnp.where(at_slot, weight[:, c : c + 1], 0.0), axis=0, keepdims=True)
        d_row = jnp.sum(jnp.where(at_slot, dense_here[:, c : c + 1], 0.0), axis=0, keepdims=True)
        both = jnp.where(sides == 0, w_row, jnp.where(sides == 1, d_row, 0.0))
        if c == 0:
            side_in[0] = both
        else:
            side_out[c] = both
            side(c).start()
    for step in range(2, 4):
        for b in range(row_blocks):
            state_summer.pass_on(step - 1, b)
    fetch_near.wait()
    for b in range(row_blocks):
        block_rows = slice(b * CHUNK, (b + 1) * CHUNK)
        even = [near[block_rows, k * LANES : (k + 1) * LANES].astype(F32) for k in range(4)]
        odd = [near[block_rows, (k + 4) * LANES : (k + 5) * LANES].astype(F32) for k in range(3)]
        whole_tiles = [jnp.where(is_odd == 1, odd[k], even[k]) for k in range(3)]
        store_own(state_ref.at[b], jnp.concatenate(whole_tiles + [even[3]], axis=1), is_odd)
        state_summer.arrive(3, b)
        state = (state_ref[b].astype(F32) + state_summer.total(b)).astype(BF)
        state_ref[b] = state
        for h in range(2):
            full[b, h, spot(h, place.z, place.x)] = state[h * HALF : (h + 1) * HALF]
        gatherer.start(0, b)
    for b in range(row_blocks):
        mixing[b * CHUNK : (b + 1) * CHUNK, :] = natural_own(state_ref.at[b], is_odd)

    for c in SPREAD:
        chosen = jnp.dot(pick(c), mixing[...].astype(BF), preferred_element_type=F32)
        store_own(outgoing.at[SPREAD.index(c)], chosen, is_odd)
        for copy in slices(c):
            copy.start()
    for b in range(row_blocks):
        for h in range(2):
            gatherer.arrive(0, b, (h,))
            gatherer.start(1, b, (h,))
    for b in range(row_blocks):
        for h in range(2):
            gatherer.arrive(1, b, (h,))
            gatherer.start(2, b, (h,))
    for c in SPREAD[:2]:
        for copy in slices(c):
            copy.wait_recv()
        spreader.start(0, c)
    for b in range(row_blocks):
        for h in range(2):
            gatherer.arrive(2, b, (h,))
            gatherer.start(3, b, (h,))
    for c in SPREAD[:2]:
        spreader.arrive(0, c)
        spreader.start(1, c)
    for c in SPREAD[:2]:
        spreader.arrive(1, c)
        spreader.start(2, c)
    for c in SPREAD[2:]:
        for copy in slices(c):
            copy.wait_recv()
        spreader.start(0, c)
    for b in range(row_blocks):
        gatherer.arrive(3, b)

    def choose_whole(c, target, halves=(0, 1)):
        chosen_rows = pick(c)

        @pl.loop(0, SIDE)
        def _(z):
            source = jnp.concatenate(
                [load_quarter(full.at[b], z) for b in range(row_blocks)], axis=0
            )
            store_quarter(
                target, z, jnp.dot(chosen_rows, source, preferred_element_type=F32), halves
            )

    for b in range(row_blocks):
        state_summer.sent(b)
    choose_whole(1, ready.at[0])
    whole(1).start()
    choose_whole(7, ready.at[1])
    whole(7).start()
    whole(1).wait_send()
    choose_whole(6, ready.at[0])
    whole(6).start()
    choose_whole(0, part.at[0])

    def back(c):
        return [
            to_group(
                ready.at[0, 1, 2 * c + h],
                returned.at[c, pl.ds(h * HALF, HALF)],
                back_send.at[c, h],
                back_recv.at[c, h],
                partner(c),
            )
            for h in range(2)
        ]

    def finish_sum(c):
        summer.arrive(3, c)
        total = summer.total(c).astype(BF)

        @pl.when(c == 0)
        def _():
            returned[0] = total

        @pl.when(c > 0)
        def _():
            for h, copy in enumerate(back(c)):
                ready[0, 1, 2 * c + h] = total[h * HALF : (h + 1) * HALF]
                copy.start()

    def mix(c):
        @pl.when(c > 0)
        def _():
            for copy in back(c):
                copy.wait_recv()

        position = jnp.sum(jnp.where(lane == c, own_pos[...], 0.0), axis=1, keepdims=True)
        at_slot = jnp.where(position == slot_lane, 1.0, 0.0).astype(BF)
        block = natural_own(returned.at[c], is_odd).astype(BF)
        mixing[...] += jnp.dot(at_slot, block, preferred_element_type=F32)

    def spread(step, chunks):
        for c in chunks:
            if step == 0:
                for copy in slices(c):
                    copy.wait_recv()
            else:
                spreader.arrive(step - 1, c)
            if step < 4:
                spreader.start(step, c)

    def widen(j):
        chunks = [part.at[2 * j + i] for i in range(2)]
        acc[...] = jnp.zeros_like(acc)

        def gather_products(z, squares):
            block = jnp.concatenate([load_quarter(chunk, z) for chunk in chunks], axis=0)
            deep = pl.ds(pl.multiple_of(z * 4 * SLICE, 4 * SLICE), 4 * SLICE)
            acc[...] += lax.dot_general(
                block, w_in[:, deep], (((1,), (1,)), ((), ())), preferred_element_type=F32
            )
            for k in range(14):
                wide = block[:, k * LANES : (k + 1) * LANES].astype(F32)
                squares = squares + wide * wide
            return squares

        squares = lax.fori_loop(0, SIDE, gather_products, jnp.zeros((2 * CHUNK, LANES), F32))
        scale = lax.rsqrt(jnp.sum(squares, axis=1, keepdims=True) / width + 1e-05)
        diagonal = lax.broadcasted_iota(jnp.int32, (CHUNK, CHUNK), 0) == lax.broadcasted_iota(
            jnp.int32, (CHUNK, CHUNK), 1
        )
        for k in range(2):
            factor = jnp.concatenate(
                [
                    jnp.sum(
                        jnp.where(diagonal, side_in[2 * j + i, k : k + 1, :], 0.0),
                        axis=1,
                        keepdims=True,
                    )
                    for i in range(2)
                ],
                axis=0,
            )
            gate, up = [
                acc[:, (2 * k + i) * hidden_size : (2 * k + i + 1) * hidden_size] * scale
                for i in range(2)
            ]
            inner = gate / (1.0 + jnp.exp(-gate)) * up * factor
            hidden[:, k * hidden_size : (k + 1) * hidden_size] = inner.astype(BF)

    def narrow(j):
        chunks = [part.at[2 * j + i] for i in range(2)]
        for chosen in (SPREAD[:2], SPREAD[2:]):

            @pl.when(2 * j == chosen[0])
            def _():
                for c in chosen:
                    spreader.sent(c)

        @pl.loop(0, SIDE)
        def _(step):
            z = ring(place.z, step + 2 - SIDE)
            columns = pl.ds(pl.multiple_of(z * 4 * SLICE, 4 * SLICE), 4 * SLICE)
            block = jnp.dot(hidden[...], w_down[:, columns], preferred_element_type=F32)
            for i in range(2):
                store_quarter(chunks[i], z, block[i * CHUNK : (i + 1) * CHUNK])

            @pl.when(step == 0)
            def _():
                for i in range(2):
                    summer.start(0, 2 * j + i, (0,))

        for i in range(2):
            summer.start(0, 2 * j + i, (1,))

    def turn(it, carry):
        def stage(lag, body):
            j = it - lag

            @pl.when((j >= 0) & (j < TURNS))
            def _():
                for i in range(2):
                    body(2 * j + i)

        def add(step):
            def body(c):
                summer.pass_on(step - 1, c)

            return body

        @pl.when(it == 0)
        def _():
            spread(3, SPREAD[:2])
            spread(1, SPREAD[2:])
            whole(1).wait_recv()
            side(1).wait_recv()
            for load in loads:
                load.wait()

        for turn_at, chosen in ((1, SPREAD[:2]), (2, SPREAD[2:])):

            @pl.when(it == turn_at)
            def _():
                spread(4, chosen)
                for c in chosen:
                    side(c).wait_recv()

        @pl.when(it == 3)
        def _():
            for c in WHOLE[1:]:
                whole(c).wait()
                side(c).wait_recv()

        @pl.when(it < TURNS)
        def _():
            widen(it)

        @pl.when(it == 0)
        def _():
            spread(2, SPREAD[2:])

        @pl.when(it == 1)
        def _():
            spread(3, SPREAD[2:])

        stage(5, mix)
        stage(4, finish_sum)
        stage(3, add(3))
        stage(2, add(2))
        stage(1, add(1))

        @pl.when(it < TURNS)
        def _():
            narrow(it)

        return carry

    lax.fori_loop(0, TURNS + 5, turn, 0)

    total = mixing[...].T
    for_odd = jnp.concatenate([total[3 * LANES + SHARED :], total[: 3 * LANES]], axis=0)
    mixed_ref[...] = jnp.where(is_odd == 1, for_odd, total[:SLICE]).astype(BF)

    @pl.loop(0, CHUNKS)
    def _(c):
        summer.sent(c)

    for copy in swaps:
        copy.wait_send()
    for b in range(row_blocks):
        gatherer.sent(b)
    for c in range(1, CHUNKS):
        side(c).wait_send()
        for copy in back(c):
            copy.wait_send()
    for c in SPREAD:
        for copy in slices(c):
            copy.wait_send()


def finish_layer(
    numerator,
    marks,
    residual,
    out_weight,
    expert_ids,
    route_weights,
    expert_gate,
    expert_up,
    expert_down,
    dense_gate,
    dense_up,
    dense_down,
):
    rows = expert_ids.shape[0]
    width, hidden_size = dense_gate.shape
    vmem = pl.BlockSpec(memory_space=pltpu.VMEM)
    hbm = pl.BlockSpec(memory_space=pl.ANY)
    row_blocks = rows // CHUNK
    return pl.pallas_call(
        layer_kernel,
        out_shape=jax.ShapeDtypeStruct((SLICE, rows), BF),
        in_specs=[vmem] * 4 + [hbm] * 8,
        out_specs=vmem,
        scratch_shapes=[
            pltpu.VMEM((rows, 4 * LANES), BF),
            pltpu.VMEM((16, rows), F32),
            pltpu.VMEM((rows, 2 * SLICE), BF),
            pltpu.VMEM((row_blocks, SLICE, LANES), BF),
            pltpu.VMEM((CHUNKS, 2, 16, HALF, LANES), BF),
            pltpu.VMEM((row_blocks, 2, 16, HALF, LANES), BF),
            pltpu.VMEM((2, 2, 16, HALF, LANES), BF),
            pltpu.VMEM((SLOTS, 2, 2, 2, HALF, LANES), BF),
            pltpu.VMEM((SLOTS, 2, 2, SIDE, HALF, LANES), BF),
            pltpu.VMEM((SLOTS, 2, 2, QUARTER, LANES), BF),
            pltpu.VMEM((SLOTS, 2, 2, HALF, LANES), BF),
            pltpu.VMEM((4 * hidden_size, width), BF),
            pltpu.VMEM((2 * hidden_size, width), BF),
            pltpu.VMEM((len(SPREAD), SLICE, LANES), BF),
            pltpu.VMEM((CHUNKS, 8, LANES), F32),
            pltpu.VMEM((CHUNKS, 8, LANES), F32),
            pltpu.VMEM((CHUNKS, SLICE, LANES), BF),
            pltpu.VMEM((rows, LANES), F32),
            pltpu.VMEM((2 * CHUNK, 4 * hidden_size), F32),
            pltpu.VMEM((2 * CHUNK, 2 * hidden_size), BF),
            pltpu.VMEM((rows, 4 * LANES), F32),
            pltpu.SemaphoreType.DMA((6,)),
            pltpu.SemaphoreType.DMA((2,)),
            pltpu.SemaphoreType.DMA((1 + row_blocks,)),
            pltpu.SemaphoreType.DMA((1 + row_blocks,)),
        ]
        + [pltpu.SemaphoreType.DMA((row_blocks, 4, 2, 2))] * 4
        + [pltpu.SemaphoreType.DMA((CHUNKS, 4, 2, 2))] * 4
        + [pltpu.SemaphoreType.DMA((CHUNKS, 2))] * 2
        + [pltpu.SemaphoreType.DMA((CHUNKS,))] * 2
        + [pltpu.SemaphoreType.DMA((CHUNKS, 2))] * 2,
        compiler_params=pltpu.CompilerParams(
            collective_id=1, has_side_effects=True, vmem_limit_bytes=64 * 1024 * 1024 - 65536
        ),
        name="layer",
    )(
        numerator,
        marks,
        expert_ids.T,
        route_weights.T,
        residual,
        out_weight,
        jnp.swapaxes(expert_gate, 1, 2),
        jnp.swapaxes(expert_up, 1, 2),
        expert_down,
        dense_gate.T,
        dense_up.T,
        dense_down,
    ).T


def attend(queries, new_kv, kv_cache, lengths):
    row_count = queries.shape[0]
    rank = lax.axis_index("tensor")
    my_head, my_part = rank // 2, rank % 2
    head_size = new_kv.shape[3]
    span = kv_cache.shape[2]
    heads = jnp.arange(queries.shape[1], dtype=jnp.int32)[None, :, None] == my_head
    rows = jnp.sum(jnp.where(heads, queries, 0).astype(F32), axis=1).astype(BF)
    rows = rows.reshape(row_count, -1, head_size)
    new_key = lax.dynamic_index_in_dim(new_kv[0], my_head, 1, keepdims=False)
    new_value = lax.dynamic_index_in_dim(new_kv[1], my_head, 1, keepdims=False)
    scale = 1.0 / math.sqrt(head_size)
    scores = jnp.einsum("tgd,tpd->tgp", rows, kv_cache[0], preferred_element_type=F32) * scale
    own = jnp.einsum("tgd,td->tg", rows, new_key, preferred_element_type=F32) * scale
    position = my_part * span + jnp.arange(span, dtype=jnp.int32)
    usable = position[None, None, :] < lengths[:, None, None]
    masked = jnp.where(usable, scores, -1e30)
    highest = jnp.maximum(jnp.max(masked, axis=-1), own)
    weights = jnp.where(usable, jnp.exp(masked - highest[..., None]), 0.0).astype(BF)
    own_weight = jnp.exp(own - highest)
    leading = (my_part == 0).astype(F32)
    numerator = jnp.einsum("tgp,tpd->tgd", weights, kv_cache[1], preferred_element_type=F32)
    numerator = numerator + leading * own_weight[..., None] * new_value.astype(F32)[:, None, :]
    denominator = jnp.sum(weights.astype(F32), axis=-1) + leading * own_weight
    flat = numerator.astype(BF).reshape(row_count, -1)
    marks = jnp.concatenate(
        [
            jnp.pad(highest.T, ((0, 1), (0, 0))),
            jnp.pad(denominator.T, ((0, 1), (0, 0)), constant_values=1.0),
        ]
    )
    return flat, marks


def shards(
    residual,
    queries,
    new_kv,
    kv_cache,
    lengths,
    out_weight,
    dense_gate,
    dense_up,
    dense_down,
    expert_ids,
    route_weights,
    expert_gate,
    expert_up,
    expert_down,
):
    numerator, marks = attend(queries, new_kv, kv_cache, lengths)
    return finish_layer(
        numerator,
        marks,
        residual,
        out_weight,
        expert_ids,
        route_weights,
        expert_gate,
        expert_up,
        expert_down,
        dense_gate,
        dense_up,
        dense_down,
    )


def solution(mesh):
    placed = (
        P("group", None),
        P("group", None, None),
        P(None, "group", None, None),
        P(None, "group", "tensor", None),
        P("group"),
        P("tensor", None),
        P(None, "tensor"),
        P(None, "tensor"),
        P("tensor", None),
        P("group", None),
        P("group", None),
        P("group", None, "tensor"),
        P("group", None, "tensor"),
        P("group", "tensor", None),
    )
    return jax.shard_map(
        shards, mesh=mesh, in_specs=placed, out_specs=P("group", "tensor"), check_vma=False
    )
```

```python
import functools
import math

import jax
import jax.numpy as jnp
from jax import lax
from jax.experimental import pallas as pl
from jax.experimental.pallas import tpu as pltpu
from jax.sharding import PartitionSpec as P

BF = jnp.bfloat16
F32 = jnp.float32
SIDE = 4
LANES = 128
CHUNK = 128
SLICE = 448
HALF = SLICE // 2
SHARED = 64
CHUNKS = 8


def ring(value, step):
    return lax.rem(value + step + SIDE, SIDE)


class Place:
    def __init__(self):
        rank = lax.axis_index("tensor")
        self.rank = rank
        self.z = rank // SIDE
        self.x = lax.rem(rank, SIDE)

    def axes(self, half):
        return (self.x, self.z) if half == 0 else (self.z, self.x)

    def at(self, half, p, q):
        return q * SIDE + p if half == 0 else p * SIDE + q


def spot(half, z, x):
    return z * SIDE + x if half == 0 else x * SIDE + z


def split_rows(low, high):
    pieces = []
    if low < HALF:
        pieces.append((0, low, min(high, HALF), 0))
    if high > HALF:
        start = max(low, HALF)
        pieces.append((1, start - HALF, high - HALF, start - low))
    return pieces


def read_rows(part, z, x, low, high):
    pieces = [part[h, spot(h, z, x), a:b, :] for h, a, b, _ in split_rows(low, high)]
    return pieces[0] if len(pieces) == 1 else jnp.concatenate(pieces, axis=0)


def write_rows(part, z, x, low, value, halves=(0, 1)):
    for h, a, b, offset in split_rows(low, low + value.shape[0]):
        if h in halves:
            part[h, spot(h, z, x), a:b, :] = value[offset : offset + b - a]


def copy_to(src, dst, send, recv, rank):
    return pltpu.make_async_remote_copy(
        src_ref=src,
        dst_ref=dst,
        send_sem=send,
        recv_sem=recv,
        device_id={"tensor": rank},
        device_id_type=pl.DeviceIdType.MESH,
    )


def lanes_low(rows):
    return lax.broadcasted_iota(jnp.int32, (rows, LANES), 1) < SHARED


def turned(block):
    return pltpu.roll(block, SHARED, 1)


def unfold_pair(even_half, odd_half):
    low = lanes_low(SHARED)
    e, o = even_half.astype(F32), odd_half.astype(F32)
    top = jnp.where(low, e, o)
    bottom = turned(jnp.where(low, o, e))
    return jnp.concatenate([top, bottom], axis=0).astype(BF)


def fold_pair(tile):
    low = lanes_low(SHARED)
    top, bottom = tile[:SHARED], turned(tile[SHARED:])
    return jnp.where(low, top, bottom).astype(BF), jnp.where(low, bottom, top).astype(BF)


def unfold_own(half):
    half = half.astype(F32)
    return jnp.concatenate([half, turned(half)], axis=0)


def fold_own(tile, is_odd):
    low = lanes_low(SHARED).astype(jnp.int32) != is_odd
    top, bottom = tile[:SHARED], turned(tile[SHARED:])
    return jnp.where(low, top, bottom)


def natural_own(ref, is_odd):
    first = pl.multiple_of(is_odd * SHARED, SHARED)
    half = pl.multiple_of((1 - is_odd) * (SLICE - SHARED), SHARED)
    tiles = [ref[pl.ds(first + k * LANES, LANES), :].astype(F32) for k in range(3)]
    return jnp.concatenate(tiles + [unfold_own(ref[pl.ds(half, SHARED), :])], axis=1)


def store_own(ref, block, is_odd):
    first = pl.multiple_of(is_odd * SHARED, SHARED)
    half = pl.multiple_of((1 - is_odd) * (SLICE - SHARED), SHARED)
    for k in range(3):
        ref[pl.ds(first + k * LANES, LANES), :] = block[:, k * LANES : (k + 1) * LANES].astype(BF)
    ref[pl.ds(half, SHARED), :] = fold_own(block[:, 3 * LANES :], is_odd).astype(BF)


def store_quarter(part, z, block, halves=(0, 1)):
    for pair in range(2):
        e, o = 2 * pair, 2 * pair + 1
        tiles = [
            block[:, (pair * 7 + k) * LANES : (pair * 7 + k + 1) * LANES] for k in range(7)
        ]
        even_half, odd_half = fold_pair(tiles[3])
        for k in range(3):
            write_rows(part, z, e, k * LANES, tiles[k].astype(BF), halves)
            write_rows(part, z, o, SHARED + k * LANES, tiles[4 + k].astype(BF), halves)
        write_rows(part, z, e, SLICE - SHARED, even_half, halves)
        write_rows(part, z, o, 0, odd_half, halves)


def load_quarter(part, z):
    blocks = []
    for pair in range(2):
        e, o = 2 * pair, 2 * pair + 1
        blocks += [read_rows(part, z, e, k * LANES, (k + 1) * LANES) for k in range(3)]
        blocks.append(
            unfold_pair(
                read_rows(part, z, e, SLICE - SHARED, SLICE), read_rows(part, z, o, 0, SHARED)
            )
        )
        blocks += [
            read_rows(part, z, o, SHARED + k * LANES, SHARED + (k + 1) * LANES) for k in range(3)
        ]
    return jnp.concatenate(blocks, axis=1)


def add_into(dst, other):
    dst[...] = (dst[...].astype(F32) + other[...].astype(F32)).astype(BF)


class Exchange:
    def start(self, step, c, halves=(0, 1)):
        for copy in self.copies(step, c, halves):
            copy.start()

    def arrive(self, step, c, halves=(0, 1)):
        for copy in self.copies(step, c, halves):
            copy.wait_recv()

    def sent(self, c):
        for step in range(4):
            for copy in self.copies(step, c):
                copy.wait_send()


WAYS = ((0, 0, 1), (0, 1, -1), (1, 0, 1), (1, 1, -1))
QUARTER = HALF // 2


class Summer(Exchange):
    def __init__(self, place, part, landing, send, recv):
        self.place, self.part, self.landing = place, part, landing
        self.send, self.recv = send, recv

    def landed(self, step, c):
        landing = self.landing[step]
        return landing.at[lax.rem(c, landing.shape[0])]

    def copies(self, step, c, halves=(0, 1)):
        place = self.place
        result = []
        for h, way, hop in WAYS:
            if h not in halves:
                continue
            part = self.part.at[c, h]
            p, q = place.axes(h)
            if step == 0:
                src = part.at[pl.ds(ring(q, 2) * SIDE + 2 * way, 2)]
                to = place.at(h, p, ring(q, hop))
            elif step == 1:
                src = part.at[pl.ds(ring(q, hop) * SIDE, SIDE)]
                to = place.at(h, p, ring(q, hop))
            elif step == 2:
                src = part.at[q * SIDE + ring(p, 2), pl.ds(way * QUARTER, QUARTER)]
                to = place.at(h, ring(p, hop), q)
            else:
                src = part.at[q * SIDE + ring(p, hop)]
                to = place.at(h, ring(p, hop), q)
            result.append(
                copy_to(
                    src,
                    self.landed(step, c).at[h, way],
                    self.send.at[c, step, h, way],
                    self.recv.at[c, step, h, way],
                    to,
                )
            )
        return result

    def pass_on(self, step, c):
        for h in range(2):
            self.arrive(step, c, (h,))
            self.add(step, c, h)
            self.start(step + 1, c, (h,))

    def add(self, step, c, h):
        part = self.part.at[c, h]
        p, q = self.place.axes(h)
        landed = self.landed(step, c).at[h]
        if step == 0:
            for way, hop in ((0, 1), (1, -1)):
                for k in range(2):
                    add_into(part.at[ring(q, hop) * SIDE + 2 * way + k], landed.at[way, k])
        elif step == 1:
            for k in range(SIDE):
                dst = part.at[q * SIDE + k]
                dst[...] = (
                    dst[...].astype(F32) + landed[0, k].astype(F32) + landed[1, k].astype(F32)
                ).astype(BF)
        elif step == 2:
            for way, hop in ((0, 1), (1, -1)):
                add_into(
                    part.at[q * SIDE + ring(p, hop), pl.ds(way * QUARTER, QUARTER)],
                    landed.at[way],
                )

    def total(self, c):
        halves = []
        for h in range(2):
            p, q = self.place.axes(h)
            landed = self.landed(3, c).at[h]
            halves.append(
                self.part[c, h, q * SIDE + p].astype(F32)
                + landed[0].astype(F32)
                + landed[1].astype(F32)
            )
        return jnp.concatenate(halves, axis=0)


class Spreader(Exchange):
    def __init__(self, place, part, send, recv, halves=None):
        self.place, self.part, self.send, self.recv = place, part, send, recv
        self.halves = halves or {}

    def copies(self, step, c, halves=(0, 1)):
        place = self.place
        result = []
        for h, way, hop in WAYS:
            if h not in halves or h not in self.halves.get(c, (0, 1)):
                continue
            part = self.part.at[c, h]
            p, q = place.axes(h)
            if step == 0:
                ref = part.at[q * SIDE + p]
                to = place.at(h, ring(p, hop), q)
            elif step == 1:
                ref = part.at[q * SIDE + ring(p, -hop), pl.ds(way * QUARTER, QUARTER)]
                to = place.at(h, ring(p, hop), q)
            elif step == 2:
                ref = part.at[pl.ds(q * SIDE, SIDE)]
                to = place.at(h, p, ring(q, hop))
            else:
                ref = part.at[pl.ds(ring(q, -hop) * SIDE + 2 * way, 2)]
                to = place.at(h, p, ring(q, hop))
            result.append(
                copy_to(
                    ref,
                    ref,
                    self.send.at[c, step, h, way],
                    self.recv.at[c, step, h, way],
                    to,
                )
            )
        return result


def greet_plane(place, barrier):
    for hop in (1, -1):
        for rank in (
            place.at(0, ring(place.x, hop), place.z),
            place.at(0, place.x, ring(place.z, hop)),
        ):
            pl.semaphore_signal(
                barrier, inc=1, device_id={"tensor": rank}, device_id_type=pl.DeviceIdType.MESH
            )


def flipped(group, bits):
    b = (lax.rem(group, 2), lax.rem(group // 2, 2), group // 4)
    return sum((b[k] + bits[k] - 2 * b[k] * bits[k]) * (1 << k) for k in range(3))


PARTNERS = (0, 1, 4, 5, 3, 7, 2, 6)
WHOLE = (1, 6, 7)
SPREAD = (2, 3, 4, 5)
SPREAD_HALVES = {2: (0, 1), 3: (0, 1), 4: (1,), 5: (0,)}
TURNS = CHUNKS // 2
SLOTS = 4


def chunk_bits(c):
    if isinstance(c, int):
        return tuple((PARTNERS[c] >> k) & 1 for k in range(3))
    return tuple(
        sum(jnp.where(c == i, 1, 0) for i in range(CHUNKS) if (PARTNERS[i] >> k) & 1)
        for k in range(3)
    )


def to_group(src, dst, send, recv, group):
    return pltpu.make_async_remote_copy(
        src_ref=src,
        dst_ref=dst,
        send_sem=send,
        recv_sem=recv,
        device_id={"group": group},
        device_id_type=pl.DeviceIdType.MESH,
    )


def layer_kernel(
    numerator_ref,
    marks_ref,
    ids_ref,
    route_ref,
    residual_ref,
    out_weight,
    expert_gate,
    expert_up,
    expert_down,
    dense_gate,
    dense_up,
    dense_down,
    mixed_ref,
    other,
    other_marks,
    near,
    state_ref,
    part,
    full,
    ready,
    r1,
    r2,
    r3,
    r4,
    w_in,
    w_down,
    outgoing,
    side_out,
    side_in,
    returned,
    own_pos,
    acc,
    hidden,
    mixing,
    load_sem,
    first_sem,
    swap_send,
    swap_recv,
    state_send,
    state_recv,
    full_send,
    full_recv,
    spread_send,
    spread_recv,
    sum_send,
    sum_recv,
    go_send,
    go_recv,
    side_send,
    side_recv,
    back_send,
    back_recv,
):
    place = Place()
    group = lax.axis_index("group")
    is_odd = lax.rem(place.rank, 2)
    hidden_size = w_in.shape[0] // 4
    rows = ids_ref.shape[1]
    row_blocks = rows // CHUNK
    width = 16 * SLICE

    head_part = lax.rem(place.rank, 2)
    skipped = pl.multiple_of(head_part * SHARED, SHARED)
    fetch_out = pltpu.make_async_copy(
        out_weight, w_in.at[pl.ds(skipped, SLICE)], first_sem.at[0]
    )
    first_column = pl.multiple_of((place.rank // 2) * 2 * SLICE, 2 * SLICE)
    fetch_near = pltpu.make_async_copy(
        residual_ref.at[:, pl.ds(first_column, 2 * SLICE)], near, first_sem.at[1]
    )
    loads = [
        pltpu.make_async_copy(
            ref, w_in.at[pl.ds(k * hidden_size, hidden_size)], load_sem.at[k]
        )
        for k, ref in enumerate((expert_gate.at[0], expert_up.at[0], dense_gate, dense_up))
    ] + [
        pltpu.make_async_copy(
            ref, w_down.at[pl.ds(k * hidden_size, hidden_size)], load_sem.at[4 + k]
        )
        for k, ref in enumerate((expert_down.at[0], dense_down))
    ]
    fetch_out.start()
    fetch_near.start()
    for load in loads[4:]:
        load.start()
    w_in[pl.ds(pl.multiple_of((1 - head_part) * SLICE, SHARED), SHARED), :] = jnp.zeros(
        (SHARED, width), BF
    )

    barrier = pltpu.get_barrier_semaphore()
    greet_plane(place, barrier)
    for c in range(1, CHUNKS):
        pl.semaphore_signal(
            barrier,
            inc=1,
            device_id={"group": flipped(group, chunk_bits(c))},
            device_id_type=pl.DeviceIdType.MESH,
        )
    pl.semaphore_wait(barrier, 4 + CHUNKS - 1)

    mate = place.rank + 1 - 2 * head_part
    theirs = pl.multiple_of((1 - head_part) * 3 * LANES, LANES)
    mine = head_part * 3 * LANES

    swaps = [copy_to(marks_ref, other_marks, swap_send.at[0], swap_recv.at[0], mate)] + [
        copy_to(
            numerator_ref.at[pl.ds(b * CHUNK, CHUNK), pl.ds(theirs, 4 * LANES)],
            other.at[pl.ds(b * CHUNK, CHUNK)],
            swap_send.at[1 + b],
            swap_recv.at[1 + b],
            mate,
        )
        for b in range(row_blocks)
    ]
    for copy in swaps:
        copy.start()

    gatherer = Spreader(place, full, full_send, full_recv)
    spreader = Spreader(place, part, spread_send, spread_recv, SPREAD_HALVES)
    summer = Summer(place, part, (r1, r2, r3, r4), sum_send, sum_recv)
    state_summer = Summer(place, ready, (r1, r2, r3, r4), state_send, state_recv)

    line = lax.broadcasted_iota(jnp.int32, (rows, rows), 0)
    column = lax.broadcasted_iota(jnp.int32, (rows, rows), 1)

    def upright(row):
        return jnp.sum(jnp.where(line == column, row, 0.0), axis=1, keepdims=True)

    flat_ids = [ids_ref[k : k + 1, :].astype(F32) for k in range(2)]
    ids = [upright(row) for row in flat_ids]
    route = [upright(route_ref[k : k + 1, :]) for k in range(2)]
    partners = [flipped(group, chunk_bits(c)).astype(F32) for c in range(CHUNKS)]
    lane = lax.broadcasted_iota(jnp.int32, (rows, LANES), 1)
    partner_of_lane = jnp.full((rows, LANES), -1.0, F32)
    sub = lax.broadcasted_iota(jnp.int32, (CHUNKS, rows), 0)
    partner_of_sub = jnp.zeros((CHUNKS, rows), F32)
    for c in range(CHUNKS):
        partner_of_lane = jnp.where(lane == c, partners[c], partner_of_lane)
        partner_of_sub = jnp.where(sub == c, partners[c], partner_of_sub)
    first_choice, second_choice = [choice == partner_of_lane for choice in ids]
    named = jnp.where(first_choice | second_choice, 1.0, 0.0)
    before = jnp.where(column < line, 1.0, 0.0).astype(BF)
    place_in = jnp.dot(before, named.astype(BF), preferred_element_type=F32)
    positions = jnp.where(named > 0.5, place_in, -1.0)
    own_pos[...] = positions
    flat_named = jnp.where(
        (flat_ids[0] == partner_of_sub) | (flat_ids[1] == partner_of_sub), 1.0, 0.0
    )
    after = jnp.where(line < column, 1.0, 0.0).astype(BF)
    flat_place = jnp.dot(flat_named.astype(BF), after, preferred_element_type=F32)
    flat_pos = jnp.where(flat_named > 0.5, flat_place, -1.0)
    weight = jnp.where(first_choice, route[0], 0.0) + jnp.where(second_choice, route[1], 0.0)
    dense_here = jnp.where(first_choice, 1.0, 0.0)
    slot_line = lax.broadcasted_iota(jnp.int32, (CHUNK, rows), 0).astype(F32)
    slot_lane = lax.broadcasted_iota(jnp.int32, (rows, CHUNK), 1).astype(F32)
    sides = lax.broadcasted_iota(jnp.int32, (8, LANES), 0)

    def pick(c):
        return jnp.where(flat_pos[c : c + 1, :] == slot_line, 1.0, 0.0).astype(BF)

    def partner(c):
        return flipped(group, chunk_bits(c))

    def side(c):
        return to_group(
            side_out.at[c], side_in.at[c], side_send.at[c], side_recv.at[c], partner(c)
        )

    def slices(c):
        return [
            to_group(
                outgoing.at[SPREAD.index(c), pl.ds(h * HALF, HALF)],
                part.at[c, h, spot(h, place.z, place.x)],
                go_send.at[c, h],
                go_recv.at[c, h],
                partner(c),
            )
            for h in SPREAD_HALVES[c]
        ]

    def whole(c):
        slot = 1 if c == 7 else 0
        return to_group(
            ready.at[slot], part.at[c], go_send.at[c, 0], go_recv.at[c, 0], partner(c)
        )

    def other_half(c):
        h = 1 - SPREAD_HALVES[c][0]
        return to_group(
            ready.at[2, h], part.at[c, h], go_send.at[c, h], go_recv.at[c, h], partner(c)
        )

    swaps[0].wait_recv()
    top = jnp.maximum(marks_ref[0:8, :], other_marks[0:8, :])
    keep = jnp.exp(marks_ref[0:8, :] - top)
    take = jnp.exp(other_marks[0:8, :] - top)
    below = 1.0 / (marks_ref[8:16, :] * keep + other_marks[8:16, :] * take)
    scales = jnp.concatenate(
        [keep * below, take * below, jnp.zeros((LANES - 16, rows), F32)], axis=0
    ).T
    low = lanes_low(CHUNK)
    for b in range(row_blocks):
        swaps[1 + b].wait_recv()
        block_rows = slice(b * CHUNK, (b + 1) * CHUNK)
        joined = []
        for k in range(4):
            factors = [
                jnp.where(
                    head_part == 1,
                    scales[block_rows, at + k + 3 : at + k + 4],
                    scales[block_rows, at + k : at + k + 1],
                )
                for at in (0, 8)
            ]
            here = numerator_ref[
                block_rows, pl.ds(pl.multiple_of(mine + k * LANES, LANES), LANES)
            ].astype(F32)
            there = other[block_rows, k * LANES : (k + 1) * LANES].astype(F32)
            tile = here * factors[0] + there * factors[1]
            if k == 0:
                tile = jnp.where(low & (head_part == 1), 0.0, tile)
            if k == 3:
                tile = jnp.where(low | (head_part == 1), tile, 0.0)
            joined.append(tile.astype(BF))
        attention = jnp.concatenate(joined, axis=1)
        if b == 0:
            fetch_out.wait()

        @pl.loop(0, SIDE)
        def _(z):
            columns = pl.ds(pl.multiple_of(z * 4 * SLICE, 4 * SLICE), 4 * SLICE)
            block = jnp.dot(
                attention, w_in[: SLICE + SHARED, columns], preferred_element_type=F32
            )
            store_quarter(ready.at[b], z, block)

        state_summer.start(0, b)
    for load in loads[:4]:
        load.start()
    for b in range(row_blocks):
        state_summer.pass_on(0, b)
    for c in range(CHUNKS):
        at_slot = positions[:, c : c + 1] == slot_lane
        w_row = jnp.sum(jnp.where(at_slot, weight[:, c : c + 1], 0.0), axis=0, keepdims=True)
        d_row = jnp.sum(jnp.where(at_slot, dense_here[:, c : c + 1], 0.0), axis=0, keepdims=True)
        both = jnp.where(sides == 0, w_row, jnp.where(sides == 1, d_row, 0.0))
        if c == 0:
            side_in[0] = both
        else:
            side_out[c] = both
            side(c).start()
    for step in range(2, 4):
        for b in range(row_blocks):
            state_summer.pass_on(step - 1, b)
    fetch_near.wait()
    for b in range(row_blocks):
        block_rows = slice(b * CHUNK, (b + 1) * CHUNK)
        even = [near[block_rows, k * LANES : (k + 1) * LANES].astype(F32) for k in range(4)]
        odd = [near[block_rows, (k + 4) * LANES : (k + 5) * LANES].astype(F32) for k in range(3)]
        whole_tiles = [jnp.where(is_odd == 1, odd[k], even[k]) for k in range(3)]
        store_own(state_ref.at[b], jnp.concatenate(whole_tiles + [even[3]], axis=1), is_odd)
        state_summer.arrive(3, b)
        state = (state_ref[b].astype(F32) + state_summer.total(b)).astype(BF)
        state_ref[b] = state
        for h in range(2):
            full[b, h, spot(h, place.z, place.x)] = state[h * HALF : (h + 1) * HALF]
        gatherer.start(0, b)
    for b in range(row_blocks):
        mixing[b * CHUNK : (b + 1) * CHUNK, :] = natural_own(state_ref.at[b], is_odd)

    for c in SPREAD:
        chosen = jnp.dot(pick(c), mixing[...].astype(BF), preferred_element_type=F32)
        store_own(outgoing.at[SPREAD.index(c)], chosen, is_odd)
        for copy in slices(c):
            copy.start()
    for b in range(row_blocks):
        for h in range(2):
            gatherer.arrive(0, b, (h,))
            gatherer.start(1, b, (h,))
    for b in range(row_blocks):
        for h in range(2):
            gatherer.arrive(1, b, (h,))
            gatherer.start(2, b, (h,))
    for c in SPREAD[:2]:
        for copy in slices(c):
            copy.wait_recv()
        spreader.start(0, c)
    for b in range(row_blocks):
        for h in range(2):
            gatherer.arrive(2, b, (h,))
            gatherer.start(3, b, (h,))
    for c in SPREAD[:2]:
        spreader.arrive(0, c)
        spreader.start(1, c)
    for c in SPREAD[:2]:
        spreader.arrive(1, c)
        spreader.start(2, c)
    for c in SPREAD[2:]:
        for copy in slices(c):
            copy.wait_recv()
        spreader.start(0, c)
    for b in range(row_blocks):
        gatherer.arrive(3, b)

    def choose_whole(c, target, halves=(0, 1)):
        chosen_rows = pick(c)

        @pl.loop(0, SIDE)
        def _(z):
            source = jnp.concatenate(
                [load_quarter(full.at[b], z) for b in range(row_blocks)], axis=0
            )
            store_quarter(
                target, z, jnp.dot(chosen_rows, source, preferred_element_type=F32), halves
            )

    for b in range(row_blocks):
        state_summer.sent(b)
    for c in SPREAD[2:]:
        choose_whole(c, ready.at[2], (1 - SPREAD_HALVES[c][0],))
        other_half(c).start()
    choose_whole(1, ready.at[0])
    whole(1).start()
    choose_whole(7, ready.at[1])
    whole(7).start()
    whole(1).wait_send()
    choose_whole(6, ready.at[0])
    whole(6).start()
    choose_whole(0, part.at[0])

    def back(c):
        return [
            to_group(
                ready.at[0, 1, 2 * c + h],
                returned.at[c, pl.ds(h * HALF, HALF)],
                back_send.at[c, h],
                back_recv.at[c, h],
                partner(c),
            )
            for h in range(2)
        ]

    def finish_sum(c):
        summer.arrive(3, c)
        total = summer.total(c).astype(BF)

        @pl.when(c == 0)
        def _():
            returned[0] = total

        @pl.when(c > 0)
        def _():
            for h, copy in enumerate(back(c)):
                ready[0, 1, 2 * c + h] = total[h * HALF : (h + 1) * HALF]
                copy.start()

    def mix(c):
        @pl.when(c > 0)
        def _():
            for copy in back(c):
                copy.wait_recv()

        position = jnp.sum(jnp.where(lane == c, own_pos[...], 0.0), axis=1, keepdims=True)
        at_slot = jnp.where(position == slot_lane, 1.0, 0.0).astype(BF)
        block = natural_own(returned.at[c], is_odd).astype(BF)
        mixing[...] += jnp.dot(at_slot, block, preferred_element_type=F32)

    def spread(step, chunks):
        for c in chunks:
            if step == 0:
                for copy in slices(c):
                    copy.wait_recv()
            else:
                spreader.arrive(step - 1, c)
            if step < 4:
                spreader.start(step, c)

    def widen(j):
        chunks = [part.at[2 * j + i] for i in range(2)]
        acc[...] = jnp.zeros_like(acc)

        def gather_products(z, squares):
            block = jnp.concatenate([load_quarter(chunk, z) for chunk in chunks], axis=0)
            deep = pl.ds(pl.multiple_of(z * 4 * SLICE, 4 * SLICE), 4 * SLICE)
            acc[...] += lax.dot_general(
                block, w_in[:, deep], (((1,), (1,)), ((), ())), preferred_element_type=F32
            )
            for k in range(14):
                wide = block[:, k * LANES : (k + 1) * LANES].astype(F32)
                squares = squares + wide * wide
            return squares

        squares = lax.fori_loop(0, SIDE, gather_products, jnp.zeros((2 * CHUNK, LANES), F32))
        scale = lax.rsqrt(jnp.sum(squares, axis=1, keepdims=True) / width + 1e-05)
        diagonal = lax.broadcasted_iota(jnp.int32, (CHUNK, CHUNK), 0) == lax.broadcasted_iota(
            jnp.int32, (CHUNK, CHUNK), 1
        )
        for k in range(2):
            factor = jnp.concatenate(
                [
                    jnp.sum(
                        jnp.where(diagonal, side_in[2 * j + i, k : k + 1, :], 0.0),
                        axis=1,
                        keepdims=True,
                    )
                    for i in range(2)
                ],
                axis=0,
            )
            gate, up = [
                acc[:, (2 * k + i) * hidden_size : (2 * k + i + 1) * hidden_size] * scale
                for i in range(2)
            ]
            inner = gate / (1.0 + jnp.exp(-gate)) * up * factor
            hidden[:, k * hidden_size : (k + 1) * hidden_size] = inner.astype(BF)

    def narrow(j):
        chunks = [part.at[2 * j + i] for i in range(2)]
        for chosen in (SPREAD[:2], SPREAD[2:]):

            @pl.when(2 * j == chosen[0])
            def _():
                for c in chosen:
                    spreader.sent(c)

        @pl.loop(0, SIDE)
        def _(step):
            z = ring(place.z, step + 2 - SIDE)
            columns = pl.ds(pl.multiple_of(z * 4 * SLICE, 4 * SLICE), 4 * SLICE)
            block = jnp.dot(hidden[...], w_down[:, columns], preferred_element_type=F32)
            for i in range(2):
                store_quarter(chunks[i], z, block[i * CHUNK : (i + 1) * CHUNK])

            @pl.when(step == 0)
            def _():
                for i in range(2):
                    summer.start(0, 2 * j + i, (0,))

        for i in range(2):
            summer.start(0, 2 * j + i, (1,))

    def turn(it, carry):
        def stage(lag, body):
            j = it - lag

            @pl.when((j >= 0) & (j < TURNS))
            def _():
                for i in range(2):
                    body(2 * j + i)

        def add(step):
            def body(c):
                summer.pass_on(step - 1, c)

            return body

        @pl.when(it == 0)
        def _():
            spread(3, SPREAD[:2])
            spread(1, SPREAD[2:])
            whole(1).wait_recv()
            side(1).wait_recv()
            for load in loads:
                load.wait()

        for turn_at, chosen in ((1, SPREAD[:2]), (2, SPREAD[2:])):

            @pl.when(it == turn_at)
            def _():
                spread(4, chosen)
                for c in chosen:
                    side(c).wait_recv()
                    if len(SPREAD_HALVES[c]) == 1:
                        other_half(c).wait()

        @pl.when(it == 3)
        def _():
            for c in WHOLE[1:]:
                whole(c).wait()
                side(c).wait_recv()

        @pl.when(it < TURNS)
        def _():
            widen(it)

        @pl.when(it == 0)
        def _():
            spread(2, SPREAD[2:])

        @pl.when(it == 1)
        def _():
            spread(3, SPREAD[2:])

        stage(5, mix)
        stage(4, finish_sum)
        stage(3, add(3))
        stage(2, add(2))
        stage(1, add(1))

        @pl.when(it < TURNS)
        def _():
            narrow(it)

        return carry

    lax.fori_loop(0, TURNS + 5, turn, 0)

    total = mixing[...].T
    for_odd = jnp.concatenate([total[3 * LANES + SHARED :], total[: 3 * LANES]], axis=0)
    mixed_ref[...] = jnp.where(is_odd == 1, for_odd, total[:SLICE])

    @pl.loop(0, CHUNKS)
    def _(c):
        summer.sent(c)

    for copy in swaps:
        copy.wait_send()
    for b in range(row_blocks):
        gatherer.sent(b)
    for c in range(1, CHUNKS):
        side(c).wait_send()
        for copy in back(c):
            copy.wait_send()
    for c in SPREAD:
        for copy in slices(c):
            copy.wait_send()


def finish_layer(
    numerator,
    marks,
    residual,
    out_weight,
    expert_ids,
    route_weights,
    expert_gate,
    expert_up,
    expert_down,
    dense_gate,
    dense_up,
    dense_down,
):
    rows = expert_ids.shape[0]
    width, hidden_size = dense_gate.shape
    vmem = pl.BlockSpec(memory_space=pltpu.VMEM)
    hbm = pl.BlockSpec(memory_space=pl.ANY)
    row_blocks = rows // CHUNK
    return pl.pallas_call(
        layer_kernel,
        out_shape=jax.ShapeDtypeStruct((SLICE, rows), F32),
        in_specs=[vmem] * 4 + [hbm] * 8,
        out_specs=vmem,
        scratch_shapes=[
            pltpu.VMEM((rows, 4 * LANES), BF),
            pltpu.VMEM((16, rows), F32),
            pltpu.VMEM((rows, 2 * SLICE), BF),
            pltpu.VMEM((row_blocks, SLICE, LANES), BF),
            pltpu.VMEM((CHUNKS, 2, 16, HALF, LANES), BF),
            pltpu.VMEM((row_blocks, 2, 16, HALF, LANES), BF),
            pltpu.VMEM((3, 2, 16, HALF, LANES), BF),
            pltpu.VMEM((SLOTS, 2, 2, 2, HALF, LANES), BF),
            pltpu.VMEM((SLOTS, 2, 2, SIDE, HALF, LANES), BF),
            pltpu.VMEM((SLOTS, 2, 2, QUARTER, LANES), BF),
            pltpu.VMEM((SLOTS, 2, 2, HALF, LANES), BF),
            pltpu.VMEM((4 * hidden_size, width), BF),
            pltpu.VMEM((2 * hidden_size, width), BF),
            pltpu.VMEM((len(SPREAD), SLICE, LANES), BF),
            pltpu.VMEM((CHUNKS, 8, LANES), F32),
            pltpu.VMEM((CHUNKS, 8, LANES), F32),
            pltpu.VMEM((CHUNKS, SLICE, LANES), BF),
            pltpu.VMEM((rows, LANES), F32),
            pltpu.VMEM((2 * CHUNK, 4 * hidden_size), F32),
            pltpu.VMEM((2 * CHUNK, 2 * hidden_size), BF),
            pltpu.VMEM((rows, 4 * LANES), F32),
            pltpu.SemaphoreType.DMA((6,)),
            pltpu.SemaphoreType.DMA((2,)),
            pltpu.SemaphoreType.DMA((1 + row_blocks,)),
            pltpu.SemaphoreType.DMA((1 + row_blocks,)),
        ]
        + [pltpu.SemaphoreType.DMA((row_blocks, 4, 2, 2))] * 4
        + [pltpu.SemaphoreType.DMA((CHUNKS, 4, 2, 2))] * 4
        + [pltpu.SemaphoreType.DMA((CHUNKS, 2))] * 2
        + [pltpu.SemaphoreType.DMA((CHUNKS,))] * 2
        + [pltpu.SemaphoreType.DMA((CHUNKS, 2))] * 2,
        compiler_params=pltpu.CompilerParams(
            collective_id=1, has_side_effects=True, vmem_limit_bytes=64 * 1024 * 1024 - 65536
        ),
        name="layer",
    )(
        numerator,
        marks,
        expert_ids.T,
        route_weights.T,
        residual,
        out_weight,
        jnp.swapaxes(expert_gate, 1, 2),
        jnp.swapaxes(expert_up, 1, 2),
        expert_down,
        dense_gate.T,
        dense_up.T,
        dense_down,
    ).astype(BF).T


def attend(queries, new_kv, kv_cache, lengths):
    row_count = queries.shape[0]
    rank = lax.axis_index("tensor")
    my_head, my_part = rank // 2, rank % 2
    head_size = new_kv.shape[3]
    span = kv_cache.shape[2]
    heads = jnp.arange(queries.shape[1], dtype=jnp.int32)[None, :, None] == my_head
    rows = jnp.sum(jnp.where(heads, queries, 0).astype(F32), axis=1).astype(BF)
    rows = rows.reshape(row_count, -1, head_size)
    new_key = lax.dynamic_index_in_dim(new_kv[0], my_head, 1, keepdims=False)
    new_value = lax.dynamic_index_in_dim(new_kv[1], my_head, 1, keepdims=False)
    scale = 1.0 / math.sqrt(head_size)
    scores = jnp.einsum("tgd,tpd->tgp", rows, kv_cache[0], preferred_element_type=F32) * scale
    own = jnp.einsum("tgd,td->tg", rows, new_key, preferred_element_type=F32) * scale
    position = my_part * span + jnp.arange(span, dtype=jnp.int32)
    usable = position[None, None, :] < lengths[:, None, None]
    masked = jnp.where(usable, scores, -1e30)
    highest = jnp.maximum(jnp.max(masked, axis=-1), own)
    weights = jnp.where(usable, jnp.exp(masked - highest[..., None]), 0.0).astype(BF)
    own_weight = jnp.exp(own - highest)
    leading = (my_part == 0).astype(F32)
    numerator = jnp.einsum("tgp,tpd->tgd", weights, kv_cache[1], preferred_element_type=F32)
    numerator = numerator + leading * own_weight[..., None] * new_value.astype(F32)[:, None, :]
    denominator = jnp.sum(weights.astype(F32), axis=-1) + leading * own_weight
    flat = numerator.astype(BF).reshape(row_count, -1)
    marks = jnp.concatenate(
        [
            jnp.pad(highest.T, ((0, 1), (0, 0))),
            jnp.pad(denominator.T, ((0, 1), (0, 0)), constant_values=1.0),
        ]
    )
    return flat, marks


def shards(
    residual,
    queries,
    new_kv,
    kv_cache,
    lengths,
    out_weight,
    dense_gate,
    dense_up,
    dense_down,
    expert_ids,
    route_weights,
    expert_gate,
    expert_up,
    expert_down,
):
    numerator, marks = attend(queries, new_kv, kv_cache, lengths)
    return finish_layer(
        numerator,
        marks,
        residual,
        out_weight,
        expert_ids,
        route_weights,
        expert_gate,
        expert_up,
        expert_down,
        dense_gate,
        dense_up,
        dense_down,
    )


def solution(mesh):
    placed = (
        P("group", None),
        P("group", None, None),
        P(None, "group", None, None),
        P(None, "group", "tensor", None),
        P("group"),
        P("tensor", None),
        P(None, "tensor"),
        P(None, "tensor"),
        P("tensor", None),
        P("group", None),
        P("group", None),
        P("group", None, "tensor"),
        P("group", None, "tensor"),
        P("group", "tensor", None),
    )
    return jax.shard_map(
        shards, mesh=mesh, in_specs=placed, out_specs=P("group", "tensor"), check_vma=False
    )
```

```python
import functools
import math

import jax
import jax.numpy as jnp
from jax import lax
from jax.experimental import pallas as pl
from jax.experimental.pallas import tpu as pltpu
from jax.sharding import PartitionSpec as P

BF = jnp.bfloat16
F32 = jnp.float32
SIDE = 4
LANES = 128
CHUNK = 128
SLICE = 448
HALF = SLICE // 2
SHARED = 64
CHUNKS = 8


def ring(value, step):
    return lax.rem(value + step + SIDE, SIDE)


class Place:
    def __init__(self):
        rank = lax.axis_index("tensor")
        self.rank = rank
        self.z = rank // SIDE
        self.x = lax.rem(rank, SIDE)

    def axes(self, half):
        return (self.x, self.z) if half == 0 else (self.z, self.x)

    def at(self, half, p, q):
        return q * SIDE + p if half == 0 else p * SIDE + q


def spot(half, z, x):
    return z * SIDE + x if half == 0 else x * SIDE + z


def split_rows(low, high):
    pieces = []
    if low < HALF:
        pieces.append((0, low, min(high, HALF), 0))
    if high > HALF:
        start = max(low, HALF)
        pieces.append((1, start - HALF, high - HALF, start - low))
    return pieces


def read_rows(part, z, x, low, high):
    pieces = [part[h, spot(h, z, x), a:b, :] for h, a, b, _ in split_rows(low, high)]
    return pieces[0] if len(pieces) == 1 else jnp.concatenate(pieces, axis=0)


def write_rows(part, z, x, low, value, halves=(0, 1)):
    for h, a, b, offset in split_rows(low, low + value.shape[0]):
        if h in halves:
            part[h, spot(h, z, x), a:b, :] = value[offset : offset + b - a]


def copy_to(src, dst, send, recv, rank):
    return pltpu.make_async_remote_copy(
        src_ref=src,
        dst_ref=dst,
        send_sem=send,
        recv_sem=recv,
        device_id={"tensor": rank},
        device_id_type=pl.DeviceIdType.MESH,
    )


def lanes_low(rows):
    return lax.broadcasted_iota(jnp.int32, (rows, LANES), 1) < SHARED


def turned(block):
    return pltpu.roll(block, SHARED, 1)


def unfold_pair(even_half, odd_half):
    low = lanes_low(SHARED)
    e, o = even_half.astype(F32), odd_half.astype(F32)
    top = jnp.where(low, e, o)
    bottom = turned(jnp.where(low, o, e))
    return jnp.concatenate([top, bottom], axis=0).astype(BF)


def fold_pair(tile):
    low = lanes_low(SHARED)
    top, bottom = tile[:SHARED], turned(tile[SHARED:])
    return jnp.where(low, top, bottom).astype(BF), jnp.where(low, bottom, top).astype(BF)


def unfold_own(half):
    half = half.astype(F32)
    return jnp.concatenate([half, turned(half)], axis=0)


def fold_own(tile, is_odd):
    low = lanes_low(SHARED).astype(jnp.int32) != is_odd
    top, bottom = tile[:SHARED], turned(tile[SHARED:])
    return jnp.where(low, top, bottom)


def natural_own(ref, is_odd):
    first = pl.multiple_of(is_odd * SHARED, SHARED)
    half = pl.multiple_of((1 - is_odd) * (SLICE - SHARED), SHARED)
    tiles = [ref[pl.ds(first + k * LANES, LANES), :].astype(F32) for k in range(3)]
    return jnp.concatenate(tiles + [unfold_own(ref[pl.ds(half, SHARED), :])], axis=1)


def store_own(ref, block, is_odd):
    first = pl.multiple_of(is_odd * SHARED, SHARED)
    half = pl.multiple_of((1 - is_odd) * (SLICE - SHARED), SHARED)
    for k in range(3):
        ref[pl.ds(first + k * LANES, LANES), :] = block[:, k * LANES : (k + 1) * LANES].astype(BF)
    ref[pl.ds(half, SHARED), :] = fold_own(block[:, 3 * LANES :], is_odd).astype(BF)


def store_quarter(part, z, block, halves=(0, 1)):
    for pair in range(2):
        e, o = 2 * pair, 2 * pair + 1
        tiles = [
            block[:, (pair * 7 + k) * LANES : (pair * 7 + k + 1) * LANES] for k in range(7)
        ]
        even_half, odd_half = fold_pair(tiles[3])
        for k in range(3):
            write_rows(part, z, e, k * LANES, tiles[k].astype(BF), halves)
            write_rows(part, z, o, SHARED + k * LANES, tiles[4 + k].astype(BF), halves)
        write_rows(part, z, e, SLICE - SHARED, even_half, halves)
        write_rows(part, z, o, 0, odd_half, halves)


def load_quarter(part, z):
    blocks = []
    for pair in range(2):
        e, o = 2 * pair, 2 * pair + 1
        blocks += [read_rows(part, z, e, k * LANES, (k + 1) * LANES) for k in range(3)]
        blocks.append(
            unfold_pair(
                read_rows(part, z, e, SLICE - SHARED, SLICE), read_rows(part, z, o, 0, SHARED)
            )
        )
        blocks += [
            read_rows(part, z, o, SHARED + k * LANES, SHARED + (k + 1) * LANES) for k in range(3)
        ]
    return jnp.concatenate(blocks, axis=1)


def add_into(dst, other):
    dst[...] = (dst[...].astype(F32) + other[...].astype(F32)).astype(BF)


class Exchange:
    def start(self, step, c, halves=(0, 1)):
        for copy in self.copies(step, c, halves):
            copy.start()

    def arrive(self, step, c, halves=(0, 1)):
        for copy in self.copies(step, c, halves):
            copy.wait_recv()

    def sent(self, c):
        for step in range(4):
            for copy in self.copies(step, c):
                copy.wait_send()


WAYS = ((0, 0, 1), (0, 1, -1), (1, 0, 1), (1, 1, -1))
QUARTER = HALF // 2


class Summer(Exchange):
    def __init__(self, place, part, landing, send, recv):
        self.place, self.part, self.landing = place, part, landing
        self.send, self.recv = send, recv

    def landed(self, step, c):
        landing = self.landing[step]
        return landing.at[lax.rem(c, landing.shape[0])]

    def copies(self, step, c, halves=(0, 1)):
        place = self.place
        result = []
        for h, way, hop in WAYS:
            if h not in halves:
                continue
            part = self.part.at[c, h]
            p, q = place.axes(h)
            if step == 0:
                src = part.at[pl.ds(ring(q, 2) * SIDE + 2 * way, 2)]
                to = place.at(h, p, ring(q, hop))
            elif step == 1:
                src = part.at[pl.ds(ring(q, hop) * SIDE, SIDE)]
                to = place.at(h, p, ring(q, hop))
            elif step == 2:
                src = part.at[q * SIDE + ring(p, 2), pl.ds(way * QUARTER, QUARTER)]
                to = place.at(h, ring(p, hop), q)
            else:
                src = part.at[q * SIDE + ring(p, hop)]
                to = place.at(h, ring(p, hop), q)
            result.append(
                copy_to(
                    src,
                    self.landed(step, c).at[h, way],
                    self.send.at[c, step, h, way],
                    self.recv.at[c, step, h, way],
                    to,
                )
            )
        return result

    def pass_on(self, step, c):
        for h in range(2):
            self.arrive(step, c, (h,))
            self.add(step, c, h)
            self.start(step + 1, c, (h,))

    def add(self, step, c, h):
        part = self.part.at[c, h]
        p, q = self.place.axes(h)
        landed = self.landed(step, c).at[h]
        if step == 0:
            for way, hop in ((0, 1), (1, -1)):
                for k in range(2):
                    add_into(part.at[ring(q, hop) * SIDE + 2 * way + k], landed.at[way, k])
        elif step == 1:
            for k in range(SIDE):
                dst = part.at[q * SIDE + k]
                dst[...] = (
                    dst[...].astype(F32) + landed[0, k].astype(F32) + landed[1, k].astype(F32)
                ).astype(BF)
        elif step == 2:
            for way, hop in ((0, 1), (1, -1)):
                add_into(
                    part.at[q * SIDE + ring(p, hop), pl.ds(way * QUARTER, QUARTER)],
                    landed.at[way],
                )

    def total(self, c):
        halves = []
        for h in range(2):
            p, q = self.place.axes(h)
            landed = self.landed(3, c).at[h]
            halves.append(
                self.part[c, h, q * SIDE + p].astype(F32)
                + landed[0].astype(F32)
                + landed[1].astype(F32)
            )
        return jnp.concatenate(halves, axis=0)


class Spreader(Exchange):
    def __init__(self, place, part, send, recv, halves=None):
        self.place, self.part, self.send, self.recv = place, part, send, recv
        self.halves = halves or {}

    def copies(self, step, c, halves=(0, 1)):
        place = self.place
        result = []
        for h, way, hop in WAYS:
            if h not in halves or h not in self.halves.get(c, (0, 1)):
                continue
            part = self.part.at[c, h]
            p, q = place.axes(h)
            if step == 0:
                ref = part.at[q * SIDE + p]
                to = place.at(h, ring(p, hop), q)
            elif step == 1:
                ref = part.at[q * SIDE + ring(p, -hop), pl.ds(way * QUARTER, QUARTER)]
                to = place.at(h, ring(p, hop), q)
            elif step == 2:
                ref = part.at[pl.ds(q * SIDE, SIDE)]
                to = place.at(h, p, ring(q, hop))
            else:
                ref = part.at[pl.ds(ring(q, -hop) * SIDE + 2 * way, 2)]
                to = place.at(h, p, ring(q, hop))
            result.append(
                copy_to(
                    ref,
                    ref,
                    self.send.at[c, step, h, way],
                    self.recv.at[c, step, h, way],
                    to,
                )
            )
        return result


def greet_plane(place, barrier):
    for hop in (1, -1):
        for rank in (
            place.at(0, ring(place.x, hop), place.z),
            place.at(0, place.x, ring(place.z, hop)),
        ):
            pl.semaphore_signal(
                barrier, inc=1, device_id={"tensor": rank}, device_id_type=pl.DeviceIdType.MESH
            )


def flipped(group, bits):
    b = (lax.rem(group, 2), lax.rem(group // 2, 2), group // 4)
    return sum((b[k] + bits[k] - 2 * b[k] * bits[k]) * (1 << k) for k in range(3))


PARTNERS = (0, 1, 4, 5, 3, 7, 2, 6)
WHOLE = (1, 6, 7)
SPREAD = (2, 3, 4, 5)
SPREAD_HALVES = {2: (0, 1), 3: (0, 1), 4: (1,), 5: (0,)}
TURNS = CHUNKS // 2
IDLE_TURN = 3
SLOTS = 4


def chunk_bits(c):
    if isinstance(c, int):
        return tuple((PARTNERS[c] >> k) & 1 for k in range(3))
    return tuple(
        sum(jnp.where(c == i, 1, 0) for i in range(CHUNKS) if (PARTNERS[i] >> k) & 1)
        for k in range(3)
    )


def to_group(src, dst, send, recv, group):
    return pltpu.make_async_remote_copy(
        src_ref=src,
        dst_ref=dst,
        send_sem=send,
        recv_sem=recv,
        device_id={"group": group},
        device_id_type=pl.DeviceIdType.MESH,
    )


def layer_kernel(
    numerator_ref,
    marks_ref,
    ids_ref,
    route_ref,
    residual_ref,
    out_weight,
    expert_gate,
    expert_up,
    expert_down,
    dense_gate,
    dense_up,
    dense_down,
    mixed_ref,
    other,
    other_marks,
    near,
    state_ref,
    part,
    full,
    ready,
    r1,
    r2,
    r3,
    r4,
    w_in,
    w_down,
    outgoing,
    side_out,
    side_in,
    returned,
    own_pos,
    acc,
    hidden,
    mixing,
    load_sem,
    first_sem,
    swap_send,
    swap_recv,
    state_send,
    state_recv,
    full_send,
    full_recv,
    spread_send,
    spread_recv,
    sum_send,
    sum_recv,
    go_send,
    go_recv,
    side_send,
    side_recv,
    back_send,
    back_recv,
):
    place = Place()
    group = lax.axis_index("group")
    is_odd = lax.rem(place.rank, 2)
    hidden_size = w_in.shape[0] // 4
    rows = ids_ref.shape[1]
    row_blocks = rows // CHUNK
    width = 16 * SLICE

    head_part = lax.rem(place.rank, 2)
    skipped = pl.multiple_of(head_part * SHARED, SHARED)
    fetch_out = pltpu.make_async_copy(
        out_weight, w_in.at[pl.ds(skipped, SLICE)], first_sem.at[0]
    )
    first_column = pl.multiple_of((place.rank // 2) * 2 * SLICE, 2 * SLICE)
    fetch_near = pltpu.make_async_copy(
        residual_ref.at[:, pl.ds(first_column, 2 * SLICE)], near, first_sem.at[1]
    )
    loads = [
        pltpu.make_async_copy(
            ref, w_in.at[pl.ds(k * hidden_size, hidden_size)], load_sem.at[k]
        )
        for k, ref in enumerate((expert_gate.at[0], expert_up.at[0], dense_gate, dense_up))
    ] + [
        pltpu.make_async_copy(
            ref, w_down.at[pl.ds(k * hidden_size, hidden_size)], load_sem.at[4 + k]
        )
        for k, ref in enumerate((expert_down.at[0], dense_down))
    ]
    fetch_out.start()
    fetch_near.start()
    for load in loads[4:]:
        load.start()
    w_in[pl.ds(pl.multiple_of((1 - head_part) * SLICE, SHARED), SHARED), :] = jnp.zeros(
        (SHARED, width), BF
    )

    barrier = pltpu.get_barrier_semaphore()
    greet_plane(place, barrier)
    for c in range(1, CHUNKS):
        pl.semaphore_signal(
            barrier,
            inc=1,
            device_id={"group": flipped(group, chunk_bits(c))},
            device_id_type=pl.DeviceIdType.MESH,
        )
    pl.semaphore_wait(barrier, 4 + CHUNKS - 1)

    mate = place.rank + 1 - 2 * head_part
    theirs = pl.multiple_of((1 - head_part) * 3 * LANES, LANES)
    mine = head_part * 3 * LANES

    swaps = [copy_to(marks_ref, other_marks, swap_send.at[0], swap_recv.at[0], mate)] + [
        copy_to(
            numerator_ref.at[pl.ds(b * CHUNK, CHUNK), pl.ds(theirs, 4 * LANES)],
            other.at[pl.ds(b * CHUNK, CHUNK)],
            swap_send.at[1 + b],
            swap_recv.at[1 + b],
            mate,
        )
        for b in range(row_blocks)
    ]
    for copy in swaps:
        copy.start()

    gatherer = Spreader(place, full, full_send, full_recv)
    spreader = Spreader(place, part, spread_send, spread_recv, SPREAD_HALVES)
    summer = Summer(place, part, (r1, r2, r3, r4), sum_send, sum_recv)
    state_summer = Summer(place, ready, (r1, r2, r3, r4), state_send, state_recv)

    line = lax.broadcasted_iota(jnp.int32, (rows, rows), 0)
    column = lax.broadcasted_iota(jnp.int32, (rows, rows), 1)

    def upright(row):
        return jnp.sum(jnp.where(line == column, row, 0.0), axis=1, keepdims=True)

    flat_ids = [ids_ref[k : k + 1, :].astype(F32) for k in range(2)]
    ids = [upright(row) for row in flat_ids]
    route = [upright(route_ref[k : k + 1, :]) for k in range(2)]
    partners = [flipped(group, chunk_bits(c)).astype(F32) for c in range(CHUNKS)]
    lane = lax.broadcasted_iota(jnp.int32, (rows, LANES), 1)
    partner_of_lane = jnp.full((rows, LANES), -1.0, F32)
    sub = lax.broadcasted_iota(jnp.int32, (CHUNKS, rows), 0)
    partner_of_sub = jnp.zeros((CHUNKS, rows), F32)
    for c in range(CHUNKS):
        partner_of_lane = jnp.where(lane == c, partners[c], partner_of_lane)
        partner_of_sub = jnp.where(sub == c, partners[c], partner_of_sub)
    first_choice, second_choice = [choice == partner_of_lane for choice in ids]
    named = jnp.where(first_choice | second_choice, 1.0, 0.0)
    before = jnp.where(column < line, 1.0, 0.0).astype(BF)
    place_in = jnp.dot(before, named.astype(BF), preferred_element_type=F32)
    positions = jnp.where(named > 0.5, place_in, -1.0)
    own_pos[...] = positions
    flat_named = jnp.where(
        (flat_ids[0] == partner_of_sub) | (flat_ids[1] == partner_of_sub), 1.0, 0.0
    )
    after = jnp.where(line < column, 1.0, 0.0).astype(BF)
    flat_place = jnp.dot(flat_named.astype(BF), after, preferred_element_type=F32)
    flat_pos = jnp.where(flat_named > 0.5, flat_place, -1.0)
    weight = jnp.where(first_choice, route[0], 0.0) + jnp.where(second_choice, route[1], 0.0)
    dense_here = jnp.where(first_choice, 1.0, 0.0)
    slot_line = lax.broadcasted_iota(jnp.int32, (CHUNK, rows), 0).astype(F32)
    slot_lane = lax.broadcasted_iota(jnp.int32, (rows, CHUNK), 1).astype(F32)
    sides = lax.broadcasted_iota(jnp.int32, (8, LANES), 0)

    def pick(c):
        return jnp.where(flat_pos[c : c + 1, :] == slot_line, 1.0, 0.0).astype(BF)

    def partner(c):
        return flipped(group, chunk_bits(c))

    def side(c):
        return to_group(
            side_out.at[c], side_in.at[c], side_send.at[c], side_recv.at[c], partner(c)
        )

    def slices(c):
        return [
            to_group(
                outgoing.at[SPREAD.index(c), pl.ds(h * HALF, HALF)],
                part.at[c, h, spot(h, place.z, place.x)],
                go_send.at[c, h],
                go_recv.at[c, h],
                partner(c),
            )
            for h in SPREAD_HALVES[c]
        ]

    def whole(c):
        slot = 1 if c == 7 else 0
        return to_group(
            ready.at[slot], part.at[c], go_send.at[c, 0], go_recv.at[c, 0], partner(c)
        )

    def other_half(c):
        h = 1 - SPREAD_HALVES[c][0]
        return to_group(
            ready.at[2, h], part.at[c, h], go_send.at[c, h], go_recv.at[c, h], partner(c)
        )

    swaps[0].wait_recv()
    top = jnp.maximum(marks_ref[0:8, :], other_marks[0:8, :])
    keep = jnp.exp(marks_ref[0:8, :] - top)
    take = jnp.exp(other_marks[0:8, :] - top)
    below = 1.0 / (marks_ref[8:16, :] * keep + other_marks[8:16, :] * take)
    scales = jnp.concatenate(
        [keep * below, take * below, jnp.zeros((LANES - 16, rows), F32)], axis=0
    ).T
    low = lanes_low(CHUNK)
    for b in range(row_blocks):
        swaps[1 + b].wait_recv()
        block_rows = slice(b * CHUNK, (b + 1) * CHUNK)
        joined = []
        for k in range(4):
            factors = [
                jnp.where(
                    head_part == 1,
                    scales[block_rows, at + k + 3 : at + k + 4],
                    scales[block_rows, at + k : at + k + 1],
                )
                for at in (0, 8)
            ]
            here = numerator_ref[
                block_rows, pl.ds(pl.multiple_of(mine + k * LANES, LANES), LANES)
            ].astype(F32)
            there = other[block_rows, k * LANES : (k + 1) * LANES].astype(F32)
            tile = here * factors[0] + there * factors[1]
            if k == 0:
                tile = jnp.where(low & (head_part == 1), 0.0, tile)
            if k == 3:
                tile = jnp.where(low | (head_part == 1), tile, 0.0)
            joined.append(tile.astype(BF))
        attention = jnp.concatenate(joined, axis=1)
        if b == 0:
            fetch_out.wait()

        @pl.loop(0, SIDE)
        def _(z):
            columns = pl.ds(pl.multiple_of(z * 4 * SLICE, 4 * SLICE), 4 * SLICE)
            block = jnp.dot(
                attention, w_in[: SLICE + SHARED, columns], preferred_element_type=F32
            )
            store_quarter(ready.at[b], z, block)

        state_summer.start(0, b)
    for load in loads[:4]:
        load.start()
    for b in range(row_blocks):
        state_summer.pass_on(0, b)
    for c in range(CHUNKS):
        at_slot = positions[:, c : c + 1] == slot_lane
        w_row = jnp.sum(jnp.where(at_slot, weight[:, c : c + 1], 0.0), axis=0, keepdims=True)
        d_row = jnp.sum(jnp.where(at_slot, dense_here[:, c : c + 1], 0.0), axis=0, keepdims=True)
        both = jnp.where(sides == 0, w_row, jnp.where(sides == 1, d_row, 0.0))
        if c == 0:
            side_in[0] = both
        else:
            side_out[c] = both
            side(c).start()
    for step in range(2, 4):
        for b in range(row_blocks):
            state_summer.pass_on(step - 1, b)
    fetch_near.wait()
    for b in range(row_blocks):
        block_rows = slice(b * CHUNK, (b + 1) * CHUNK)
        even = [near[block_rows, k * LANES : (k + 1) * LANES].astype(F32) for k in range(4)]
        odd = [near[block_rows, (k + 4) * LANES : (k + 5) * LANES].astype(F32) for k in range(3)]
        whole_tiles = [jnp.where(is_odd == 1, odd[k], even[k]) for k in range(3)]
        store_own(state_ref.at[b], jnp.concatenate(whole_tiles + [even[3]], axis=1), is_odd)
        state_summer.arrive(3, b)
        state = (state_ref[b].astype(F32) + state_summer.total(b)).astype(BF)
        state_ref[b] = state
        for h in range(2):
            full[b, h, spot(h, place.z, place.x)] = state[h * HALF : (h + 1) * HALF]
        gatherer.start(0, b)
    for b in range(row_blocks):
        mixing[b * CHUNK : (b + 1) * CHUNK, :] = natural_own(state_ref.at[b], is_odd)

    for c in SPREAD:
        chosen = jnp.dot(pick(c), mixing[...].astype(BF), preferred_element_type=F32)
        store_own(outgoing.at[SPREAD.index(c)], chosen, is_odd)
        for copy in slices(c):
            copy.start()
    for b in range(row_blocks):
        for h in range(2):
            gatherer.arrive(0, b, (h,))
            gatherer.start(1, b, (h,))
    for b in range(row_blocks):
        for h in range(2):
            gatherer.arrive(1, b, (h,))
            gatherer.start(2, b, (h,))
    for c in SPREAD[:2]:
        for copy in slices(c):
            copy.wait_recv()
        spreader.start(0, c)
    for b in range(row_blocks):
        for h in range(2):
            gatherer.arrive(2, b, (h,))
            gatherer.start(3, b, (h,))
    for c in SPREAD[:2]:
        spreader.arrive(0, c)
        spreader.start(1, c)
    for c in SPREAD[:2]:
        spreader.arrive(1, c)
        spreader.start(2, c)
    for c in SPREAD[2:]:
        for copy in slices(c):
            copy.wait_recv()
        spreader.start(0, c)
    for b in range(row_blocks):
        gatherer.arrive(3, b)

    def choose_whole(c, target, halves=(0, 1)):
        chosen_rows = pick(c)

        @pl.loop(0, SIDE)
        def _(z):
            source = jnp.concatenate(
                [load_quarter(full.at[b], z) for b in range(row_blocks)], axis=0
            )
            store_quarter(
                target, z, jnp.dot(chosen_rows, source, preferred_element_type=F32), halves
            )

    for b in range(row_blocks):
        state_summer.sent(b)
    for c in SPREAD[2:]:
        choose_whole(c, ready.at[2], (1 - SPREAD_HALVES[c][0],))
        other_half(c).start()
    choose_whole(1, ready.at[0])
    whole(1).start()
    choose_whole(7, ready.at[1])
    whole(7).start()
    whole(1).wait_send()
    choose_whole(6, ready.at[0])
    whole(6).start()
    choose_whole(0, part.at[0])

    def back(c):
        return [
            to_group(
                ready.at[0, 1, 2 * c + h],
                returned.at[c, pl.ds(h * HALF, HALF)],
                back_send.at[c, h],
                back_recv.at[c, h],
                partner(c),
            )
            for h in range(2)
        ]

    def finish_sum(c):
        summer.arrive(3, c)
        total = summer.total(c).astype(BF)

        @pl.when(c == 0)
        def _():
            returned[0] = total

        @pl.when(c > 0)
        def _():
            for h, copy in enumerate(back(c)):
                ready[0, 1, 2 * c + h] = total[h * HALF : (h + 1) * HALF]
                copy.start()

    def mix(c):
        @pl.when(c > 0)
        def _():
            for copy in back(c):
                copy.wait_recv()

        position = jnp.sum(jnp.where(lane == c, own_pos[...], 0.0), axis=1, keepdims=True)
        at_slot = jnp.where(position == slot_lane, 1.0, 0.0).astype(BF)
        block = natural_own(returned.at[c], is_odd).astype(BF)
        mixing[...] += jnp.dot(at_slot, block, preferred_element_type=F32)

    def spread(step, chunks):
        for c in chunks:
            if step == 0:
                for copy in slices(c):
                    copy.wait_recv()
            else:
                spreader.arrive(step - 1, c)
            if step < 4:
                spreader.start(step, c)

    def widen(j):
        chunks = [part.at[2 * j + i] for i in range(2)]
        acc[...] = jnp.zeros_like(acc)

        def gather_products(z, squares):
            block = jnp.concatenate([load_quarter(chunk, z) for chunk in chunks], axis=0)
            deep = pl.ds(pl.multiple_of(z * 4 * SLICE, 4 * SLICE), 4 * SLICE)
            acc[...] += lax.dot_general(
                block, w_in[:, deep], (((1,), (1,)), ((), ())), preferred_element_type=F32
            )
            for k in range(14):
                wide = block[:, k * LANES : (k + 1) * LANES].astype(F32)
                squares = squares + wide * wide
            return squares

        squares = lax.fori_loop(0, SIDE, gather_products, jnp.zeros((2 * CHUNK, LANES), F32))
        scale = lax.rsqrt(jnp.sum(squares, axis=1, keepdims=True) / width + 1e-05)
        diagonal = lax.broadcasted_iota(jnp.int32, (CHUNK, CHUNK), 0) == lax.broadcasted_iota(
            jnp.int32, (CHUNK, CHUNK), 1
        )
        for k in range(2):
            factor = jnp.concatenate(
                [
                    jnp.sum(
                        jnp.where(diagonal, side_in[2 * j + i, k : k + 1, :], 0.0),
                        axis=1,
                        keepdims=True,
                    )
                    for i in range(2)
                ],
                axis=0,
            )
            gate, up = [
                acc[:, (2 * k + i) * hidden_size : (2 * k + i + 1) * hidden_size] * scale
                for i in range(2)
            ]
            inner = gate / (1.0 + jnp.exp(-gate)) * up * factor
            hidden[:, k * hidden_size : (k + 1) * hidden_size] = inner.astype(BF)

    def narrow(j):
        chunks = [part.at[2 * j + i] for i in range(2)]
        for chosen in (SPREAD[:2], SPREAD[2:]):

            @pl.when(2 * j == chosen[0])
            def _():
                for c in chosen:
                    spreader.sent(c)

        @pl.loop(0, SIDE)
        def _(step):
            z = ring(place.z, step + 2 - SIDE)
            columns = pl.ds(pl.multiple_of(z * 4 * SLICE, 4 * SLICE), 4 * SLICE)
            block = jnp.dot(hidden[...], w_down[:, columns], preferred_element_type=F32)
            for i in range(2):
                store_quarter(chunks[i], z, block[i * CHUNK : (i + 1) * CHUNK])

            @pl.when(step == 0)
            def _():
                for i in range(2):
                    summer.start(0, 2 * j + i, (0,))

        for i in range(2):
            summer.start(0, 2 * j + i, (1,))

    def pair_of(started):
        return started - started // TURNS

    def turn(it, carry):
        computes = (it <= TURNS) & (it != IDLE_TURN)

        def stage(lag, body):
            started = it - lag

            @pl.when((started >= 0) & (started <= TURNS) & (started != IDLE_TURN))
            def _():
                for i in range(2):
                    body(2 * pair_of(started) + i)

        def add(step):
            def body(c):
                summer.pass_on(step - 1, c)

            return body

        @pl.when(it == 0)
        def _():
            spread(3, SPREAD[:2])
            spread(1, SPREAD[2:])
            whole(1).wait_recv()
            side(1).wait_recv()
            for load in loads:
                load.wait()

        for turn_at, chosen in ((1, SPREAD[:2]), (2, SPREAD[2:])):

            @pl.when(it == turn_at)
            def _():
                spread(4, chosen)
                for c in chosen:
                    side(c).wait_recv()
                    if len(SPREAD_HALVES[c]) == 1:
                        other_half(c).wait()

        @pl.when(it == TURNS)
        def _():
            for c in WHOLE[1:]:
                whole(c).wait()
                side(c).wait_recv()

        @pl.when(computes)
        def _():
            widen(pair_of(it))

        @pl.when(it == 0)
        def _():
            spread(2, SPREAD[2:])

        @pl.when(it == 1)
        def _():
            spread(3, SPREAD[2:])

        stage(5, mix)
        stage(4, finish_sum)
        stage(3, add(3))
        stage(2, add(2))
        stage(1, add(1))

        @pl.when(computes)
        def _():
            narrow(pair_of(it))

        return carry

    lax.fori_loop(0, TURNS + 6, turn, 0)

    total = mixing[...].T
    for_odd = jnp.concatenate([total[3 * LANES + SHARED :], total[: 3 * LANES]], axis=0)
    mixed_ref[...] = jnp.where(is_odd == 1, for_odd, total[:SLICE])

    @pl.loop(0, CHUNKS)
    def _(c):
        summer.sent(c)

    for copy in swaps:
        copy.wait_send()
    for b in range(row_blocks):
        gatherer.sent(b)
    for c in range(1, CHUNKS):
        side(c).wait_send()
        for copy in back(c):
            copy.wait_send()
    for c in SPREAD:
        for copy in slices(c):
            copy.wait_send()


def finish_layer(
    numerator,
    marks,
    residual,
    out_weight,
    expert_ids,
    route_weights,
    expert_gate,
    expert_up,
    expert_down,
    dense_gate,
    dense_up,
    dense_down,
):
    rows = expert_ids.shape[0]
    width, hidden_size = dense_gate.shape
    vmem = pl.BlockSpec(memory_space=pltpu.VMEM)
    hbm = pl.BlockSpec(memory_space=pl.ANY)
    row_blocks = rows // CHUNK
    return pl.pallas_call(
        layer_kernel,
        out_shape=jax.ShapeDtypeStruct((SLICE, rows), F32),
        in_specs=[vmem] * 4 + [hbm] * 8,
        out_specs=vmem,
        scratch_shapes=[
            pltpu.VMEM((rows, 4 * LANES), BF),
            pltpu.VMEM((16, rows), F32),
            pltpu.VMEM((rows, 2 * SLICE), BF),
            pltpu.VMEM((row_blocks, SLICE, LANES), BF),
            pltpu.VMEM((CHUNKS, 2, 16, HALF, LANES), BF),
            pltpu.VMEM((row_blocks, 2, 16, HALF, LANES), BF),
            pltpu.VMEM((3, 2, 16, HALF, LANES), BF),
            pltpu.VMEM((SLOTS, 2, 2, 2, HALF, LANES), BF),
            pltpu.VMEM((SLOTS, 2, 2, SIDE, HALF, LANES), BF),
            pltpu.VMEM((SLOTS, 2, 2, QUARTER, LANES), BF),
            pltpu.VMEM((SLOTS, 2, 2, HALF, LANES), BF),
            pltpu.VMEM((4 * hidden_size, width), BF),
            pltpu.VMEM((2 * hidden_size, width), BF),
            pltpu.VMEM((len(SPREAD), SLICE, LANES), BF),
            pltpu.VMEM((CHUNKS, 8, LANES), F32),
            pltpu.VMEM((CHUNKS, 8, LANES), F32),
            pltpu.VMEM((CHUNKS, SLICE, LANES), BF),
            pltpu.VMEM((rows, LANES), F32),
            pltpu.VMEM((2 * CHUNK, 4 * hidden_size), F32),
            pltpu.VMEM((2 * CHUNK, 2 * hidden_size), BF),
            pltpu.VMEM((rows, 4 * LANES), F32),
            pltpu.SemaphoreType.DMA((6,)),
            pltpu.SemaphoreType.DMA((2,)),
            pltpu.SemaphoreType.DMA((1 + row_blocks,)),
            pltpu.SemaphoreType.DMA((1 + row_blocks,)),
        ]
        + [pltpu.SemaphoreType.DMA((row_blocks, 4, 2, 2))] * 4
        + [pltpu.SemaphoreType.DMA((CHUNKS, 4, 2, 2))] * 4
        + [pltpu.SemaphoreType.DMA((CHUNKS, 2))] * 2
        + [pltpu.SemaphoreType.DMA((CHUNKS,))] * 2
        + [pltpu.SemaphoreType.DMA((CHUNKS, 2))] * 2,
        compiler_params=pltpu.CompilerParams(
            collective_id=1, has_side_effects=True, vmem_limit_bytes=64 * 1024 * 1024 - 65536
        ),
        name="layer",
    )(
        numerator,
        marks,
        expert_ids.T,
        route_weights.T,
        residual,
        out_weight,
        jnp.swapaxes(expert_gate, 1, 2),
        jnp.swapaxes(expert_up, 1, 2),
        expert_down,
        dense_gate.T,
        dense_up.T,
        dense_down,
    ).astype(BF).T


def attend(queries, new_kv, kv_cache, lengths):
    row_count = queries.shape[0]
    rank = lax.axis_index("tensor")
    my_head, my_part = rank // 2, rank % 2
    head_size = new_kv.shape[3]
    span = kv_cache.shape[2]
    heads = jnp.arange(queries.shape[1], dtype=jnp.int32)[None, :, None] == my_head
    rows = jnp.sum(jnp.where(heads, queries, 0).astype(F32), axis=1).astype(BF)
    rows = rows.reshape(row_count, -1, head_size)
    new_key = lax.dynamic_index_in_dim(new_kv[0], my_head, 1, keepdims=False)
    new_value = lax.dynamic_index_in_dim(new_kv[1], my_head, 1, keepdims=False)
    scale = 1.0 / math.sqrt(head_size)
    scores = jnp.einsum("tgd,tpd->tgp", rows, kv_cache[0], preferred_element_type=F32) * scale
    own = jnp.einsum("tgd,td->tg", rows, new_key, preferred_element_type=F32) * scale
    position = my_part * span + jnp.arange(span, dtype=jnp.int32)
    usable = position[None, None, :] < lengths[:, None, None]
    masked = jnp.where(usable, scores, -1e30)
    highest = jnp.maximum(jnp.max(masked, axis=-1), own)
    weights = jnp.where(usable, jnp.exp(masked - highest[..., None]), 0.0).astype(BF)
    own_weight = jnp.exp(own - highest)
    leading = (my_part == 0).astype(F32)
    numerator = jnp.einsum("tgp,tpd->tgd", weights, kv_cache[1], preferred_element_type=F32)
    numerator = numerator + leading * own_weight[..., None] * new_value.astype(F32)[:, None, :]
    denominator = jnp.sum(weights.astype(F32), axis=-1) + leading * own_weight
    flat = numerator.astype(BF).reshape(row_count, -1)
    marks = jnp.concatenate(
        [
            jnp.pad(highest.T, ((0, 1), (0, 0))),
            jnp.pad(denominator.T, ((0, 1), (0, 0)), constant_values=1.0),
        ]
    )
    return flat, marks


def shards(
    residual,
    queries,
    new_kv,
    kv_cache,
    lengths,
    out_weight,
    dense_gate,
    dense_up,
    dense_down,
    expert_ids,
    route_weights,
    expert_gate,
    expert_up,
    expert_down,
):
    numerator, marks = attend(queries, new_kv, kv_cache, lengths)
    return finish_layer(
        numerator,
        marks,
        residual,
        out_weight,
        expert_ids,
        route_weights,
        expert_gate,
        expert_up,
        expert_down,
        dense_gate,
        dense_up,
        dense_down,
    )


def solution(mesh):
    placed = (
        P("group", None),
        P("group", None, None),
        P(None, "group", None, None),
        P(None, "group", "tensor", None),
        P("group"),
        P("tensor", None),
        P(None, "tensor"),
        P(None, "tensor"),
        P("tensor", None),
        P("group", None),
        P("group", None),
        P("group", None, "tensor"),
        P("group", None, "tensor"),
        P("group", "tensor", None),
    )
    return jax.shard_map(
        shards, mesh=mesh, in_specs=placed, out_specs=P("group", "tensor"), check_vma=False
    )
```
